32 devices in a mesh: rows: 8 (over y, x, core), feat: 4 (over z).
Axes of the slice: x: 2, y: 2, z: 4, core: 2. Of those that a mesh axis runs over, the one named last changes fastest.
Arguments:
- tokens: bfloat16 [32, 128, 768], P(('rows', 'feat')), may hold values from -6 to 6
- cotangent: bfloat16 [32, 128, 768], P(('rows', 'feat')), may hold values from -6 to 6
- seg_ids: int32 [32, 128], P(('rows', 'feat')), may hold values from 0 to 7, as said below
- pad_mask: int32 [32, 128], P(('rows', 'feat')), may hold values from 0 to 1, as said below
- norm1_gain: bfloat16 [768], replicated, may hold values from 0.5 to 1.5
- w_query: bfloat16 [768, 768], replicated, may hold values from -0.21875 to 0.21875
- w_key: bfloat16 [768, 768], replicated, may hold values from -0.21875 to 0.21875
- w_value: bfloat16 [768, 768], replicated, may hold values from -0.21875 to 0.21875
- w_gate: bfloat16 [768, 768], replicated, may hold values from -0.21875 to 0.21875
- w_rate: bfloat16 [768, 12], replicated, may hold values from -0.21875 to 0.21875
- b_rate: bfloat16 [12], replicated, may hold values from -3 to 3
- inner_w1: bfloat16 [12, 64, 256], replicated, may hold values from -0.75 to 0.75
- inner_b1: bfloat16 [12, 256], replicated, may hold values from -2 to 2
- inner_w2: bfloat16 [12, 256, 64], replicated, may hold values from -0.375 to 0.375
- inner_b2: bfloat16 [12, 64], replicated, may hold values from -2 to 2
- inner_gain: bfloat16 [12, 64], replicated, may hold values from 0.5 to 1.5
- inner_bias: bfloat16 [12, 64], replicated, may hold values from -2 to 2
- w_out: bfloat16 [768, 768], replicated, may hold values from -0.21875 to 0.21875
- norm2_gain: bfloat16 [768], replicated, may hold values from 0.5 to 1.5
- ffn_gate: bfloat16 [768, 2048], P(None, 'feat'), may hold values from -0.21875 to 0.21875
- ffn_up: bfloat16 [768, 2048], P(None, 'feat'), may hold values from -0.21875 to 0.21875
- ffn_down: bfloat16 [2048, 768], P('feat'), may hold values from -0.125 to 0.125
Outputs:
- mixed: bfloat16 [32, 128, 768], P(('rows', 'feat'))
- grad_tokens: float32 [32, 128, 768], P(('rows', 'feat'))
- grad_norm1_gain: float32 [768], P('feat')
- grad_w_query: float32 [768, 768], P('feat')
- grad_w_key: float32 [768, 768], P('feat')
- grad_w_value: float32 [768, 768], P('feat')
- grad_w_gate: float32 [768, 768], P('feat')
- grad_w_rate: float32 [768, 12], P('feat')
- grad_b_rate: float32 [12], replicated
- grad_inner_w1: float32 [12, 64, 256], replicated
- grad_inner_b1: float32 [12, 256], replicated
- grad_inner_w2: float32 [12, 256, 64], replicated
- grad_inner_b2: float32 [12, 64], replicated
- grad_inner_gain: float32 [12, 64], replicated
- grad_inner_bias: float32 [12, 64], replicated
- grad_w_out: float32 [768, 768], P('feat')
- grad_norm2_gain: float32 [768], P('feat')
- grad_ffn_gate: float32 [768, 2048], P(None, 'feat')
- grad_ffn_up: float32 [768, 2048], P(None, 'feat')
- grad_ffn_down: float32 [2048, 768], P('feat')
The draws below stay inside these ranges and needn't reach their ends.
Inputs may be any that keep to these rules, and one draw needn't show every extreme that they name: Within a row seg_ids start at 0, never fall, rise by one at each new document and change only at multiples of 16 positions; padding is a tail of whole mini-batches with its own id. In some row every mini-batch begins a new document. `pad_mask`: zeros form the tail of a row, a multiple of 16 tokens long and at most half the row; the first mini-batch of every row is live.
All inputs are finite; a program needn't handle non-finite values.
Results may differ from the reference program's by a relative error of at most 0.018.
Values may be sent and summed in bfloat16 or wider, within the bound.
No kernel may reach another device: no remote copies, remote signals or barrier semaphores. Data moves between devices by JAX's collectives and lax.ppermute only.
A program may use at most 128 MiB of HBM per device.

```python
from functools import partial
import jax
import jax.numpy as jnp
from jax import lax

D = 768
HEADS = 12
HD = 64
INNER = 256
FF = 2048
MB = 16
ROW_LEN = 128
ROWS = 32


def row_layout(key):
    blocks = ROW_LEN // MB
    first_key, second_key, third_key, fourth_key = jax.random.split(key, 4)
    tempo = jax.random.randint(first_key, (ROWS, 1), 1, 4)
    ticket = jax.random.randint(second_key, (ROWS, blocks), 0, 64)
    chosen = jax.random.randint(fourth_key, (1, 1), 0, ROWS)
    row_number = jnp.arange(ROWS, dtype=jnp.int32)[:, None]
    threshold = jnp.where(tempo == 1, 1, jnp.where(tempo == 2, 4, 16))
    threshold = jnp.where(row_number == chosen, 64, threshold)
    position = jnp.arange(blocks, dtype=jnp.int32)[None, :]
    padded = jax.random.randint(third_key, (ROWS, 1), 0, blocks // 2 + 1)
    live_blocks = position < blocks - padded
    starts = (ticket < threshold) | (position == 0) | (position == blocks - padded)
    block_ids = jnp.cumsum(starts.astype(jnp.int32), axis=1) - 1
    segments = jnp.repeat(block_ids, MB, axis=1).astype(jnp.int32)
    live = jnp.repeat(live_blocks.astype(jnp.int32), MB, axis=1)
    return (segments, live)


def draw_seg_ids(key, part):
    return row_layout(key)[0]


def draw_pad_mask(key, part):
    return row_layout(key)[1]


def shard_levels(stream_key, dims, cuts, least, high):
    def one(axis_at, blocks):
        steps = jax.random.uniform(jax.random.fold_in(jax.random.fold_in(stream_key, 6), axis_at), (blocks,), jnp.float32, least / len(cuts), high / len(cuts))
        return jnp.repeat(jnp.exp(steps), dims[axis_at] // blocks).reshape((-1,) + (1,) * (len(dims) - axis_at - 1))

    gain = one(*cuts[0])
    for cut in cuts[1:]:
        gain = gain * one(*cut)
    return gain


def centred(own_key, shape, scale, most, shards=(), held_as=jnp.bfloat16):
    entries = scale * jax.random.normal(own_key, shape, jnp.float32)
    if shards:
        entries = entries * shard_levels(own_key, shape, shards, -0.22, 0.18)
    return jnp.clip(entries, -most, most).astype(held_as)


def setup_inputs(seed: int = 0) -> dict:
    streams_of = jax.random.split(jax.random.key(seed), 23)
    tokens = centred(streams_of[0], (ROWS, ROW_LEN, D), 1.0, 6.0, ((0, 32),))
    cotangent = centred(streams_of[1], (ROWS, ROW_LEN, D), 1.0, 6.0, ((0, 32),))
    seg_ids = draw_seg_ids(jax.random.fold_in(streams_of[22], 71), 0)
    pad_mask = draw_pad_mask(jax.random.fold_in(streams_of[22], 71), 0)
    norm1_gain = jnp.clip(1.0 + 0.1 * jax.random.normal(streams_of[4], (D,), jnp.float32), 0.5, 1.5).astype(jnp.bfloat16)
    w_query = centred(streams_of[5], (D, D), D ** -0.5, 0.21875)
    w_key = centred(streams_of[6], (D, D), D ** -0.5, 0.21875)
    w_value = centred(streams_of[7], (D, D), D ** -0.5, 0.21875)
    w_gate = centred(streams_of[8], (D, D), D ** -0.5, 0.21875)
    w_rate = centred(streams_of[9], (D, HEADS), D ** -0.5, 0.21875)
    b_rate = centred(streams_of[10], (HEADS,), 1.0, 3.0)
    inner_w1 = centred(streams_of[11], (HEADS, HD, INNER), HD ** -0.5, 0.75)
    inner_b1 = centred(streams_of[12], (HEADS, INNER), 0.3, 2.0)
    inner_w2 = centred(streams_of[13], (HEADS, INNER, HD), INNER ** -0.5, 0.375)
    inner_b2 = centred(streams_of[14], (HEADS, HD), 0.3, 2.0)
    inner_gain = jnp.clip(1.0 + 0.1 * jax.random.normal(streams_of[15], (HEADS, HD), jnp.float32), 0.5, 1.5).astype(jnp.bfloat16)
    inner_bias = centred(streams_of[16], (HEADS, HD), 0.3, 2.0)
    w_out = centred(streams_of[17], (D, D), D ** -0.5, 0.21875)
    norm2_gain = jnp.clip(1.0 + 0.1 * jax.random.normal(streams_of[18], (D,), jnp.float32), 0.5, 1.5).astype(jnp.bfloat16)
    ffn_gate = centred(streams_of[19], (D, FF), D ** -0.5, 0.21875, ((1, 4),))
    ffn_up = centred(streams_of[20], (D, FF), D ** -0.5, 0.21875, ((1, 4),))
    ffn_down = centred(streams_of[21], (FF, D), FF ** -0.5, 0.125, ((0, 4),))
    return {"tokens": tokens, "cotangent": cotangent, "seg_ids": seg_ids, "pad_mask": pad_mask, "norm1_gain": norm1_gain, "w_query": w_query, "w_key": w_key, "w_value": w_value, "w_gate": w_gate, "w_rate": w_rate, "b_rate": b_rate, "inner_w1": inner_w1, "inner_b1": inner_b1, "inner_w2": inner_w2, "inner_b2": inner_b2, "inner_gain": inner_gain, "inner_bias": inner_bias, "w_out": w_out, "norm2_gain": norm2_gain, "ffn_gate": ffn_gate, "ffn_up": ffn_up, "ffn_down": ffn_down}


EPSILON = 1e-06
BASE_RATE = 0.1
FULL_PRECISION = lax.Precision.HIGHEST

@jax.custom_vjp
def low(v):
    return lax.optimization_barrier(v.astype(jnp.bfloat16)).astype(jnp.float32)

@jax.custom_vjp
def low_back(v):
    return v

def low_keep(v):
    return (low(v), None)

def low_pass(kept, grad):
    return (grad,)

def back_keep(v):
    return (v, None)

def back_low(kept, grad):
    return (low(grad),)
low.defvjp(low_keep, low_pass)
low_back.defvjp(back_keep, back_low)

def gelu_exact(values):
    return 0.5 * values * (1.0 + lax.erf(values * 0.7071067811865476))

def gelu_slope(values):
    return 0.5 * (1.0 + lax.erf(values * 0.7071067811865476)) + values * jnp.exp(-0.5 * values * values) * 0.3989422804014327

def product(form, left, right):
    return jnp.einsum(form, left, right, precision=FULL_PRECISION)

def matmul(left, right):
    return jnp.dot(left, right, precision=FULL_PRECISION)

def layer_norm(values, norm_gain, norm_bias):
    center = values - lax.optimization_barrier(jnp.mean(values, -1, keepdims=True))
    spread = lax.rsqrt(lax.optimization_barrier(jnp.mean(center * center, -1, keepdims=True)) + EPSILON)
    normed = center * spread
    return (normed, spread, norm_gain * normed + norm_bias)

def rms_norm(values, norm_gain):
    return values * lax.rsqrt(lax.optimization_barrier(jnp.mean(values * values, -1, keepdims=True)) + EPSILON) * norm_gain

def minibatch(state, inputs, initial, norm_gain, norm_bias):
    queries, keys_in, values_in, rates, reset = inputs
    first_w, first_b, second_w, second_b = [reset * begin + (1.0 - reset) * carry for begin, carry in zip(initial, state)]
    gain_row = norm_gain[:, None, :]
    bias_row = norm_bias[:, None, :]
    key_pre = product('hbf,hfi->hbi', keys_in, first_w) + first_b[:, None, :]
    key_act = gelu_exact(key_pre)
    key_out = product('hbi,hif->hbf', key_act, second_w) + second_b[:, None, :]
    normed, spread, fitted = layer_norm(key_out, gain_row, bias_row)
    shares = gain_row * (fitted - (values_in - keys_in))
    grad_out = spread * (shares - lax.optimization_barrier(jnp.mean(shares, -1, keepdims=True)) - normed * lax.optimization_barrier(jnp.mean(shares * normed, -1, keepdims=True)))
    grad_pre = product('hbf,hif->hbi', grad_out, second_w) * gelu_slope(key_pre)
    block = queries.shape[1]
    lower = jnp.tril(jnp.ones((block, block), queries.dtype))
    weigh_first = (product('hbf,hcf->hbc', queries, keys_in) + 1.0) * lower * rates[:, None, :]
    query_pre = product('hbf,hfi->hbi', queries, first_w) + first_b[:, None, :] - product('hbc,hci->hbi', weigh_first, grad_pre)
    query_act = gelu_exact(query_pre)
    weigh_second = (product('hbi,hci->hbc', query_act, key_act) + 1.0) * lower * rates[:, None, :]
    query_out = product('hbi,hif->hbf', query_act, second_w) + second_b[:, None, :] - product('hbc,hcf->hbf', weigh_second, grad_out)
    result = queries + layer_norm(query_out, gain_row, bias_row)[2]
    scaled_pre = rates[:, :, None] * grad_pre
    scaled_out = rates[:, :, None] * grad_out
    new_state = (first_w - product('hbf,hbi->hfi', keys_in, scaled_pre), first_b - lax.optimization_barrier(jnp.sum(scaled_pre, 1)), second_w - product('hbi,hbf->hif', key_act, scaled_out), second_b - lax.optimization_barrier(jnp.sum(scaled_out, 1)))
    return (new_state, result)

def inner_core(queries, keys_in, values_in, rate_pre, live, segments, first_w, first_b, second_w, second_b, norm_gain, norm_bias):
    length = queries.shape[0]
    blocks = length // MB
    heads = norm_gain.shape[0]
    width = norm_gain.shape[1]
    rates = BASE_RATE / width * jax.nn.sigmoid(rate_pre) * live[:, None]
    reset = jnp.concatenate([jnp.ones((1,), queries.dtype), (segments[MB::MB] != segments[MB - 1:-1:MB]).astype(queries.dtype)])

    def split(values):
        return values.reshape(blocks, MB, heads, width).transpose(0, 2, 1, 3)
    rate_blocks = rates.reshape(blocks, MB, heads).transpose(0, 2, 1)
    initial = (first_w, first_b, second_w, second_b)
    step = jax.checkpoint(partial(minibatch, initial=initial, norm_gain=norm_gain, norm_bias=norm_bias))
    _, outputs = lax.scan(step, initial, (split(queries), split(keys_in), split(values_in), rate_blocks, reset))
    return outputs.transpose(0, 2, 1, 3).reshape(length, heads * width)

def layer_row(inputs, segments, live, norm1_gain, w_query, w_key, w_value, w_gate, w_rate, b_rate, inner_w1, inner_b1, inner_w2, inner_b2, inner_gain, inner_bias, w_out, norm2_gain, ffn_gate, ffn_up, ffn_down):
    normed = low(rms_norm(inputs, norm1_gain))
    queries = low_back(matmul(normed, w_query))
    keys_in = low_back(matmul(normed, w_key))
    values_in = low_back(matmul(normed, w_value))
    gate_pre = low_back(matmul(normed, w_gate))
    rate_pre = low_back(matmul(normed, w_rate)) + b_rate
    inner_out = inner_core(queries, keys_in, values_in, rate_pre, live, segments, inner_w1, inner_b1, inner_w2, inner_b2, inner_gain, inner_bias)
    gated = low(inner_out * gelu_exact(gate_pre))
    resid = inputs + low_back(matmul(gated, w_out))
    normed_two = low(rms_norm(resid, norm2_gain))
    gate_vals = low_back(matmul(normed_two, ffn_gate))
    up_vals = low_back(matmul(normed_two, ffn_up))
    act = low(jax.nn.silu(gate_vals) * up_vals)
    return resid + low_back(matmul(act, ffn_down))

def reference(tokens, cotangent, seg_ids, pad_mask, norm1_gain, w_query, w_key, w_value, w_gate, w_rate, b_rate, inner_w1, inner_b1, inner_w2, inner_b2, inner_gain, inner_bias, w_out, norm2_gain, ffn_gate, ffn_up, ffn_down):
    params = tuple((p.astype(jnp.float32) for p in (norm1_gain, w_query, w_key, w_value, w_gate, w_rate, b_rate, inner_w1, inner_b1, inner_w2, inner_b2, inner_gain, inner_bias, w_out, norm2_gain, ffn_gate, ffn_up, ffn_down)))

    def row_step(totals, row):
        row_tokens, row_cot, row_seg, row_mask = row
        live = row_mask.astype(jnp.float32)

        def forward(inputs, *weights):
            return layer_row(inputs, row_seg, live, *weights)
        output, pull = jax.vjp(forward, row_tokens.astype(jnp.float32), *params)
        grads = pull(row_cot.astype(jnp.float32))
        summed = tuple((total + grad for total, grad in zip(totals, grads[1:])))
        return (summed, (output.astype(jnp.bfloat16), grads[0]))
    zeros = tuple((jnp.zeros_like(p) for p in params))
    totals, (mixed, grad_tokens) = lax.scan(row_step, zeros, (tokens, cotangent, seg_ids, pad_mask))
    return (mixed, grad_tokens, totals[0], totals[1], totals[2], totals[3], totals[4], totals[5], totals[6], totals[7], totals[8], totals[9], totals[10], totals[11], totals[12], totals[13], totals[14], totals[15], totals[16], totals[17])
```

```python
from functools import partial

import jax
import jax.numpy as jnp
from jax import lax
from jax.experimental import pallas as pl
from jax.experimental.pallas import tpu as pltpu
from jax.sharding import PartitionSpec as P

MB = 16
EPSILON = 1e-06
BASE_RATE = 0.1
F32 = jnp.float32
BF16 = jnp.bfloat16
VMEM_BYTES = 56 * 2**20


def dot(left, right, left_dim=1, right_dim=0):
    return lax.dot_general(
        left, right, (((left_dim,), (right_dim,)), ((), ())), preferred_element_type=F32
    )


def low(values):
    return values.astype(BF16)


def gelu_parts(values):
    phi = 0.5 + 0.5 * lax.erf(values * 0.7071067811865476)
    density = jnp.exp(-0.5 * values * values) * 0.3989422804014327
    return (values * phi, phi + values * density, density * (2.0 - values * values))


def mean_last(values):
    return jnp.sum(values, -1, keepdims=True) * (1.0 / values.shape[-1])


def sum_rows(values):
    return jnp.sum(values, 0, keepdims=True)


def column_of(row):
    size = row.shape[1]
    return jnp.transpose(jnp.broadcast_to(row, (size, size)))[:, 0:1]


def segment_masks(seg_row):
    size = seg_row.shape[1]
    rows = lax.broadcasted_iota(jnp.int32, (size, size), 0)
    cols = lax.broadcasted_iota(jnp.int32, (size, size), 1)
    same = column_of(seg_row) == seg_row
    block = MB.bit_length() - 1
    later = lax.shift_right_logical(rows, block) > lax.shift_right_logical(cols, block)
    inclusive = jnp.where(same & (cols <= rows), 1.0, 0.0)
    strict = jnp.where(same & later, 1.0, 0.0)
    return (inclusive, strict)


def forward_kernel(
    seg_smem,
    seg_ref,
    live_ref,
    tok_ref,
    gain1_ref,
    wq_ref,
    wk_ref,
    wv_ref,
    wg_ref,
    wr_ref,
    br_ref,
    w1_ref,
    b1_ref,
    w2_ref,
    b2_ref,
    ig_ref,
    ib_ref,
    wo_ref,
    gain2_ref,
    normed_ref,
    normed_two_ref,
    resid_ref,
    gated_ref,
    gelu_ref,
    slope_ref,
    qk_ref,
    ecol_ref,
    erow_ref,
    fcol_ref,
    w2t_ref,
    slope1_ref,
    curve1_ref,
    act_ref,
    d1_ref,
    d2_ref,
    n_ref,
    s_ref,
    fit_ref,
    w2s_ref,
    p1_ref,
    p2_ref,
    slopeq_ref,
    nq_ref,
    sq_ref,
    q_s,
    k_s,
    v_s,
    out_s,
    w1_s,
    w1b_s,
    b1_s,
    w2_s,
    b2_s,
    b1f,
    b2f,
    igf,
    ibf,
):
    length, width = tok_ref.shape[1], tok_ref.shape[2]
    heads, head = w1_ref.shape[0], w1_ref.shape[1]
    blocks = length // MB
    tok = tok_ref[0].astype(F32)
    spread = lax.rsqrt(mean_last(tok * tok) + EPSILON)
    normed = low(tok * spread * gain1_ref[...].astype(F32))
    normed_ref[...] = normed
    seg_row = seg_ref[...].astype(F32)
    live = column_of(live_ref[...].astype(F32))
    rate_pre = dot(normed, wr_ref[...]) + br_ref[...].astype(F32)
    sig = jax.nn.sigmoid(rate_pre)
    rates = (BASE_RATE / head) * sig * live
    ecol_ref[...] = jnp.zeros(ecol_ref.shape, F32)
    ecol_ref[:, 0:heads] = rates
    fcol_ref[...] = jnp.zeros(fcol_ref.shape, F32)
    fcol_ref[:, 0:heads] = rates * (1.0 - sig)
    erow_ref[...] = jnp.transpose(ecol_ref[...])[0 : erow_ref.shape[0]]
    for w_ref, to in ((wq_ref, q_s), (wk_ref, k_s), (wv_ref, v_s)):
        whole = dot(normed, w_ref[...])
        for h in range(heads):
            to[h] = whole[:, h * head : (h + 1) * head]
    b1f[...] = b1_ref[...].astype(F32)
    b2f[...] = b2_ref[...].astype(F32)
    igf[...] = ig_ref[...].astype(F32)
    ibf[...] = ib_ref[...].astype(F32)
    for h in range(heads):
        qk_ref[h, 0:length] = low(q_s[h])
        qk_ref[h, length : 2 * length] = low(k_s[h])
        w2t_ref[h] = low(jnp.transpose(w2_ref[h].astype(F32)))

    def step(b, carry):
        here = pl.multiple_of(b * MB, MB)
        before = jnp.maximum(here - 1, 0)
        fresh = (b == 0) | (seg_smem[0, here] != seg_smem[0, before])

        @pl.when(fresh)
        def _():
            for h in range(heads):
                first = w1_ref[h]
                second = w2t_ref[h]
                w1_s[h] = first.astype(F32)
                w1b_s[h] = first
                w2_s[h] = second.astype(F32)
                w2s_ref[b, h] = second
                b1_s[h] = b1f[h : h + 1]
                b2_s[h] = b2f[h : h + 1]

        @pl.when(jnp.logical_not(fresh))
        def _():
            for h in range(heads):
                w2s_ref[b, h] = low(w2_s[h])

        ds = pl.ds(here, MB)
        rng = range(heads)
        k = [k_s[h, ds, :] for h in rng]
        v = [v_s[h, ds, :] for h in rng]
        e = [ecol_ref[ds, h : h + 1] for h in rng]
        w1 = [w1b_s[h] for h in rng]
        w2 = [w2s_ref[b, h] for h in rng]
        w1f = [w1_s[h] for h in rng]
        w2f = [w2_s[h] for h in rng]
        b1 = [b1_s[h] for h in rng]
        b2 = [b2_s[h] for h in rng]
        g = [igf[h : h + 1] for h in rng]
        gb = [ibf[h : h + 1] for h in rng]
        parts = [gelu_parts(dot(low(k[h]), w1[h]) + b1[h]) for h in rng]
        act = [low(parts[h][0]) for h in rng]
        z2 = [dot(act[h], w2[h], 1, 1) + b2[h] for h in rng]
        c = [z - mean_last(z) for z in z2]
        s = [lax.rsqrt(mean_last(x * x) + EPSILON) for x in c]
        n = [c[h] * s[h] for h in rng]
        fit = [g[h] * n[h] + gb[h] - (v[h] - k[h]) for h in rng]
        share = [g[h] * fit[h] for h in rng]
        m1 = [mean_last(share[h]) for h in rng]
        m2 = [mean_last(share[h] * n[h]) for h in rng]
        d2 = [s[h] * (share[h] - m1[h] - n[h] * m2[h]) for h in rng]
        back = [dot(low(d2[h]), w2[h]) for h in rng]
        d1 = [back[h] * parts[h][1] for h in rng]
        d1b = [low(d1[h]) for h in rng]
        ed2 = [d2[h] * e[h] for h in rng]
        up1 = [dot(low(k[h] * e[h]), d1b[h], 0, 0) for h in rng]
        up2 = [dot(low(ed2[h]), act[h], 0, 0) for h in rng]
        for h in rng:
            w1n = w1f[h] - up1[h]
            w1_s[h] = w1n
            w1b_s[h] = low(w1n)
            w2_s[h] = w2f[h] - up2[h]
            b1_s[h] = b1[h] - sum_rows(d1[h] * e[h])
            b2_s[h] = b2[h] - sum_rows(ed2[h])
            act_ref[h, pl.ds(length + here, MB), :] = act[h]
            slope1_ref[h, ds, :] = low(parts[h][1])
            curve1_ref[h, ds, :] = low(back[h] * parts[h][2])
            d1_ref[h, ds, :] = d1b[h]
            d2_ref[h, ds, :] = d2[h]
            n_ref[h, ds, :] = n[h]
            s_ref[h, ds, :] = s[h]
            fit_ref[h, ds, :] = fit[h]
        return carry

    lax.fori_loop(0, blocks, step, 0)
    inclusive, _ = segment_masks(seg_row)
    for h in range(heads):
        queries = qk_ref[h, 0:length]
        keys = qk_ref[h, length : 2 * length]
        key_act = act_ref[h, length : 2 * length]
        er = erow_ref[h : h + 1, :]
        p1 = (dot(queries, keys, 1, 1) + 1.0) * inclusive
        p1_ref[h] = low(p1)
        zq1 = dot(queries, w1_ref[h]) + b1f[h : h + 1] - dot(low(p1 * er), d1_ref[h])
        aq, slope, _ = gelu_parts(zq1)
        aqb = low(aq)
        act_ref[h, 0:length] = aqb
        slopeq_ref[h] = low(slope)
        p2 = (dot(aqb, key_act, 1, 1) + 1.0) * inclusive
        p2_ref[h] = low(p2)
        zq2 = dot(aqb, w2t_ref[h], 1, 1) + b2f[h : h + 1] - dot(low(p2 * er), low(d2_ref[h]))
        c = zq2 - mean_last(zq2)
        s = lax.rsqrt(mean_last(c * c) + EPSILON)
        n = c * s
        nq_ref[h] = n
        sq_ref[h] = s
        out_s[:, h * head : (h + 1) * head] = q_s[h] + igf[h : h + 1] * n + ibf[h : h + 1]
    inner_out = out_s[...]
    gate, slope, _ = gelu_parts(dot(normed, wg_ref[...]))
    gelu_ref[...] = gate
    slope_ref[...] = inner_out * slope
    gated = low(inner_out * gate)
    gated_ref[...] = gated
    resid = tok + dot(gated, wo_ref[...])
    resid_ref[...] = resid
    spread_two = lax.rsqrt(mean_last(resid * resid) + EPSILON)
    normed_two_ref[...] = low(resid * spread_two * gain2_ref[...].astype(F32))


def ffn_kernel(x_ref, c_ref, wg_ref, wu_ref, wd_ref, act_ref, gg_ref, gu_ref, gx_ref):
    x = x_ref[...]
    gate = dot(x, wg_ref[...])
    up = dot(x, wu_ref[...])
    grad_act = dot(c_ref[...], wd_ref[...], 1, 1)
    sigma = jax.nn.sigmoid(gate)
    silu = gate * sigma
    act_ref[...] = low(silu * up)
    gg = low(grad_act * up * sigma * (1.0 + gate * (1.0 - sigma)))
    gu = low(grad_act * silu)
    gg_ref[...] = gg
    gu_ref[...] = gu
    gx_ref[...] = low(dot(gg, wg_ref[...], 1, 1) + dot(gu, wu_ref[...], 1, 1))


def ffn_weights_kernel(parts, *refs):
    x_refs, c_refs, act_refs, gg_refs, gu_refs = (
        refs[i * parts : (i + 1) * parts] for i in range(5)
    )
    wd_ref = refs[5 * parts]
    grad_gate_ref, grad_up_ref, grad_down_ref = refs[5 * parts + 1 : 5 * parts + 4]
    out_refs = refs[5 * parts + 4 : 6 * parts + 4]
    x_s, c_s, act_s, gg_s, gu_s = refs[6 * parts + 4 :]
    rows = x_refs[0].shape[0]
    for i in range(parts):
        at = slice(i * rows, (i + 1) * rows)
        x_s[at] = x_refs[i][...]
        c_s[at] = c_refs[i][...]
        act_s[at] = act_refs[i][...]
        gg_s[at] = gg_refs[i][...]
        gu_s[at] = gu_refs[i][...]
        out_refs[i][...] = low(dot(act_refs[i][...], wd_ref[...]))
    grad_gate_ref[...] = low(dot(x_s[...], gg_s[...], 0, 0))
    grad_up_ref[...] = low(dot(x_s[...], gu_s[...], 0, 0))
    grad_down_ref[...] = low(dot(act_s[...], c_s[...], 0, 0))


def between_kernel(parts, *refs):
    pieces = refs[0:parts]
    resid_ref, cot_ref, gain2_ref, wo_ref, gelu_ref, slope_ref, gated_ref, normed_ref = refs[
        parts : parts + 8
    ]
    resid_grad_ref, go_ref, gg_ref, gwo_ref, gwg_ref, gain_grad_ref = refs[parts + 8 :]
    grad = pieces[0][...].astype(F32)
    for piece in pieces[1:]:
        grad = grad + piece[...].astype(F32)
    resid = resid_ref[...]
    spread = lax.rsqrt(mean_last(resid * resid) + EPSILON)
    scaled = gain2_ref[...].astype(F32) * grad
    grad_resid = (
        cot_ref[0].astype(F32)
        + spread * scaled
        - resid * (spread * spread * spread * mean_last(scaled * resid))
    )
    gain_grad_ref[...] = sum_rows(grad * resid * spread)
    resid_grad_ref[...] = grad_resid
    grad_branch = low(grad_resid)
    grad_gated = dot(grad_branch, wo_ref[...], 1, 1)
    go_ref[...] = grad_gated * gelu_ref[...]
    grad_gates = low(grad_gated * slope_ref[...])
    gg_ref[...] = grad_gates
    gwo_ref[...] = low(dot(gated_ref[...], grad_branch, 0, 0))
    gwg_ref[...] = low(dot(normed_ref[...], grad_gates, 0, 0))


def backward_kernel(
    seg_smem,
    seg_ref,
    go_ref,
    normed_ref,
    qk_ref,
    ecol_ref,
    erow_ref,
    fcol_ref,
    w1_ref,
    w2t_ref,
    ig_ref,
    slope1_ref,
    curve1_ref,
    act_ref,
    d1_ref,
    d2_ref,
    n_ref,
    s_ref,
    fit_ref,
    w2s_ref,
    p1_ref,
    p2_ref,
    slopeq_ref,
    nq_ref,
    sq_ref,
    gq_ref,
    gk_ref,
    gv_ref,
    gr_ref,
    gw_ref,
    ginner_ref,
    small_ref,
    igf,
    t1_s,
    t2_s,
    ga_s,
    hh1_s,
    hh2_s,
    u_s,
    share_s,
    ge_s,
    gw1_s,
    gw1b_s,
    gb1_s,
    gw2_s,
    gw2b_s,
    gb2_s,
):
    length = go_ref.shape[0]
    heads, head, inner = w1_ref.shape
    blocks = length // MB
    top, bottom = slice(0, length), slice(length, 2 * length)
    igf[...] = ig_ref[...].astype(F32)
    inclusive, strict = segment_masks(seg_ref[...].astype(F32))
    for h in range(heads):
        g = igf[h : h + 1]
        er = erow_ref[h : h + 1, :]
        go = go_ref[:, h * head : (h + 1) * head]
        n = nq_ref[h]
        x = go * g
        hq2 = low(sq_ref[h] * (x - mean_last(x) - n * mean_last(x * n)))
        hh2_s[h, top] = hq2
        t2_s[h] = dot(p2_ref[h], hq2, 0, 0)
        mix = low(-dot(hq2, low(d2_ref[h]), 1, 1) * (inclusive * er))
        aq = act_ref[h, top]
        gaq = dot(hq2, w2t_ref[h]) + dot(mix, act_ref[h, bottom])
        ga_s[h] = dot(mix, aq, 0, 0)
        hq1 = low(gaq * slopeq_ref[h].astype(F32))
        hh1_s[h, top] = hq1
        t1_s[h] = dot(p1_ref[h], hq1, 0, 0)
    ge_s[...] = jnp.zeros(ge_s.shape, F32)

    def step(i, carry):
        b = blocks - 1 - i
        here = pl.multiple_of(b * MB, MB)
        after = jnp.minimum(here + MB, length - 1)
        fresh = (i == 0) | (seg_smem[0, after] != seg_smem[0, after - 1])

        @pl.when(fresh)
        def _():
            for ref in (gw1_s, gw1b_s, gb1_s, gw2_s, gw2b_s, gb2_s):
                ref[...] = jnp.zeros(ref.shape, ref.dtype)

        ds = pl.ds(here, MB)
        ds_low = pl.ds(length + here, MB)
        rng = range(heads)
        k = [qk_ref[h, ds_low, :] for h in rng]
        act = [act_ref[h, ds_low, :] for h in rng]
        e = [ecol_ref[ds, h : h + 1] for h in rng]
        w2 = [w2s_ref[b, h] for h in rng]
        gw1b = [gw1b_s[h] for h in rng]
        gw2b = [gw2b_s[h] for h in rng]
        gw1 = [gw1_s[h] for h in rng]
        gw2 = [gw2_s[h] for h in rng]
        gb1 = [gb1_s[h] for h in rng]
        gb2 = [gb2_s[h] for h in rng]
        d1 = [d1_ref[h, ds, :].astype(F32) for h in rng]
        d2 = [d2_ref[h, ds, :] for h in rng]
        n = [n_ref[h, ds, :] for h in rng]
        s = [s_ref[h, ds, :] for h in rng]
        fit = [fit_ref[h, ds, :] for h in rng]
        slope = [slope1_ref[h, ds, :].astype(F32) for h in rng]
        curve = [curve1_ref[h, ds, :].astype(F32) for h in rng]
        g = [igf[h : h + 1] for h in rng]
        share = [g[h] * fit[h] for h in rng]
        t1 = [t1_s[h, ds, :] + dot(k[h], gw1b[h]) + gb1[h] for h in rng]
        t2 = [t2_s[h, ds, :] + dot(act[h], gw2b[h], 1, 1) + gb2[h] for h in rng]
        g1 = [-e[h] * t1[h] for h in rng]
        u = [low(g1[h] * slope[h]) for h in rng]
        ed2 = [low(-e[h] * d2[h]) for h in rng]
        ga = [ga_s[h, ds, :] + dot(ed2[h], gw2b[h]) for h in rng]
        g2 = [dot(u[h], w2[h], 1, 1) - e[h] * t2[h] for h in rng]
        y = [s[h] * g2[h] for h in rng]
        my = [mean_last(y[h]) for h in rng]
        myn = [mean_last(y[h] * n[h]) for h in rng]
        msn = [mean_last(share[h] * n[h]) for h in rng]
        mgd = [mean_last(g2[h] * d2[h]) for h in rng]
        gshare = [y[h] - my[h] - n[h] * myn[h] for h in rng]
        gn = [g[h] * (g[h] * gshare[h]) - y[h] * msn[h] - share[h] * myn[h] for h in rng]
        mn = [mean_last(gn[h]) for h in rng]
        mnn = [mean_last(gn[h] * n[h]) for h in rng]
        h2 = [
            low(s[h] * (gn[h] - mn[h] - n[h] * (mnn[h] + mgd[h]))) for h in rng
        ]
        ga = [ga[h] + dot(h2[h], w2[h]) for h in rng]
        h1f = [ga[h] * slope[h] + g1[h] * curve[h] for h in rng]
        h1 = [low(x) for x in h1f]
        up1 = [dot(k[h], h1[h], 0, 0) for h in rng]
        up2 = [
            dot(low(d2[h]), u[h], 0, 0) + dot(h2[h], act[h], 0, 0) for h in rng
        ]
        for h in rng:
            w1n = gw1[h] + up1[h]
            w2n = gw2[h] + up2[h]
            gw1_s[h] = w1n
            gw1b_s[h] = low(w1n)
            gw2_s[h] = w2n
            gw2b_s[h] = low(w2n)
            gb1_s[h] = gb1[h] + sum_rows(h1f[h])
            gb2_s[h] = gb2[h] + sum_rows(h2[h].astype(F32))
            u_s[h, ds, :] = u[h]
            hh1_s[h, ds_low, :] = h1[h]
            hh2_s[h, ds_low, :] = h2[h]
            share_s[h, ds, :] = gshare[h]
            ge_s[ds, h : h + 1] = -jnp.sum(d1[h] * t1[h], -1, keepdims=True) - jnp.sum(
                d2[h] * t2[h], -1, keepdims=True
            )
        return carry

    lax.fori_loop(0, blocks, step, 0)
    small_ref[...] = jnp.zeros(small_ref.shape, F32)
    per_row = small_ref.shape[1] // inner
    for h in range(heads):
        cols = slice(h * head, (h + 1) * head)
        g = igf[h : h + 1]
        er = erow_ref[h : h + 1, :]
        hh1 = hh1_s[h]
        hh2 = hh2_s[h]
        qk = qk_ref[h]
        keys = qk_ref[h, bottom]
        both = dot(hh1, d1_ref[h], 1, 1)
        mixq = low(-both[top] * (inclusive * er))
        mixk = low(-both[bottom] * (strict * er))
        direct = dot(hh1, w1_ref[h], 1, 1)
        share = share_s[h]
        spread = dot(mixq, qk_ref[h, top], 0, 0) + dot(mixk, keys, 0, 0)
        go = go_ref[:, cols]
        gq_ref[:, cols] = low(go + direct[top] + dot(mixq, keys))
        gk_ref[:, cols] = low(g * share + direct[bottom] + dot(mixk, keys) + spread)
        gv_ref[:, cols] = low(-g * share)
        ginner_ref[h] = low(dot(qk, hh1, 0, 0))
        ginner_ref[heads + h] = low(
            dot(hh2, act_ref[h], 0, 0) + dot(low(d2_ref[h]), u_s[h], 0, 0)
        )
        row, lane = 14 + h // per_row, (h % per_row) * inner
        small_ref[row : row + 1, lane : lane + inner] = sum_rows(hh1.astype(F32))
        row = 14 + heads // per_row
        small_ref[row : row + 1, cols] = sum_rows(hh2.astype(F32))
        small_ref[row + 1 : row + 2, cols] = sum_rows(go * nq_ref[h]) + sum_rows(
            share * (fit_ref[h] + g * n_ref[h])
        )
        small_ref[row + 2 : row + 3, cols] = sum_rows(go) + g * sum_rows(share)
    grad_rates = ge_s[...] * fcol_ref[...]
    row = 17 + heads // per_row
    small_ref[row : row + 1, 0 : grad_rates.shape[1]] = sum_rows(grad_rates)
    gr_ref[...] = low(grad_rates)
    normed = normed_ref[...]
    small_ref[2 : 2 + heads] = dot(low(grad_rates), normed, 0, 0)[0:heads]
    for i, ref in enumerate((gq_ref, gk_ref, gv_ref)):
        gw_ref[i] = low(dot(normed, ref[...], 0, 0))


def input_kernel(
    gq_ref,
    gk_ref,
    gv_ref,
    gg_ref,
    gr_ref,
    wq_ref,
    wk_ref,
    wv_ref,
    wg_ref,
    wr_ref,
    tok_ref,
    gain1_ref,
    resid_grad_ref,
    small_ref,
    gain_two_ref,
    grad_ref,
    small_out,
):
    heads = wr_ref.shape[1]
    grad = dot(gq_ref[...], wq_ref[...], 1, 1) + dot(gk_ref[...], wk_ref[...], 1, 1)
    grad = grad + dot(gv_ref[...], wv_ref[...], 1, 1) + dot(gg_ref[...], wg_ref[...], 1, 1)
    grad = grad + dot(gr_ref[:, 0:heads], wr_ref[...], 1, 1)
    tok = tok_ref[0].astype(F32)
    spread = lax.rsqrt(mean_last(tok * tok) + EPSILON)
    scaled = gain1_ref[...].astype(F32) * grad
    grad_ref[0] = (
        resid_grad_ref[...]
        + spread * scaled
        - tok * (spread * spread * spread * mean_last(scaled * tok))
    )
    small_out[...] = small_ref[...]
    small_out[0:1] = sum_rows(grad * tok * spread)
    small_out[1:2] = gain_two_ref[...]


def call(kernel, outs, inputs, scratch=(), smem=0):
    specs = [pl.BlockSpec(memory_space=pltpu.SMEM)] * smem
    specs += [pl.BlockSpec(memory_space=pltpu.VMEM)] * (len(inputs) - smem)
    return pl.pallas_call(
        kernel,
        out_shape=[jax.ShapeDtypeStruct(s, d) for s, d in outs],
        in_specs=specs,
        out_specs=[pl.BlockSpec(memory_space=pltpu.VMEM)] * len(outs),
        scratch_shapes=[pltpu.VMEM(s, d) for s, d in scratch],
        compiler_params=pltpu.CompilerParams(vmem_limit_bytes=VMEM_BYTES),
    )(*inputs)


def exchange(values, axis, size, distance):
    return lax.ppermute(values, axis, [(i, i ^ distance) for i in range(size)])


def add_low(left, right):
    return low(left.astype(F32) + right.astype(F32))


def halve(values, axis, size, distance, dim):
    side = lax.bitwise_and(lax.axis_index(axis) // distance, 1)
    half = values.shape[dim] // 2
    kept = lax.dynamic_slice_in_dim(values, side * half, half, dim)
    sent = lax.dynamic_slice_in_dim(values, (1 - side) * half, half, dim)
    return add_low(kept, exchange(sent, axis, size, distance))


def double(values, axis, size, distance, dim):
    side = lax.bitwise_and(lax.axis_index(axis) // distance, 1)
    other = exchange(values, axis, size, distance)
    return jnp.where(
        side == 0,
        jnp.concatenate([values, other], dim),
        jnp.concatenate([other, values], dim),
    )


def distances(size):
    found = []
    step = 1
    while step < size:
        found.append(step)
        step *= 2
    return found


def scatter_rows(values, size, dim):
    for d in distances(size):
        values = halve(values, "rows", size, d, dim)
    return values


def gather_rows(values, size, dim):
    for d in reversed(distances(size)):
        values = double(values, "rows", size, d, dim)
    return values


def scatter_feat(values, size, dim):
    me = lax.axis_index("feat")
    total = lax.dynamic_index_in_dim(values, me, dim, keepdims=False).astype(F32)
    for s in range(1, size):
        piece = lax.dynamic_index_in_dim(values, lax.bitwise_xor(me, s), dim, keepdims=False)
        total = total + exchange(piece, "feat", size, s).astype(F32)
    return low(total)


def on_device(
    rows,
    feats,
    tokens,
    cotangent,
    seg_ids,
    pad_mask,
    norm1_gain,
    w_query,
    w_key,
    w_value,
    w_gate,
    w_rate,
    b_rate,
    inner_w1,
    inner_b1,
    inner_w2,
    inner_b2,
    inner_gain,
    inner_bias,
    w_out,
    norm2_gain,
    ffn_gate,
    ffn_up,
    ffn_down,
):
    _, length, width = tokens.shape
    heads, head, inner = inner_w1.shape
    hidden = ffn_gate.shape[1]
    blocks = length // MB
    gain_one = norm1_gain[None]
    gain_two = norm2_gain[None]
    line = (length, width)
    wide = (heads, length, inner)
    slim = (heads, length, head)
    thin = (heads, length, 1)
    square = (heads, length, length)
    state = (heads, head, inner)
    cots = [cotangent[0]]
    for s in range(1, feats):
        cots.append(exchange(cots[0], "feat", feats, s))
    saved = call(
        forward_kernel,
        [
            (line, BF16),
            (line, BF16),
            (line, F32),
            (line, BF16),
            (line, F32),
            (line, F32),
            ((heads, 2 * length, head), BF16),
            ((length, 128), F32),
            ((16, length), F32),
            ((length, 128), F32),
            (state, BF16),
            (wide, BF16),
            (wide, BF16),
            ((heads, 2 * length, inner), BF16),
            (wide, BF16),
            (slim, F32),
            (slim, F32),
            (thin, F32),
            (slim, F32),
            ((blocks,) + state, BF16),
            (square, BF16),
            (square, BF16),
            (wide, BF16),
            (slim, F32),
            (thin, F32),
        ],
        [
            seg_ids,
            seg_ids,
            pad_mask,
            tokens,
            gain_one,
            w_query,
            w_key,
            w_value,
            w_gate,
            w_rate,
            b_rate[None],
            inner_w1,
            inner_b1,
            inner_w2,
            inner_b2,
            inner_gain,
            inner_bias,
            w_out,
            gain_two,
        ],
        [
            (slim, F32),
            (slim, F32),
            (slim, F32),
            (line, F32),
            (state, F32),
            (state, BF16),
            ((heads, 1, inner), F32),
            (state, F32),
            ((heads, 1, head), F32),
            ((heads, inner), F32),
            ((heads, head), F32),
            ((heads, head), F32),
            ((heads, head), F32),
        ],
        smem=1,
    )
    normed, normed_two, resid, gated, gelu_gate, gate_slope = saved[0:6]
    qk, ecol, erow, fcol, w2t = saved[6:11]
    rest = saved[11:]
    blocks_in = [normed_two]
    for s in range(1, feats):
        blocks_in.append(exchange(normed_two, "feat", feats, s))
    acts, ggs, gus, pieces = [], [], [], []
    for s in range(feats):
        act, gg, gu, gx = call(
            ffn_kernel,
            [((length, hidden), BF16)] * 3 + [(line, BF16)],
            [blocks_in[s], cots[s], ffn_gate, ffn_up, ffn_down],
        )
        acts.append(act)
        ggs.append(gg)
        gus.append(gu)
        pieces.append(gx if s == 0 else exchange(gx, "feat", feats, s))
    whole = feats * length
    ffn_grads = call(
        partial(ffn_weights_kernel, feats),
        [((width, hidden), BF16), ((width, hidden), BF16), ((hidden, width), BF16)]
        + [(line, BF16)] * feats,
        blocks_in + cots + acts + ggs + gus + [ffn_down],
        [((whole, width), BF16), ((whole, width), BF16)] + [((whole, hidden), BF16)] * 3,
    )
    ffn_out = ffn_grads[3].astype(F32)
    for s in range(1, feats):
        ffn_out = ffn_out + exchange(ffn_grads[3 + s], "feat", feats, s).astype(F32)
    mixed = low(resid + ffn_out)
    grad_resid, grad_inner_out, grad_gates, grad_w_out, grad_w_gate, grad_gain_two = call(
        partial(between_kernel, feats),
        [
            (line, F32),
            (line, F32),
            (line, BF16),
            ((width, width), BF16),
            ((width, width), BF16),
            ((1, width), F32),
        ],
        pieces
        + [resid, cotangent, gain_two, w_out, gelu_gate, gate_slope, gated, normed],
    )

    def shares(values):
        return values.reshape((feats, width // feats, width))

    def reduced_by_features(values):
        values = scatter_rows(values, rows, 1)
        values = scatter_feat(values, feats, 0)
        return gather_rows(values, rows, 0).astype(F32)

    def reduced_over_rows(values):
        return gather_rows(scatter_rows(values, rows, 0), rows, 0).astype(F32)

    total_ffn = [reduced_over_rows(x) for x in ffn_grads[0:3]]
    total_out = reduced_by_features(shares(grad_w_out))
    total_gate = reduced_by_features(shares(grad_w_gate))
    gq, gk, gv, gr, gw, ginner, small = call(
        backward_kernel,
        [
            (line, BF16),
            (line, BF16),
            (line, BF16),
            ((length, 128), BF16),
            ((3, width, width), BF16),
            ((2 * heads, head, inner), BF16),
            ((24, width), F32),
        ],
        [seg_ids, seg_ids, grad_inner_out, normed, qk, ecol, erow, fcol, inner_w1, w2t]
        + [inner_gain]
        + list(rest),
        [
            ((heads, head), F32),
            (wide, F32),
            (slim, F32),
            (wide, F32),
            ((heads, 2 * length, inner), BF16),
            ((heads, 2 * length, head), BF16),
            (wide, BF16),
            (slim, F32),
            ((length, 128), F32),
            (state, F32),
            (state, BF16),
            ((heads, 1, inner), F32),
            (state, F32),
            (state, BF16),
            ((heads, 1, head), F32),
        ],
        smem=1,
    )
    grad_tokens, small = call(
        input_kernel,
        [((1,) + line, F32), ((24, width), F32)],
        [gq, gk, gv, grad_gates, gr, w_query, w_key, w_value, w_gate, w_rate]
        + [tokens, gain_one, grad_resid, small, grad_gain_two],
    )
    totals = [reduced_by_features(shares(gw[i])) for i in range(3)]
    inner_sum = scatter_rows(ginner.reshape((-1, inner)), rows, 0)
    for d in distances(feats):
        inner_sum = add_low(inner_sum, exchange(inner_sum, "feat", feats, d))
    inner_sum = gather_rows(inner_sum, rows, 0).astype(F32).reshape((2,) + state)
    for d in distances(rows):
        small = small + exchange(small, "rows", rows, d)
    for d in distances(feats):
        small = small + exchange(small, "feat", feats, d)
    me = lax.axis_index("feat")
    mine = lax.dynamic_slice_in_dim(small, me * (width // feats), width // feats, 1)
    bias_rows = heads * inner // width
    at = 14 + bias_rows
    return (
        mixed[None],
        grad_tokens,
        mine[0],
        totals[0],
        totals[1],
        totals[2],
        total_gate,
        jnp.transpose(mine[2 : 2 + heads]),
        small[at + 3, 0:heads],
        inner_sum[0],
        small[14:at].reshape((heads, inner)),
        jnp.transpose(inner_sum[1], (0, 2, 1)),
        small[at].reshape((heads, head)),
        small[at + 1].reshape((heads, head)),
        small[at + 2].reshape((heads, head)),
        total_out,
        mine[1],
        total_ffn[0],
        total_ffn[1],
        total_ffn[2],
    )


def solution(mesh):
    batch = ("rows", "feat")
    placed = (
        (P(batch, None, None), P(batch, None, None), P(batch, None), P(batch, None))
        + (P(),) * 15
        + (P(None, "feat"), P(None, "feat"), P("feat", None))
    )
    return jax.shard_map(
        partial(on_device, mesh.shape["rows"], mesh.shape["feat"]),
        mesh=mesh,
        in_specs=placed,
        out_specs=(
            P(batch, None, None),
            P(batch, None, None),
            P("feat"),
            P("feat", None),
            P("feat", None),
            P("feat", None),
            P("feat", None),
            P("feat", None),
            P(),
            P(),
            P(),
            P(),
            P(),
            P(),
            P(),
            P("feat", None),
            P("feat"),
            P(None, "feat"),
            P(None, "feat"),
            P("feat", None),
        ),
        check_vma=False,
    )
```

```python
from functools import partial

import jax
import jax.numpy as jnp
from jax import lax
from jax.experimental import pallas as pl
from jax.experimental.pallas import tpu as pltpu
from jax.sharding import PartitionSpec as P

MB = 16
EPSILON = 1e-06
BASE_RATE = 0.1
F32 = jnp.float32
BF16 = jnp.bfloat16
VMEM_BYTES = 56 * 2**20


def dot(left, right, left_dim=1, right_dim=0):
    return lax.dot_general(
        left, right, (((left_dim,), (right_dim,)), ((), ())), preferred_element_type=F32
    )


def low(values):
    return values.astype(BF16)


def gelu_parts(values):
    phi = 0.5 + 0.5 * lax.erf(values * 0.7071067811865476)
    density = jnp.exp(-0.5 * values * values) * 0.3989422804014327
    return (values * phi, phi + values * density, density * (2.0 - values * values))


def mean_last(values):
    return jnp.sum(values, -1, keepdims=True) * (1.0 / values.shape[-1])


def sum_rows(values):
    return jnp.sum(values, 0, keepdims=True)


def column_of(row):
    size = row.shape[1]
    return jnp.transpose(jnp.broadcast_to(row, (size, size)))[:, 0:1]


def segment_masks(seg_row):
    size = seg_row.shape[1]
    rows = lax.broadcasted_iota(jnp.int32, (size, size), 0)
    cols = lax.broadcasted_iota(jnp.int32, (size, size), 1)
    same = column_of(seg_row) == seg_row
    block = MB.bit_length() - 1
    later = lax.shift_right_logical(rows, block) > lax.shift_right_logical(cols, block)
    inclusive = jnp.where(same & (cols <= rows), 1.0, 0.0)
    strict = jnp.where(same & later, 1.0, 0.0)
    return (inclusive, strict)


def forward_kernel(
    seg_smem,
    seg_ref,
    live_ref,
    tok_ref,
    gain1_ref,
    wq_ref,
    wk_ref,
    wv_ref,
    wg_ref,
    wr_ref,
    br_ref,
    w1_ref,
    b1_ref,
    w2t_ref,
    b2_ref,
    ig_ref,
    ib_ref,
    wo_ref,
    gain2_ref,
    pair_ref,
    normed_two_ref,
    resid_ref,
    gelu_ref,
    slope_ref,
    qk_ref,
    ecol_ref,
    erow_ref,
    fcol_ref,
    slope1_ref,
    curve1_ref,
    act_ref,
    d1_ref,
    d2_ref,
    n_ref,
    s_ref,
    fit_ref,
    w2s_ref,
    p1_ref,
    p2_ref,
    slopeq_ref,
    nq_ref,
    sq_ref,
    q_s,
    k_s,
    v_s,
    out_s,
    w1_s,
    w1b_s,
    b1_s,
    w2_s,
    b2_s,
    b1f,
    b2f,
    igf,
    ibf,
):
    length, width = tok_ref.shape[1], tok_ref.shape[2]
    heads, head = w1_ref.shape[0], w1_ref.shape[1]
    blocks = length // MB
    tok = tok_ref[0].astype(F32)
    spread = lax.rsqrt(mean_last(tok * tok) + EPSILON)
    normed = low(tok * spread * gain1_ref[...].astype(F32))
    pair_ref[0] = normed
    seg_row = seg_ref[...].astype(F32)
    live = column_of(live_ref[...].astype(F32))
    rate_pre = dot(normed, wr_ref[...], 1, 1) + br_ref[...].astype(F32)
    sig = jax.nn.sigmoid(rate_pre)
    rates = (BASE_RATE / head) * sig * live
    ecol_ref[...] = jnp.zeros(ecol_ref.shape, F32)
    ecol_ref[:, 0:heads] = rates
    fcol_ref[...] = jnp.zeros(fcol_ref.shape, F32)
    fcol_ref[:, 0:heads] = rates * (1.0 - sig)
    erow_ref[...] = jnp.transpose(ecol_ref[...])[0 : erow_ref.shape[0]]
    for w_ref, to in ((wq_ref, q_s), (wk_ref, k_s), (wv_ref, v_s)):
        whole = dot(normed, w_ref[...])
        for h in range(heads):
            to[h] = whole[:, h * head : (h + 1) * head]
    b1f[...] = b1_ref[...].astype(F32)
    b2f[...] = b2_ref[...].astype(F32)
    igf[...] = ig_ref[...].astype(F32)
    ibf[...] = ib_ref[...].astype(F32)
    for h in range(heads):
        qk_ref[h, 0:length] = low(q_s[h])
        qk_ref[h, length : 2 * length] = low(k_s[h])

    def step(b, carry):
        here = pl.multiple_of(b * MB, MB)
        before = jnp.maximum(here - 1, 0)
        fresh = (b == 0) | (seg_smem[0, here] != seg_smem[0, before])

        @pl.when(fresh)
        def _():
            for h in range(heads):
                first = w1_ref[h]
                second = w2t_ref[h]
                w1_s[h] = first.astype(F32)
                w1b_s[h] = first
                w2_s[h] = second.astype(F32)
                w2s_ref[b, h] = second
                b1_s[h] = b1f[h : h + 1]
                b2_s[h] = b2f[h : h + 1]

        @pl.when(jnp.logical_not(fresh))
        def _():
            for h in range(heads):
                w2s_ref[b, h] = low(w2_s[h])

        ds = pl.ds(here, MB)
        rng = range(heads)
        k = [k_s[h, ds, :] for h in rng]
        v = [v_s[h, ds, :] for h in rng]
        e = [ecol_ref[ds, h : h + 1] for h in rng]
        w1 = [w1b_s[h] for h in rng]
        w2 = [w2s_ref[b, h] for h in rng]
        w1f = [w1_s[h] for h in rng]
        w2f = [w2_s[h] for h in rng]
        b1 = [b1_s[h] for h in rng]
        b2 = [b2_s[h] for h in rng]
        g = [igf[h : h + 1] for h in rng]
        gb = [ibf[h : h + 1] for h in rng]
        parts = [gelu_parts(dot(low(k[h]), w1[h]) + b1[h]) for h in rng]
        act = [low(parts[h][0]) for h in rng]
        z2 = [dot(act[h], w2[h], 1, 1) + b2[h] for h in rng]
        c = [z - mean_last(z) for z in z2]
        s = [lax.rsqrt(mean_last(x * x) + EPSILON) for x in c]
        n = [c[h] * s[h] for h in rng]
        fit = [g[h] * n[h] + gb[h] - (v[h] - k[h]) for h in rng]
        share = [g[h] * fit[h] for h in rng]
        m1 = [mean_last(share[h]) for h in rng]
        m2 = [mean_last(share[h] * n[h]) for h in rng]
        d2 = [s[h] * (share[h] - m1[h] - n[h] * m2[h]) for h in rng]
        back = [dot(low(d2[h]), w2[h]) for h in rng]
        d1 = [back[h] * parts[h][1] for h in rng]
        d1b = [low(d1[h]) for h in rng]
        ed2 = [d2[h] * e[h] for h in rng]
        up1 = [dot(low(k[h] * e[h]), d1b[h], 0, 0) for h in rng]
        up2 = [dot(low(ed2[h]), act[h], 0, 0) for h in rng]
        for h in rng:
            w1n = w1f[h] - up1[h]
            w1_s[h] = w1n
            w1b_s[h] = low(w1n)
            w2_s[h] = w2f[h] - up2[h]
            b1_s[h] = b1[h] - sum_rows(d1[h] * e[h])
            b2_s[h] = b2[h] - sum_rows(ed2[h])
            act_ref[h, pl.ds(length + here, MB), :] = act[h]
            slope1_ref[h, ds, :] = low(parts[h][1])
            curve1_ref[h, ds, :] = low(back[h] * parts[h][2])
            d1_ref[h, ds, :] = d1b[h]
            d2_ref[h, ds, :] = d2[h]
            n_ref[h, ds, :] = n[h]
            s_ref[h, ds, :] = s[h]
            fit_ref[h, ds, :] = fit[h]
        return carry

    lax.fori_loop(0, blocks, step, 0)
    inclusive, _ = segment_masks(seg_row)
    for h in range(heads):
        queries = qk_ref[h, 0:length]
        keys = qk_ref[h, length : 2 * length]
        key_act = act_ref[h, length : 2 * length]
        er = erow_ref[h : h + 1, :]
        p1 = (dot(queries, keys, 1, 1) + 1.0) * inclusive
        p1_ref[h] = low(p1)
        zq1 = dot(queries, w1_ref[h]) + b1f[h : h + 1] - dot(low(p1 * er), d1_ref[h])
        aq, slope, _ = gelu_parts(zq1)
        aqb = low(aq)
        act_ref[h, 0:length] = aqb
        slopeq_ref[h] = low(slope)
        p2 = (dot(aqb, key_act, 1, 1) + 1.0) * inclusive
        p2_ref[h] = low(p2)
        zq2 = dot(aqb, w2t_ref[h], 1, 1) + b2f[h : h + 1] - dot(low(p2 * er), low(d2_ref[h]))
        c = zq2 - mean_last(zq2)
        s = lax.rsqrt(mean_last(c * c) + EPSILON)
        n = c * s
        nq_ref[h] = n
        sq_ref[h] = s
        out_s[:, h * head : (h + 1) * head] = q_s[h] + igf[h : h + 1] * n + ibf[h : h + 1]
    inner_out = out_s[...]
    gate, slope, _ = gelu_parts(dot(normed, wg_ref[...]))
    gelu_ref[...] = gate
    slope_ref[...] = inner_out * slope
    gated = low(inner_out * gate)
    pair_ref[1] = gated
    resid = tok + dot(gated, wo_ref[...])
    resid_ref[...] = resid
    spread_two = lax.rsqrt(mean_last(resid * resid) + EPSILON)
    normed_two_ref[...] = low(resid * spread_two * gain2_ref[...].astype(F32))


def ffn_kernel(x_ref, c_ref, wg_ref, wu_ref, wd_ref, act_ref, gg_ref, gu_ref, gx_ref):
    x = x_ref[...]
    gate = dot(x, wg_ref[...])
    up = dot(x, wu_ref[...])
    grad_act = dot(c_ref[...], wd_ref[...], 1, 1)
    sigma = jax.nn.sigmoid(gate)
    silu = gate * sigma
    act_ref[...] = low(silu * up)
    gg = low(grad_act * up * sigma * (1.0 + gate * (1.0 - sigma)))
    gu = low(grad_act * silu)
    gg_ref[...] = gg
    gu_ref[...] = gu
    gx_ref[...] = low(dot(gg, wg_ref[...], 1, 1) + dot(gu, wu_ref[...], 1, 1))


def ffn_weights_kernel(parts, ids_smem, *refs):
    x_refs, c_refs, act_refs, gg_refs, gu_refs = (
        refs[i * parts : (i + 1) * parts] for i in range(5)
    )
    wd_ref, kept_ref, sent_ref = refs[5 * parts : 5 * parts + 3]
    out_refs = refs[5 * parts + 3 : 6 * parts + 3]
    x_s, c_s, act_s, gg_s, gu_s = refs[6 * parts + 3 :]
    rows = x_refs[0].shape[0]
    for i in range(parts):
        at = slice(i * rows, (i + 1) * rows)
        x_s[at] = x_refs[i][...]
        c_s[at] = c_refs[i][...]
        act_s[at] = act_refs[i][...]
        gg_s[at] = gg_refs[i][...]
        gu_s[at] = gu_refs[i][...]
        out_refs[i][...] = low(dot(act_refs[i][...], wd_ref[...]))
    half = kept_ref.shape[2]
    core = ids_smem[0]
    for i, (left, right) in enumerate(((x_s, gg_s), (x_s, gu_s), (c_s, act_s))):
        whole = low(dot(left[...], right[...], 0, 0))

        @pl.when(core == 0)
        def _(whole=whole, i=i):
            kept_ref[i] = whole[:, 0:half]
            sent_ref[i] = whole[:, half:]

        @pl.when(core != 0)
        def _(whole=whole, i=i):
            kept_ref[i] = whole[:, half:]
            sent_ref[i] = whole[:, 0:half]


def cut_rows_kernel(ids_smem, kept_ref, got_ref, *out_refs):
    chip = ids_smem[1]
    rows = out_refs[0].shape[1]
    for s, out in enumerate(out_refs):
        at = pl.ds(pl.multiple_of(lax.bitwise_xor(chip, s) * rows, rows), rows)
        out[...] = low(kept_ref[:, at, :].astype(F32) + got_ref[:, at, :].astype(F32))


def between_kernel(parts, *refs):
    pieces = refs[0:parts]
    resid_ref, cot_ref, gain2_ref, wo_ref, gelu_ref, slope_ref = refs[parts : parts + 6]
    resid_grad_ref, go_ref, pair_ref, gain_grad_ref = refs[parts + 6 :]
    grad = pieces[0][...].astype(F32)
    for piece in pieces[1:]:
        grad = grad + piece[...].astype(F32)
    resid = resid_ref[...]
    spread = lax.rsqrt(mean_last(resid * resid) + EPSILON)
    scaled = gain2_ref[...].astype(F32) * grad
    grad_resid = (
        cot_ref[0].astype(F32)
        + spread * scaled
        - resid * (spread * spread * spread * mean_last(scaled * resid))
    )
    gain_grad_ref[...] = sum_rows(grad * resid * spread)
    resid_grad_ref[...] = grad_resid
    grad_branch = low(grad_resid)
    grad_gated = dot(grad_branch, wo_ref[...], 1, 1)
    go_ref[...] = grad_gated * gelu_ref[...]
    pair_ref[0] = low(grad_gated * slope_ref[...])
    pair_ref[1] = grad_branch


def backward_kernel(
    ids_smem,
    seg_smem,
    seg_ref,
    go_ref,
    qk_ref,
    ecol_ref,
    erow_ref,
    fcol_ref,
    w1_ref,
    w2t_ref,
    ig_ref,
    slope1_ref,
    curve1_ref,
    act_ref,
    d1_ref,
    d2_ref,
    n_ref,
    s_ref,
    fit_ref,
    w2s_ref,
    p1_ref,
    p2_ref,
    slopeq_ref,
    nq_ref,
    sq_ref,
    triple_ref,
    gr_ref,
    kept_ref,
    sent_ref,
    small_ref,
    igf,
    t1_s,
    t2_s,
    ga_s,
    hh1_s,
    hh2_s,
    u_s,
    share_s,
    ge_s,
    gw1_s,
    gw1b_s,
    gb1_s,
    gw2_s,
    gw2b_s,
    gb2_s,
):
    length = go_ref.shape[0]
    heads, head, inner = w1_ref.shape
    blocks = length // MB
    top, bottom = slice(0, length), slice(length, 2 * length)
    igf[...] = ig_ref[...].astype(F32)
    inclusive, strict = segment_masks(seg_ref[...].astype(F32))
    for h in range(heads):
        g = igf[h : h + 1]
        er = erow_ref[h : h + 1, :]
        go = go_ref[:, h * head : (h + 1) * head]
        n = nq_ref[h]
        x = go * g
        hq2 = low(sq_ref[h] * (x - mean_last(x) - n * mean_last(x * n)))
        hh2_s[h, top] = hq2
        t2_s[h] = dot(p2_ref[h], hq2, 0, 0)
        mix = low(-dot(hq2, low(d2_ref[h]), 1, 1) * (inclusive * er))
        aq = act_ref[h, top]
        gaq = dot(hq2, w2t_ref[h]) + dot(mix, act_ref[h, bottom])
        ga_s[h] = dot(mix, aq, 0, 0)
        hq1 = low(gaq * slopeq_ref[h].astype(F32))
        hh1_s[h, top] = hq1
        t1_s[h] = dot(p1_ref[h], hq1, 0, 0)
    ge_s[...] = jnp.zeros(ge_s.shape, F32)

    def step(i, carry):
        b = blocks - 1 - i
        here = pl.multiple_of(b * MB, MB)
        after = jnp.minimum(here + MB, length - 1)
        fresh = (i == 0) | (seg_smem[0, after] != seg_smem[0, after - 1])

        @pl.when(fresh)
        def _():
            for ref in (gw1_s, gw1b_s, gb1_s, gw2_s, gw2b_s, gb2_s):
                ref[...] = jnp.zeros(ref.shape, ref.dtype)

        ds = pl.ds(here, MB)
        ds_low = pl.ds(length + here, MB)
        rng = range(heads)
        k = [qk_ref[h, ds_low, :] for h in rng]
        act = [act_ref[h, ds_low, :] for h in rng]
        e = [ecol_ref[ds, h : h + 1] for h in rng]
        w2 = [w2s_ref[b, h] for h in rng]
        gw1b = [gw1b_s[h] for h in rng]
        gw2b = [gw2b_s[h] for h in rng]
        gw1 = [gw1_s[h] for h in rng]
        gw2 = [gw2_s[h] for h in rng]
        gb1 = [gb1_s[h] for h in rng]
        gb2 = [gb2_s[h] for h in rng]
        d1 = [d1_ref[h, ds, :].astype(F32) for h in rng]
        d2 = [d2_ref[h, ds, :] for h in rng]
        n = [n_ref[h, ds, :] for h in rng]
        s = [s_ref[h, ds, :] for h in rng]
        fit = [fit_ref[h, ds, :] for h in rng]
        slope = [slope1_ref[h, ds, :].astype(F32) for h in rng]
        curve = [curve1_ref[h, ds, :].astype(F32) for h in rng]
        g = [igf[h : h + 1] for h in rng]
        share = [g[h] * fit[h] for h in rng]
        t1 = [t1_s[h, ds, :] + dot(k[h], gw1b[h]) + gb1[h] for h in rng]
        t2 = [t2_s[h, ds, :] + dot(act[h], gw2b[h], 1, 1) + gb2[h] for h in rng]
        g1 = [-e[h] * t1[h] for h in rng]
        u = [low(g1[h] * slope[h]) for h in rng]
        ed2 = [low(-e[h] * d2[h]) for h in rng]
        ga = [ga_s[h, ds, :] + dot(ed2[h], gw2b[h]) for h in rng]
        g2 = [dot(u[h], w2[h], 1, 1) - e[h] * t2[h] for h in rng]
        y = [s[h] * g2[h] for h in rng]
        my = [mean_last(y[h]) for h in rng]
        myn = [mean_last(y[h] * n[h]) for h in rng]
        msn = [mean_last(share[h] * n[h]) for h in rng]
        mgd = [mean_last(g2[h] * d2[h]) for h in rng]
        gshare = [y[h] - my[h] - n[h] * myn[h] for h in rng]
        gn = [g[h] * (g[h] * gshare[h]) - y[h] * msn[h] - share[h] * myn[h] for h in rng]
        mn = [mean_last(gn[h]) for h in rng]
        mnn = [mean_last(gn[h] * n[h]) for h in rng]
        h2 = [
            low(s[h] * (gn[h] - mn[h] - n[h] * (mnn[h] + mgd[h]))) for h in rng
        ]
        ga = [ga[h] + dot(h2[h], w2[h]) for h in rng]
        h1f = [ga[h] * slope[h] + g1[h] * curve[h] for h in rng]
        h1 = [low(x) for x in h1f]
        up1 = [dot(k[h], h1[h], 0, 0) for h in rng]
        up2 = [
            dot(low(d2[h]), u[h], 0, 0) + dot(h2[h], act[h], 0, 0) for h in rng
        ]
        for h in rng:
            w1n = gw1[h] + up1[h]
            w2n = gw2[h] + up2[h]
            gw1_s[h] = w1n
            gw1b_s[h] = low(w1n)
            gw2_s[h] = w2n
            gw2b_s[h] = low(w2n)
            gb1_s[h] = gb1[h] + sum_rows(h1f[h])
            gb2_s[h] = gb2[h] + sum_rows(h2[h].astype(F32))
            u_s[h, ds, :] = u[h]
            hh1_s[h, ds_low, :] = h1[h]
            hh2_s[h, ds_low, :] = h2[h]
            share_s[h, ds, :] = gshare[h]
            ge_s[ds, h : h + 1] = -jnp.sum(d1[h] * t1[h], -1, keepdims=True) - jnp.sum(
                d2[h] * t2[h], -1, keepdims=True
            )
        return carry

    lax.fori_loop(0, blocks, step, 0)
    small_ref[...] = jnp.zeros(small_ref.shape, F32)
    core = ids_smem[0]
    pad = small_ref.shape[0] // 2
    for h in range(heads):
        cols = slice(h * head, (h + 1) * head)
        rows = slice(h * head, (h + 1) * head)
        g = igf[h : h + 1]
        er = erow_ref[h : h + 1, :]
        hh1 = hh1_s[h]
        hh2 = hh2_s[h]
        qk = qk_ref[h]
        keys = qk_ref[h, bottom]
        both = dot(hh1, d1_ref[h], 1, 1)
        mixq = low(-both[top] * (inclusive * er))
        mixk = low(-both[bottom] * (strict * er))
        direct = dot(hh1, w1_ref[h], 1, 1)
        share = share_s[h]
        spread = dot(mixq, qk_ref[h, top], 0, 0) + dot(mixk, keys, 0, 0)
        go = go_ref[:, cols]
        triple_ref[0, :, cols] = low(go + direct[top] + dot(mixq, keys))
        triple_ref[1, :, cols] = low(g * share + direct[bottom] + dot(mixk, keys) + spread)
        triple_ref[2, :, cols] = low(-g * share)
        first = low(dot(qk, hh1, 0, 0))
        second = low(dot(hh2, act_ref[h], 0, 0) + dot(low(d2_ref[h]), u_s[h], 0, 0))

        @pl.when(core == 0)
        def _(first=first, second=second, rows=rows):
            kept_ref[rows] = first
            sent_ref[rows] = second

        @pl.when(core != 0)
        def _(first=first, second=second, rows=rows):
            kept_ref[rows] = second
            sent_ref[rows] = first

        small_ref[h : h + 1] = sum_rows(hh1.astype(F32))
        row = slice(pad + h, pad + h + 1)
        small_ref[row, 0:head] = sum_rows(hh2.astype(F32))
        small_ref[row, head : 2 * head] = sum_rows(go * nq_ref[h]) + sum_rows(
            share * (fit_ref[h] + g * n_ref[h])
        )
        small_ref[row, 2 * head : 3 * head] = sum_rows(go) + g * sum_rows(share)
    grad_rates = ge_s[...] * fcol_ref[...]
    gr_ref[...] = low(grad_rates)
    total = jnp.broadcast_to(sum_rows(grad_rates), (grad_rates.shape[1], grad_rates.shape[1]))
    small_ref[pad : pad + heads, 3 * head : 3 * head + 1] = jnp.transpose(total)[0:heads, 0:1]


def put_matrix(to_ref, values, index, count, feats):
    chips = to_ref.shape[0]
    rows = values.shape[0] // (feats * chips)
    chunks = values.shape[1] // 128
    for f in range(feats):
        for l in range(chunks):
            row = ((f * count + index) * chunks + l) * rows
            for j in range(chips):
                at = (f * chips + j) * rows
                to_ref[j, row : row + rows, :] = values[at : at + rows, l * 128 : (l + 1) * 128]


def core_columns(core, values):
    half = values.shape[1] // 2
    return jnp.where(core == 0, values[:, 0:half], values[:, half:])


def gate_weights_kernel(
    feats, ids_smem, mine_ref, other_ref, grads_ref, other_grads_ref, wg_ref, *refs
):
    part_ref = refs[0]
    pieces_s, left_s, right_s = refs[-3:]
    outs = refs[1:-3]
    core, chip = ids_smem[0], ids_smem[1]
    length = mine_ref.shape[1]
    for i in range(2):
        left_s[i, 0:length] = mine_ref[i]
        left_s[i, length : 2 * length] = other_ref[i]
        right_s[i, 0:length] = core_columns(core, grads_ref[i])
        right_s[i, length : 2 * length] = core_columns(core, other_grads_ref[i])
    for i in range(2):
        put_matrix(pieces_s, low(dot(left_s[i], right_s[i], 0, 0)), i, 2, feats)
    for s, out in enumerate(outs):
        out[...] = pieces_s[lax.bitwise_xor(chip, s)]
    part_ref[...] = dot(grads_ref[0], wg_ref[...], 1, 1)


def input_kernel(
    feats,
    triple_ref,
    gr_ref,
    pair_ref,
    wq_ref,
    wk_ref,
    wv_ref,
    wr_ref,
    part_ref,
    tok_ref,
    gain1_ref,
    resid_grad_ref,
    small_ref,
    gain_two_ref,
    grad_ref,
    small_out,
):
    heads = wr_ref.shape[0]
    grad = part_ref[...] + dot(triple_ref[0], wq_ref[...], 1, 1)
    grad = grad + dot(triple_ref[1], wk_ref[...], 1, 1) + dot(triple_ref[2], wv_ref[...], 1, 1)
    gr = gr_ref[...]
    grad = grad + dot(gr[:, 0:heads], wr_ref[...])
    tok = tok_ref[0].astype(F32)
    spread = lax.rsqrt(mean_last(tok * tok) + EPSILON)
    scaled = gain1_ref[...].astype(F32) * grad
    grad_ref[0] = (
        resid_grad_ref[...]
        + spread * scaled
        - tok * (spread * spread * spread * mean_last(scaled * tok))
    )
    rate_rows = dot(gr, pair_ref[0], 0, 0)
    gain_row = sum_rows(grad * tok * spread)
    small_out[...] = jnp.zeros(small_out.shape, BF16)
    share = tok.shape[1] // feats
    for f in range(feats):
        cols = slice(f * share, (f + 1) * share)
        small_out[f * 16 : f * 16 + 16, 0:share] = low(
            jnp.concatenate(
                [rate_rows[0:heads, cols], gain_row[:, cols], gain_two_ref[:, cols]]
                + [jnp.zeros((14 - heads, share), F32)],
                0,
            )
        )
    at = feats * 16
    small_out[at : at + small_ref.shape[0]] = low(small_ref[...])


def late_weights_kernel(
    feats,
    ids_smem,
    mine_ref,
    other_ref,
    triple_ref,
    other_triple_ref,
    kept_ref,
    got_ref,
    small_ref,
    *refs,
):
    pieces_s, left_s, right_s = refs[-3:]
    outs = refs[:-3]
    core, chip = ids_smem[0], ids_smem[1]
    length = mine_ref.shape[1]
    chips = pieces_s.shape[0]
    left_s[0:length] = mine_ref[0]
    left_s[length : 2 * length] = other_ref[0]
    for i in range(3):
        right_s[i, 0:length] = core_columns(core, triple_ref[i])
        right_s[i, length : 2 * length] = core_columns(core, other_triple_ref[i])
    for i in range(3):
        put_matrix(pieces_s, low(dot(left_s[...], right_s[i], 0, 0)), i, 3, feats)
    inner = low(kept_ref[...].astype(F32) + got_ref[...].astype(F32))
    rows = inner.shape[0] // chips
    extra = small_ref.shape[0] // chips
    start = pieces_s.shape[1] - 2 * (rows + extra)
    for j in range(chips):
        at = start
        for l in range(2):
            cols = slice(l * 128, (l + 1) * 128)
            pieces_s[j, at : at + rows] = inner[j * rows : (j + 1) * rows, cols]
            at += rows
            pieces_s[j, at : at + extra] = small_ref[j * extra : (j + 1) * extra, cols]
            at += extra
    for s, out in enumerate(outs):
        out[...] = pieces_s[lax.bitwise_xor(chip, s)]


def cut_feat_kernel(parts, ids_smem, *refs):
    outs = refs[parts:]
    feat = ids_smem[2]
    total_rows = refs[0].shape[0]
    each = outs[0].shape[0]
    common = (len(outs) * each - total_rows) // (len(outs) - 1)
    own = each - common

    def total(at):
        value = refs[0][at].astype(F32)
        for ref in refs[1:parts]:
            value = value + ref[at].astype(F32)
        return low(value)

    for s, out in enumerate(outs):
        at = pl.ds(pl.multiple_of(lax.bitwise_xor(feat, s) * own, 16), own)
        out[0:own] = total((at, slice(None)))
    if common:
        shared = total((slice(own * len(outs), total_rows), slice(None)))
        for out in outs:
            out[own:each] = shared


def take_matrices(ids_smem, pieces, outs):
    core, chip = ids_smem[0], ids_smem[1]
    count = len(outs)
    chunks = outs[0].shape[1] // 256
    rows = outs[0].shape[0] // len(pieces)
    for s, both in enumerate(pieces):
        at = pl.ds(pl.multiple_of(lax.bitwise_xor(chip, s) * rows, 16), rows)
        for i, out in enumerate(outs):
            for l in range(chunks):
                row = (i * chunks + l) * rows
                mine = both[0][row : row + rows, :].astype(F32)
                other = both[1][row : row + rows, :].astype(F32)

                @pl.when(core == 0)
                def _(out=out, at=at, l=l, mine=mine, other=other):
                    out[at, l * 128 : (l + 1) * 128] = mine
                    out[at, (chunks + l) * 128 : (chunks + l + 1) * 128] = other

                @pl.when(core != 0)
                def _(out=out, at=at, l=l, mine=mine, other=other):
                    out[at, l * 128 : (l + 1) * 128] = other
                    out[at, (chunks + l) * 128 : (chunks + l + 1) * 128] = mine


def early_totals_kernel(chips, ids_smem, *refs):
    ffn = [(refs[s], refs[chips + s]) for s in range(chips)]
    pair = [(refs[2 * chips + s], refs[3 * chips + s]) for s in range(chips)]
    gate_ref, up_ref, down_ref, wg_ref, wo_ref, down_s = refs[4 * chips :]
    core, chip = ids_smem[0], ids_smem[1]
    half = ffn[0][0].shape[2]
    rows = ffn[0][0].shape[1]
    for s, both in enumerate(ffn):
        at = pl.ds(pl.multiple_of(lax.bitwise_xor(chip, s) * rows, 16), rows)
        for i, out in enumerate((gate_ref, up_ref, down_s)):
            mine = both[0][i].astype(F32)
            other = both[1][i].astype(F32)

            @pl.when(core == 0)
            def _(out=out, at=at, mine=mine, other=other):
                out[at, 0:half] = mine
                out[at, half : 2 * half] = other

            @pl.when(core != 0)
            def _(out=out, at=at, mine=mine, other=other):
                out[at, 0:half] = other
                out[at, half : 2 * half] = mine

    down_ref[...] = jnp.transpose(down_s[...])
    take_matrices(ids_smem, pair, (wg_ref, wo_ref))


def late_totals_kernel(chips, feats, heads, head, ids_smem, *refs):
    pieces = [(refs[s], refs[chips + s]) for s in range(chips)]
    (wq_ref, wk_ref, wv_ref, first_ref, second_ref) = refs[2 * chips : 2 * chips + 5]
    (rate_ref, norm1_ref, norm2_ref, b1_ref, b2_ref, ig_ref, ib_ref, br_ref) = refs[
        2 * chips + 5 : 2 * chips + 13
    ]
    small_s = refs[2 * chips + 13]
    core, chip, feat = ids_smem[0], ids_smem[1], ids_smem[2]
    take_matrices(ids_smem, pieces, (wq_ref, wk_ref, wv_ref))
    rows = first_ref.shape[0] // chips
    extra = small_s.shape[0] // chips
    start = refs[0].shape[0] - 2 * (rows + extra)
    for s, both in enumerate(pieces):
        place = lax.bitwise_xor(chip, s)
        at = pl.ds(pl.multiple_of(place * rows, 16), rows)
        at_small = pl.ds(pl.multiple_of(place * extra, 16), extra)
        row = start
        for l in range(2):
            cols = slice(l * 128, (l + 1) * 128)
            mine = both[0][row : row + rows].astype(F32)
            other = both[1][row : row + rows].astype(F32)
            row += rows

            @pl.when(core == 0)
            def _(at=at, cols=cols, mine=mine, other=other):
                first_ref[at, cols] = mine
                second_ref[at, cols] = other

            @pl.when(core != 0)
            def _(at=at, cols=cols, mine=mine, other=other):
                first_ref[at, cols] = other
                second_ref[at, cols] = mine

            small_s[at_small, cols] = both[0][row : row + extra].astype(F32) + both[1][
                row : row + extra
            ].astype(F32)
            row += extra
    share = rate_ref.shape[1]
    block = small_s[pl.ds(pl.multiple_of(feat * 16, 16), 16), :]
    rate_ref[...] = block[0:heads, 0:share]
    norm1_ref[...] = block[heads : heads + 1, 0:share]
    norm2_ref[...] = block[heads + 1 : heads + 2, 0:share]
    at = feats * 16
    b1_ref[...] = small_s[at : at + heads, :]
    packed = small_s[at + 16 : at + 16 + heads, :]
    b2_ref[...] = packed[:, 0:head]
    ig_ref[...] = packed[:, head : 2 * head]
    ib_ref[...] = packed[:, 2 * head : 3 * head]
    br_ref[...] = packed[:, 3 * head : 3 * head + 1]


def call(kernel, outs, inputs, scratch=(), smem=0, us=1.0):
    specs = [pl.BlockSpec(memory_space=pltpu.SMEM)] * smem
    specs += [pl.BlockSpec(memory_space=pltpu.VMEM)] * (len(inputs) - smem)
    return pl.pallas_call(
        kernel,
        out_shape=[jax.ShapeDtypeStruct(s, d) for s, d in outs],
        in_specs=specs,
        out_specs=[pl.BlockSpec(memory_space=pltpu.VMEM)] * len(outs),
        scratch_shapes=[pltpu.VMEM(s, d) for s, d in scratch],
        cost_estimate=pl.CostEstimate(
            flops=int(us * 1e9), bytes_accessed=int(us * 1e6), transcendentals=0
        ),
        compiler_params=pltpu.CompilerParams(vmem_limit_bytes=VMEM_BYTES),
    )(*inputs)


def exchange(values, axis, size, distance):
    return lax.ppermute(values, axis, [(i, i ^ distance) for i in range(size)])


def add_low(left, right):
    return low(left.astype(F32) + right.astype(F32))


def halve(values, axis, size, distance, dim):
    side = lax.bitwise_and(lax.axis_index(axis) // distance, 1)
    half = values.shape[dim] // 2
    kept = lax.dynamic_slice_in_dim(values, side * half, half, dim)
    sent = lax.dynamic_slice_in_dim(values, (1 - side) * half, half, dim)
    return add_low(kept, exchange(sent, axis, size, distance))


def double(values, axis, size, distance, dim):
    side = lax.bitwise_and(lax.axis_index(axis) // distance, 1)
    other = exchange(values, axis, size, distance)
    return jnp.where(
        side == 0,
        jnp.concatenate([values, other], dim),
        jnp.concatenate([other, values], dim),
    )


def distances(size):
    found = []
    step = 1
    while step < size:
        found.append(step)
        step *= 2
    return found


def across_chips(values, rows):
    return [values[0]] + [
        exchange(values[s], "rows", rows, 2 * s) for s in range(1, len(values))
    ]


def across_feats(values, feats):
    return [values[0]] + [exchange(values[s], "feat", feats, s) for s in range(1, feats)]


def other_core(values, rows):
    return exchange(values, "rows", rows, 1)


def sum_low(values):
    values = [v.astype(F32) for v in values]
    while len(values) > 1:
        values = [values[i] + values[i + 1] for i in range(0, len(values), 2)]
    return low(values[0])


def scatter_rows(values, size, dim):
    for d in distances(size):
        values = halve(values, "rows", size, d, dim)
    return values


def gather_rows(values, size, dim):
    for d in reversed(distances(size)):
        values = double(values, "rows", size, d, dim)
    return values


def scatter_feat(values, size, dim):
    me = lax.axis_index("feat")
    total = lax.dynamic_index_in_dim(values, me, dim, keepdims=False).astype(F32)
    for s in range(1, size):
        piece = lax.dynamic_index_in_dim(values, lax.bitwise_xor(me, s), dim, keepdims=False)
        total = total + exchange(piece, "feat", size, s).astype(F32)
    return low(total)


def on_device(
    rows,
    feats,
    tokens,
    cotangent,
    seg_ids,
    pad_mask,
    norm1_gain,
    w_query,
    w_key,
    w_value,
    w_gate,
    w_rate,
    b_rate,
    inner_w1,
    inner_b1,
    inner_w2,
    inner_b2,
    inner_gain,
    inner_bias,
    w_out,
    norm2_gain,
    ffn_gate,
    ffn_up,
    ffn_down,
):
    _, length, width = tokens.shape
    heads, head, inner = inner_w1.shape
    hidden = ffn_gate.shape[1]
    blocks = length // MB
    chips = rows // 2
    gain_one = norm1_gain[None]
    gain_two = norm2_gain[None]
    line = (length, width)
    wide = (heads, length, inner)
    slim = (heads, length, head)
    thin = (heads, length, 1)
    square = (heads, length, length)
    state = (heads, head, inner)
    w2t = jnp.transpose(inner_w2, (0, 2, 1))
    w_rate_t = jnp.transpose(w_rate)
    place = lax.axis_index("rows")
    me = lax.axis_index("feat")
    ids = jnp.stack([lax.bitwise_and(place, 1), lax.shift_right_logical(place, 1), me])
    cots = across_feats([cotangent[0]] * feats, feats)
    saved = call(
        forward_kernel,
        [
            ((2,) + line, BF16),
            (line, BF16),
            (line, F32),
            (line, F32),
            (line, F32),
            ((heads, 2 * length, head), BF16),
            ((length, 128), F32),
            ((16, length), F32),
            ((length, 128), F32),
            (wide, BF16),
            (wide, BF16),
            ((heads, 2 * length, inner), BF16),
            (wide, BF16),
            (slim, F32),
            (slim, F32),
            (thin, F32),
            (slim, F32),
            ((blocks,) + state, BF16),
            (square, BF16),
            (square, BF16),
            (wide, BF16),
            (slim, F32),
            (thin, F32),
        ],
        [
            seg_ids,
            seg_ids,
            pad_mask,
            tokens,
            gain_one,
            w_query,
            w_key,
            w_value,
            w_gate,
            w_rate_t,
            b_rate[None],
            inner_w1,
            inner_b1,
            w2t,
            inner_b2,
            inner_gain,
            inner_bias,
            w_out,
            gain_two,
        ],
        [
            (slim, F32),
            (slim, F32),
            (slim, F32),
            (line, F32),
            (state, F32),
            (state, BF16),
            ((heads, 1, inner), F32),
            (state, F32),
            ((heads, 1, head), F32),
            ((heads, inner), F32),
            ((heads, head), F32),
            ((heads, head), F32),
            ((heads, head), F32),
        ],
        smem=1,
        us=25,
    )
    pair, normed_two, resid, gelu_gate, gate_slope = saved[0:5]
    qk, ecol, erow, fcol = saved[5:9]
    rest = saved[9:]
    blocks_in = across_feats([normed_two] * feats, feats)
    acts, ggs, gus, pieces = [], [], [], []
    for s in range(feats):
        act, gg, gu, gx = call(
            ffn_kernel,
            [((length, hidden), BF16)] * 3 + [(line, BF16)],
            [blocks_in[s], cots[s], ffn_gate, ffn_up, ffn_down],
            us=3,
        )
        acts.append(act)
        ggs.append(gg)
        gus.append(gu)
        pieces.append(gx if s == 0 else exchange(gx, "feat", feats, s))
    grad_resid, grad_inner_out, grad_pair, grad_gain_two = call(
        partial(between_kernel, feats),
        [(line, F32), (line, F32), ((2,) + line, BF16), ((1, width), F32)],
        pieces + [resid, cotangent, gain_two, w_out, gelu_gate, gate_slope],
        us=4,
    )
    triple, grad_rates, kept, sent, small = call(
        backward_kernel,
        [
            ((3,) + line, BF16),
            ((length, 128), BF16),
            ((heads * head, inner), BF16),
            ((heads * head, inner), BF16),
            ((32, inner), F32),
        ],
        [ids, seg_ids, seg_ids, grad_inner_out, qk, ecol, erow, fcol, inner_w1, w2t]
        + [inner_gain]
        + list(rest),
        [
            ((heads, head), F32),
            (wide, F32),
            (slim, F32),
            (wide, F32),
            ((heads, 2 * length, inner), BF16),
            ((heads, 2 * length, head), BF16),
            (wide, BF16),
            (slim, F32),
            ((length, 128), F32),
            (state, F32),
            (state, BF16),
            ((heads, 1, inner), F32),
            (state, F32),
            (state, BF16),
            ((heads, 1, head), F32),
        ],
        smem=2,
        us=28,
    )
    step = 16 * chips
    small_rows = -(-(16 * feats + 32) // step) * step

    def finish(part):
        return call(
            partial(input_kernel, feats),
            [((1,) + line, F32), ((small_rows, inner), BF16)],
            [triple, grad_rates, pair, w_query, w_key, w_value, w_rate_t, part]
            + [tokens, gain_one, grad_resid, small, grad_gain_two],
            us=4,
        )

    if (width // feats) % step or hidden % 256 or width % 256:
        out, grads = plain_totals(
            rows, feats, blocks_in, cots, acts, ggs, gus, ffn_down, pair, grad_pair, w_gate
        )
        grad_tokens, small = finish(grads.pop())
        late = plain_late_totals(rows, feats, pair, triple, kept, sent, small, state)
        mixed = low(resid + sum(x.astype(F32) for x in across_feats(out, feats)))
        return arrange(mixed, grad_tokens, grads, late, state)
    ffn = call(
        partial(ffn_weights_kernel, feats),
        [((3, width, hidden // 2), BF16)] * 2 + [(line, BF16)] * feats,
        [ids] + blocks_in + cots + acts + ggs + gus + [ffn_down],
        [((feats * length, width), BF16)] * 2 + [((feats * length, hidden), BF16)] * 3,
        smem=1,
        us=6,
    )
    out = across_feats(ffn[2:], feats)
    mixed = low(resid + sum(x.astype(F32) for x in out))
    ffn_pieces = call(
        cut_rows_kernel,
        [((3, width // chips, hidden // 2), BF16)] * chips,
        [ids, ffn[0], other_core(ffn[1], rows)],
        smem=1,
        us=2,
    )
    ffn_total = sum_low(across_chips(ffn_pieces, rows))
    ffn_all = across_chips([ffn_total] * chips, rows)
    ffn_others = [other_core(x, rows) for x in ffn_all]
    pair_other = other_core(pair, rows)
    half = width // 2
    per = width // (feats * chips) * (half // 128)
    gate = call(
        partial(gate_weights_kernel, feats),
        [(line, F32)] + [((feats * 2 * per, 128), BF16)] * chips,
        [ids, pair, pair_other, grad_pair, other_core(grad_pair, rows), w_gate],
        [
            ((chips, feats * 2 * per, 128), BF16),
            ((2, 2 * length, width), BF16),
            ((2, 2 * length, half), BF16),
        ],
        smem=1,
        us=4,
    )
    gate_cut = call(
        partial(cut_feat_kernel, chips),
        [((2 * per, 128), BF16)] * feats,
        [ids] + across_chips(gate[1:], rows),
        smem=1,
        us=2,
    )
    gate_total = sum_low(across_feats(gate_cut, feats))
    gate_all = across_chips([gate_total] * chips, rows)
    gate_others = [other_core(x, rows) for x in gate_all]
    share = (width // feats, width)
    early = call(
        partial(early_totals_kernel, chips),
        [((width, hidden), F32)] * 2 + [((hidden, width), F32)] + [(share, F32)] * 2,
        [ids] + ffn_all + ffn_others + gate_all + gate_others,
        [((width, hidden), F32)],
        smem=1,
        us=4,
    )
    triple_other = other_core(triple, rows)
    got = other_core(sent, rows)
    grad_tokens, small = finish(gate[0])
    tail = 2 * (heads * head + small_rows) // chips
    late = call(
        partial(late_weights_kernel, feats),
        [((feats * 3 * per + tail, 128), BF16)] * chips,
        [ids, pair, pair_other, triple, triple_other, kept, got, small],
        [
            ((chips, feats * 3 * per + tail, 128), BF16),
            ((2 * length, width), BF16),
            ((3, 2 * length, half), BF16),
        ],
        smem=1,
        us=4,
    )
    late_cut = call(
        partial(cut_feat_kernel, chips),
        [((3 * per + tail, 128), BF16)] * feats,
        [ids] + across_chips(late, rows),
        smem=1,
        us=2,
    )
    late_total = sum_low(across_feats(late_cut, feats))
    late_all = across_chips([late_total] * chips, rows)
    late_others = [other_core(x, rows) for x in late_all]
    late = call(
        partial(late_totals_kernel, chips, feats, heads, head),
        [(share, F32)] * 3
        + [((heads * head, inner), F32)] * 2
        + [((heads, width // feats), F32)]
        + [((1, width // feats), F32)] * 2
        + [((heads, inner), F32)]
        + [((heads, head), F32)] * 3
        + [((heads, 1), F32)],
        [ids] + late_all + late_others,
        [((small_rows, inner), F32)],
        smem=1,
        us=4,
    )
    return arrange(mixed, grad_tokens, early, late, state)


def arrange(mixed, grad_tokens, early, late, state):
    return (
        mixed[None],
        grad_tokens,
        late[6][0],
        late[0],
        late[1],
        late[2],
        early[3],
        jnp.transpose(late[5]),
        late[12][:, 0],
        late[3].reshape(state),
        late[8],
        jnp.transpose(late[4].reshape(state), (0, 2, 1)),
        late[9],
        late[10],
        late[11],
        early[4],
        late[7][0],
        early[0],
        early[1],
        early[2],
    )


def contract(left, right):
    return low(dot(left, right, 0, 0))


def plain_features(values, rows, feats):
    width = values.shape[0]
    values = values.reshape((feats, width // feats, width))
    values = scatter_feat(scatter_rows(values, rows, 1), feats, 0)
    return gather_rows(values, rows, 0).astype(F32)


def plain_totals(
    rows, feats, blocks_in, cots, acts, ggs, gus, ffn_down, pair, grad_pair, w_gate
):
    def joined(parts):
        return jnp.concatenate(parts, 0)

    def over_rows(values):
        return gather_rows(scatter_rows(values, rows, 0), rows, 0).astype(F32)

    x, c, act = joined(blocks_in), joined(cots), joined(acts)
    out = [low(dot(a, ffn_down)) for a in acts]
    grads = [contract(x, joined(ggs)), contract(x, joined(gus)), contract(act, c)]
    grads = [over_rows(g) for g in grads]
    for i in range(2):
        grads.append(plain_features(contract(pair[i], grad_pair[i]), rows, feats))
    grads.append(dot(grad_pair[0], w_gate, 1, 1))
    return out, grads


def plain_late_totals(rows, feats, pair, triple, kept, sent, small, state):
    heads, head, _ = state
    me = lax.axis_index("feat")
    core = lax.bitwise_and(lax.axis_index("rows"), 1)
    late = [plain_features(contract(pair[0], triple[i]), rows, feats) for i in range(3)]
    both = jnp.where(core == 0, jnp.stack([kept, sent]), jnp.stack([sent, kept]))
    both = scatter_rows(both, rows, 1)
    for d in distances(feats):
        both = add_low(both, exchange(both, "feat", feats, d))
    both = gather_rows(both, rows, 1).astype(F32)
    for d in distances(rows):
        small = add_low(small, exchange(small, "rows", rows, d))
    for d in distances(feats):
        small = add_low(small, exchange(small, "feat", feats, d))
    small = small.astype(F32)
    share = pair.shape[2] // feats
    block = lax.dynamic_slice_in_dim(small, me * 16, 16, 0)[:, 0:share]
    at = feats * 16
    packed = small[at + 16 : at + 16 + heads]
    return late + [
        both[0],
        both[1],
        block[0:heads],
        block[heads : heads + 1],
        block[heads + 1 : heads + 2],
        small[at : at + heads],
        packed[:, 0:head],
        packed[:, head : 2 * head],
        packed[:, 2 * head : 3 * head],
        packed[:, 3 * head : 3 * head + 1],
    ]


def solution(mesh):
    batch = ("rows", "feat")
    placed = (
        (P(batch, None, None), P(batch, None, None), P(batch, None), P(batch, None))
        + (P(),) * 15
        + (P(None, "feat"), P(None, "feat"), P("feat", None))
    )
    return jax.shard_map(
        partial(on_device, mesh.shape["rows"], mesh.shape["feat"]),
        mesh=mesh,
        in_specs=placed,
        out_specs=(
            P(batch, None, None),
            P(batch, None, None),
            P("feat"),
            P("feat", None),
            P("feat", None),
            P("feat", None),
            P("feat", None),
            P("feat", None),
            P(),
            P(),
            P(),
            P(),
            P(),
            P(),
            P(),
            P("feat", None),
            P("feat"),
            P(None, "feat"),
            P(None, "feat"),
            P("feat", None),
        ),
        check_vma=False,
    )
```

```python
from functools import partial

import jax
import jax.numpy as jnp
from jax import lax
from jax.experimental import pallas as pl
from jax.experimental.pallas import tpu as pltpu
from jax.sharding import PartitionSpec as P

MB = 16
EPSILON = 1e-06
BASE_RATE = 0.1
F32 = jnp.float32
BF16 = jnp.bfloat16


def dot(left, right, left_dim=1, right_dim=0):
    return lax.dot_general(
        left, right, (((left_dim,), (right_dim,)), ((), ())), preferred_element_type=F32
    )


def low(values):
    return values.astype(BF16)


def gelu_parts(values):
    phi = 0.5 + 0.5 * lax.erf(values * 0.7071067811865476)
    density = jnp.exp(-0.5 * values * values) * 0.3989422804014327
    return (values * phi, phi + values * density, density * (2.0 - values * values))


def mean_last(values):
    return jnp.sum(values, -1, keepdims=True) * (1.0 / values.shape[-1])


def sum_rows(values):
    return jnp.sum(values, 0, keepdims=True)


def column_of(row):
    size = row.shape[1]
    return jnp.transpose(jnp.broadcast_to(row, (size, size)))[:, 0:1]


def segment_masks(seg_row):
    size = seg_row.shape[1]
    rows = lax.broadcasted_iota(jnp.int32, (size, size), 0)
    cols = lax.broadcasted_iota(jnp.int32, (size, size), 1)
    same = column_of(seg_row) == seg_row
    block = MB.bit_length() - 1
    later = lax.shift_right_logical(rows, block) > lax.shift_right_logical(cols, block)
    inclusive = jnp.where(same & (cols <= rows), 1.0, 0.0)
    strict = jnp.where(same & later, 1.0, 0.0)
    return (inclusive, strict)


def forward_kernel(
    seg_smem,
    seg_ref,
    live_ref,
    tok_ref,
    gains_ref,
    wq_hbm,
    wk_hbm,
    wv_hbm,
    wg_hbm,
    wr_ref,
    br_ref,
    w1_ref,
    b1_ref,
    w2t_ref,
    b2_ref,
    ig_ref,
    ib_ref,
    wo_hbm,
    pair_ref,
    normed_two_ref,
    *refs,
):
    saved = (len(refs) - 15) // 2
    outs, kept, scratch = refs[0:saved], refs[saved : 2 * saved], refs[2 * saved :]
    (
        resid_ref,
        gelu_ref,
        slope_ref,
        qk_ref,
        ecol_ref,
        erow_ref,
        fcol_ref,
        slope1_ref,
        curve1_ref,
        act_ref,
        d1_ref,
        d2_ref,
        n_ref,
        s_ref,
        fit_ref,
        w2s_ref,
        p1_ref,
        p2_ref,
        slopeq_ref,
        nq_ref,
        sq_ref,
    ) = kept
    q_s, k_s, v_s, out_s, w1_s, w1b_s, b1_s, w2_s, b2_s, b1f, b2f, igf, ibf, weights_s, sems = scratch
    length, width = tok_ref.shape[1], tok_ref.shape[2]
    copies = [
        pltpu.make_async_copy(w, weights_s.at[i], sems.at[i])
        for i, w in enumerate((wq_hbm, wk_hbm, wv_hbm, wg_hbm, wo_hbm))
    ]
    for copy in copies:
        copy.start()
    saves = [
        pltpu.make_async_copy(kept[i], outs[i], sems.at[len(copies) + i]) for i in range(saved)
    ]

    def save(*indices):
        for i in indices:
            saves[i].start()

    heads, head = w1_ref.shape[0], w1_ref.shape[1]
    blocks = length // MB
    tok = tok_ref[0].astype(F32)
    spread = lax.rsqrt(mean_last(tok * tok) + EPSILON)
    normed = low(tok * spread * gains_ref[0:1].astype(F32))
    pair_ref[0] = normed
    seg_row = seg_ref[...].astype(F32)
    live = column_of(live_ref[...].astype(F32))
    rate_pre = dot(normed, wr_ref[...], 1, 1) + br_ref[...].astype(F32)
    sig = jax.nn.sigmoid(rate_pre)
    rates = (BASE_RATE / head) * sig * live
    ecol_ref[...] = jnp.zeros(ecol_ref.shape, F32)
    ecol_ref[:, 0:heads] = rates
    fcol_ref[...] = jnp.zeros(fcol_ref.shape, F32)
    fcol_ref[:, 0:heads] = rates * (1.0 - sig)
    erow_ref[...] = jnp.transpose(ecol_ref[...])[0 : erow_ref.shape[0]]
    for i, to in enumerate((q_s, k_s, v_s)):
        copies[i].wait()
        whole = dot(normed, weights_s[i])
        for h in range(heads):
            to[h] = whole[:, h * head : (h + 1) * head]
    b1f[...] = b1_ref[...].astype(F32)
    b2f[...] = b2_ref[...].astype(F32)
    igf[...] = ig_ref[...].astype(F32)
    ibf[...] = ib_ref[...].astype(F32)
    for h in range(heads):
        qk_ref[h, 0:length] = low(q_s[h])
        qk_ref[h, length : 2 * length] = low(k_s[h])

    def step(b, carry):
        here = pl.multiple_of(b * MB, MB)
        before = jnp.maximum(here - 1, 0)
        fresh = (b == 0) | (seg_smem[0, here] != seg_smem[0, before])

        @pl.when(fresh)
        def _():
            for h in range(heads):
                first = w1_ref[h]
                second = w2t_ref[h]
                w1_s[h] = first.astype(F32)
                w1b_s[h] = first
                w2_s[h] = second.astype(F32)
                w2s_ref[b, h] = second
                b1_s[h] = b1f[h : h + 1]
                b2_s[h] = b2f[h : h + 1]

        @pl.when(jnp.logical_not(fresh))
        def _():
            for h in range(heads):
                w2s_ref[b, h] = low(w2_s[h])

        ds = pl.ds(here, MB)
        rng = range(heads)
        k = [k_s[h, ds, :] for h in rng]
        v = [v_s[h, ds, :] for h in rng]
        e = [ecol_ref[ds, h : h + 1] for h in rng]
        w1 = [w1b_s[h] for h in rng]
        w2 = [w2s_ref[b, h] for h in rng]
        w1f = [w1_s[h] for h in rng]
        w2f = [w2_s[h] for h in rng]
        b1 = [b1_s[h] for h in rng]
        b2 = [b2_s[h] for h in rng]
        g = [igf[h : h + 1] for h in rng]
        gb = [ibf[h : h + 1] for h in rng]
        parts = [gelu_parts(dot(low(k[h]), w1[h]) + b1[h]) for h in rng]
        act = [low(parts[h][0]) for h in rng]
        z2 = [dot(act[h], w2[h], 1, 1) + b2[h] for h in rng]
        c = [z - mean_last(z) for z in z2]
        s = [lax.rsqrt(mean_last(x * x) + EPSILON) for x in c]
        n = [c[h] * s[h] for h in rng]
        fit = [g[h] * n[h] + gb[h] - (v[h] - k[h]) for h in rng]
        share = [g[h] * fit[h] for h in rng]
        m1 = [mean_last(share[h]) for h in rng]
        m2 = [mean_last(share[h] * n[h]) for h in rng]
        d2 = [s[h] * (share[h] - m1[h] - n[h] * m2[h]) for h in rng]
        back = [dot(low(d2[h]), w2[h]) for h in rng]
        d1 = [back[h] * parts[h][1] for h in rng]
        d1b = [low(d1[h]) for h in rng]
        ed2 = [d2[h] * e[h] for h in rng]
        up1 = [dot(low(k[h] * e[h]), d1b[h], 0, 0) for h in rng]
        up2 = [dot(low(ed2[h]), act[h], 0, 0) for h in rng]
        for h in rng:
            w1n = w1f[h] - up1[h]
            w1_s[h] = w1n
            w1b_s[h] = low(w1n)
            w2_s[h] = w2f[h] - up2[h]
            b1_s[h] = b1[h] - sum_rows(d1[h] * e[h])
            b2_s[h] = b2[h] - sum_rows(ed2[h])
            act_ref[h, pl.ds(length + here, MB), :] = act[h]
            slope1_ref[h, ds, :] = low(parts[h][1])
            curve1_ref[h, ds, :] = low(back[h] * parts[h][2])
            d1_ref[h, ds, :] = d1b[h]
            d2_ref[h, ds, :] = d2[h]
            n_ref[h, ds, :] = n[h]
            s_ref[h, ds, :] = s[h]
            fit_ref[h, ds, :] = fit[h]
        return carry

    save(3, 4, 5, 6)
    lax.fori_loop(0, blocks, step, 0)
    save(7, 8, 10, 11, 12, 13, 14, 15)
    inclusive, _ = segment_masks(seg_row)
    for h in range(heads):
        queries = qk_ref[h, 0:length]
        keys = qk_ref[h, length : 2 * length]
        key_act = act_ref[h, length : 2 * length]
        er = erow_ref[h : h + 1, :]
        p1 = (dot(queries, keys, 1, 1) + 1.0) * inclusive
        p1_ref[h] = low(p1)
        zq1 = dot(queries, w1_ref[h]) + b1f[h : h + 1] - dot(low(p1 * er), d1_ref[h])
        aq, slope, _ = gelu_parts(zq1)
        aqb = low(aq)
        act_ref[h, 0:length] = aqb
        slopeq_ref[h] = low(slope)
        p2 = (dot(aqb, key_act, 1, 1) + 1.0) * inclusive
        p2_ref[h] = low(p2)
        zq2 = dot(aqb, w2t_ref[h], 1, 1) + b2f[h : h + 1] - dot(low(p2 * er), low(d2_ref[h]))
        c = zq2 - mean_last(zq2)
        s = lax.rsqrt(mean_last(c * c) + EPSILON)
        n = c * s
        nq_ref[h] = n
        sq_ref[h] = s
        out_s[:, h * head : (h + 1) * head] = q_s[h] + igf[h : h + 1] * n + ibf[h : h + 1]
    save(9, 16, 17, 18, 19, 20)
    inner_out = out_s[...]
    copies[3].wait()
    gate, slope, _ = gelu_parts(dot(normed, weights_s[3]))
    gelu_ref[...] = gate
    slope_ref[...] = inner_out * slope
    gated = low(inner_out * gate)
    pair_ref[1] = gated
    copies[4].wait()
    resid = tok + dot(gated, weights_s[4])
    resid_ref[...] = resid
    spread_two = lax.rsqrt(mean_last(resid * resid) + EPSILON)
    normed_two_ref[...] = low(resid * spread_two * gains_ref[1:2].astype(F32))
    save(0, 1, 2)
    for copy in saves:
        copy.wait()


def ffn_kernel(x_ref, c_ref, wg_ref, wu_ref, wd_ref, act_ref, gg_ref, gu_ref, gx_ref):
    x = x_ref[...]
    gate = dot(x, wg_ref[...])
    up = dot(x, wu_ref[...])
    grad_act = dot(c_ref[...], wd_ref[...], 1, 1)
    sigma = jax.nn.sigmoid(gate)
    silu = gate * sigma
    act_ref[...] = low(silu * up)
    gg = low(grad_act * up * sigma * (1.0 + gate * (1.0 - sigma)))
    gu = low(grad_act * silu)
    gg_ref[...] = gg
    gu_ref[...] = gu
    gx_ref[...] = low(dot(gg, wg_ref[...], 1, 1) + dot(gu, wu_ref[...], 1, 1))


def ffn_weights_kernel(parts, ids_smem, *refs):
    x_refs, c_refs, act_refs, gg_refs, gu_refs = (
        refs[i * parts : (i + 1) * parts] for i in range(5)
    )
    wd_ref, kept_ref, sent_ref = refs[5 * parts : 5 * parts + 3]
    out_refs = refs[5 * parts + 3 : 6 * parts + 3]
    x_s, c_s, act_s, gg_s, gu_s = refs[6 * parts + 3 :]
    rows = x_refs[0].shape[0]
    for i in range(parts):
        at = slice(i * rows, (i + 1) * rows)
        x_s[at] = x_refs[i][...]
        c_s[at] = c_refs[i][...]
        act_s[at] = act_refs[i][...]
        gg_s[at] = gg_refs[i][...]
        gu_s[at] = gu_refs[i][...]
        out_refs[i][...] = low(dot(act_refs[i][...], wd_ref[...]))
    half = kept_ref.shape[2]
    core = ids_smem[0]
    for i, (left, right) in enumerate(((x_s, gg_s), (x_s, gu_s), (c_s, act_s))):
        whole = low(dot(left[...], right[...], 0, 0))

        @pl.when(core == 0)
        def _(whole=whole, i=i):
            kept_ref[i] = whole[:, 0:half]
            sent_ref[i] = whole[:, half:]

        @pl.when(core != 0)
        def _(whole=whole, i=i):
            kept_ref[i] = whole[:, half:]
            sent_ref[i] = whole[:, 0:half]


def between_kernel(parts, *refs):
    pieces = refs[0:parts]
    resid_ref, cot_ref, gains_ref, wo_ref, gelu_ref, slope_ref = refs[parts : parts + 6]
    resid_grad_ref, go_ref, pair_ref, gain_grad_ref = refs[parts + 6 :]
    grad = pieces[0][...].astype(F32)
    for piece in pieces[1:]:
        grad = grad + piece[...].astype(F32)
    resid = resid_ref[...]
    spread = lax.rsqrt(mean_last(resid * resid) + EPSILON)
    scaled = gains_ref[1:2].astype(F32) * grad
    grad_resid = (
        cot_ref[0].astype(F32)
        + spread * scaled
        - resid * (spread * spread * spread * mean_last(scaled * resid))
    )
    gain_grad_ref[...] = sum_rows(grad * resid * spread)
    resid_grad_ref[...] = grad_resid
    grad_branch = low(grad_resid)
    grad_gated = dot(grad_branch, wo_ref[...], 1, 1)
    go_ref[...] = grad_gated * gelu_ref[...]
    pair_ref[0] = low(grad_gated * slope_ref[...])
    pair_ref[1] = grad_branch


def backward_kernel(
    ids_smem,
    seg_smem,
    seg_ref,
    go_ref,
    qk_ref,
    ecol_ref,
    erow_ref,
    fcol_ref,
    w1_ref,
    w2t_ref,
    ig_ref,
    slope1_ref,
    curve1_ref,
    act_ref,
    d1_ref,
    d2_ref,
    n_ref,
    s_ref,
    fit_ref,
    w2s_ref,
    p1_ref,
    p2_ref,
    slopeq_ref,
    nq_ref,
    sq_ref,
    triple_ref,
    gr_ref,
    kept_ref,
    sent_ref,
    small_ref,
    igf,
    t1_s,
    t2_s,
    ga_s,
    hh1_s,
    hh2_s,
    u_s,
    share_s,
    ge_s,
    gw1_s,
    gw1b_s,
    gb1_s,
    gw2_s,
    gw2b_s,
    gb2_s,
):
    length = go_ref.shape[0]
    heads, head, inner = w1_ref.shape
    blocks = length // MB
    top, bottom = slice(0, length), slice(length, 2 * length)
    igf[...] = ig_ref[...].astype(F32)
    inclusive, strict = segment_masks(seg_ref[...].astype(F32))
    for h in range(heads):
        g = igf[h : h + 1]
        er = erow_ref[h : h + 1, :]
        go = go_ref[:, h * head : (h + 1) * head]
        n = nq_ref[h]
        x = go * g
        hq2 = low(sq_ref[h] * (x - mean_last(x) - n * mean_last(x * n)))
        hh2_s[h, top] = hq2
        t2_s[h] = dot(p2_ref[h], hq2, 0, 0)
        mix = low(-dot(hq2, low(d2_ref[h]), 1, 1) * (inclusive * er))
        aq = act_ref[h, top]
        gaq = dot(hq2, w2t_ref[h]) + dot(mix, act_ref[h, bottom])
        ga_s[h] = dot(mix, aq, 0, 0)
        hq1 = low(gaq * slopeq_ref[h].astype(F32))
        hh1_s[h, top] = hq1
        t1_s[h] = dot(p1_ref[h], hq1, 0, 0)
    ge_s[...] = jnp.zeros(ge_s.shape, F32)

    def step(i, carry):
        b = blocks - 1 - i
        here = pl.multiple_of(b * MB, MB)
        after = jnp.minimum(here + MB, length - 1)
        fresh = (i == 0) | (seg_smem[0, after] != seg_smem[0, after - 1])

        @pl.when(fresh)
        def _():
            for ref in (gw1_s, gw1b_s, gb1_s, gw2_s, gw2b_s, gb2_s):
                ref[...] = jnp.zeros(ref.shape, ref.dtype)

        ds = pl.ds(here, MB)
        ds_low = pl.ds(length + here, MB)
        rng = range(heads)
        k = [qk_ref[h, ds_low, :] for h in rng]
        act = [act_ref[h, ds_low, :] for h in rng]
        e = [ecol_ref[ds, h : h + 1] for h in rng]
        w2 = [w2s_ref[b, h] for h in rng]
        gw1b = [gw1b_s[h] for h in rng]
        gw2b = [gw2b_s[h] for h in rng]
        gw1 = [gw1_s[h] for h in rng]
        gw2 = [gw2_s[h] for h in rng]
        gb1 = [gb1_s[h] for h in rng]
        gb2 = [gb2_s[h] for h in rng]
        d1 = [d1_ref[h, ds, :].astype(F32) for h in rng]
        d2 = [d2_ref[h, ds, :] for h in rng]
        n = [n_ref[h, ds, :] for h in rng]
        s = [s_ref[h, ds, :] for h in rng]
        fit = [fit_ref[h, ds, :] for h in rng]
        slope = [slope1_ref[h, ds, :].astype(F32) for h in rng]
        curve = [curve1_ref[h, ds, :].astype(F32) for h in rng]
        g = [igf[h : h + 1] for h in rng]
        share = [g[h] * fit[h] for h in rng]
        t1 = [t1_s[h, ds, :] + dot(k[h], gw1b[h]) + gb1[h] for h in rng]
        t2 = [t2_s[h, ds, :] + dot(act[h], gw2b[h], 1, 1) + gb2[h] for h in rng]
        g1 = [-e[h] * t1[h] for h in rng]
        u = [low(g1[h] * slope[h]) for h in rng]
        ed2 = [low(-e[h] * d2[h]) for h in rng]
        ga = [ga_s[h, ds, :] + dot(ed2[h], gw2b[h]) for h in rng]
        g2 = [dot(u[h], w2[h], 1, 1) - e[h] * t2[h] for h in rng]
        y = [s[h] * g2[h] for h in rng]
        my = [mean_last(y[h]) for h in rng]
        myn = [mean_last(y[h] * n[h]) for h in rng]
        msn = [mean_last(share[h] * n[h]) for h in rng]
        mgd = [mean_last(g2[h] * d2[h]) for h in rng]
        gshare = [y[h] - my[h] - n[h] * myn[h] for h in rng]
        gn = [g[h] * (g[h] * gshare[h]) - y[h] * msn[h] - share[h] * myn[h] for h in rng]
        mn = [mean_last(gn[h]) for h in rng]
        mnn = [mean_last(gn[h] * n[h]) for h in rng]
        h2 = [
            low(s[h] * (gn[h] - mn[h] - n[h] * (mnn[h] + mgd[h]))) for h in rng
        ]
        ga = [ga[h] + dot(h2[h], w2[h]) for h in rng]
        h1f = [ga[h] * slope[h] + g1[h] * curve[h] for h in rng]
        h1 = [low(x) for x in h1f]
        up1 = [dot(k[h], h1[h], 0, 0) for h in rng]
        up2 = [
            dot(low(d2[h]), u[h], 0, 0) + dot(h2[h], act[h], 0, 0) for h in rng
        ]
        for h in rng:
            w1n = gw1[h] + up1[h]
            w2n = gw2[h] + up2[h]
            gw1_s[h] = w1n
            gw1b_s[h] = low(w1n)
            gw2_s[h] = w2n
            gw2b_s[h] = low(w2n)
            gb1_s[h] = gb1[h] + sum_rows(h1f[h])
            gb2_s[h] = gb2[h] + sum_rows(h2[h].astype(F32))
            u_s[h, ds, :] = u[h]
            hh1_s[h, ds_low, :] = h1[h]
            hh2_s[h, ds_low, :] = h2[h]
            share_s[h, ds, :] = gshare[h]
            ge_s[ds, h : h + 1] = -jnp.sum(d1[h] * t1[h], -1, keepdims=True) - jnp.sum(
                d2[h] * t2[h], -1, keepdims=True
            )
        return carry

    lax.fori_loop(0, blocks, step, 0)
    small_ref[...] = jnp.zeros(small_ref.shape, F32)
    core = ids_smem[0]
    pad = small_ref.shape[0] // 2
    for h in range(heads):
        cols = slice(h * head, (h + 1) * head)
        rows = slice(h * head, (h + 1) * head)
        g = igf[h : h + 1]
        er = erow_ref[h : h + 1, :]
        hh1 = hh1_s[h]
        hh2 = hh2_s[h]
        qk = qk_ref[h]
        keys = qk_ref[h, bottom]
        both = dot(hh1, d1_ref[h], 1, 1)
        mixq = low(-both[top] * (inclusive * er))
        mixk = low(-both[bottom] * (strict * er))
        direct = dot(hh1, w1_ref[h], 1, 1)
        share = share_s[h]
        spread = dot(mixq, qk_ref[h, top], 0, 0) + dot(mixk, keys, 0, 0)
        go = go_ref[:, cols]
        triple_ref[0, :, cols] = low(go + direct[top] + dot(mixq, keys))
        triple_ref[1, :, cols] = low(g * share + direct[bottom] + dot(mixk, keys) + spread)
        triple_ref[2, :, cols] = low(-g * share)
        first = low(dot(qk, hh1, 0, 0))
        second = low(dot(hh2, act_ref[h], 0, 0) + dot(low(d2_ref[h]), u_s[h], 0, 0))

        @pl.when(core == 0)
        def _(first=first, second=second, rows=rows):
            kept_ref[rows] = first
            sent_ref[rows] = second

        @pl.when(core != 0)
        def _(first=first, second=second, rows=rows):
            kept_ref[rows] = second
            sent_ref[rows] = first

        small_ref[h : h + 1] = sum_rows(hh1.astype(F32))
        row = slice(pad + h, pad + h + 1)
        small_ref[row, 0:head] = sum_rows(hh2.astype(F32))
        small_ref[row, head : 2 * head] = sum_rows(go * nq_ref[h]) + sum_rows(
            share * (fit_ref[h] + g * n_ref[h])
        )
        small_ref[row, 2 * head : 3 * head] = sum_rows(go) + g * sum_rows(share)
    grad_rates = ge_s[...] * fcol_ref[...]
    gr_ref[...] = low(grad_rates)
    total = jnp.broadcast_to(sum_rows(grad_rates), (grad_rates.shape[1], grad_rates.shape[1]))
    small_ref[pad : pad + heads, 3 * head : 3 * head + 1] = jnp.transpose(total)[0:heads, 0:1]


def put_matrix(to_ref, values, index, count, feats):
    chips = to_ref.shape[0]
    rows = values.shape[0] // (feats * chips)
    chunks = values.shape[1] // 128
    for f in range(feats):
        for l in range(chunks):
            row = ((f * count + index) * chunks + l) * rows
            for j in range(chips):
                at = (f * chips + j) * rows
                to_ref[j, row : row + rows, :] = values[at : at + rows, l * 128 : (l + 1) * 128]


def core_columns(core, values):
    half = values.shape[1] // 2
    return jnp.where(core == 0, values[:, 0:half], values[:, half:])


def gate_weights_kernel(
    feats,
    chips,
    ids_smem,
    mine_ref,
    other_ref,
    grads_ref,
    other_grads_ref,
    wg_ref,
    kept_ref,
    got_ref,
    part_ref,
    *refs,
):
    outs = refs[0:chips]
    pieces_s, left_s, right_s = refs[chips:]
    core, chip = ids_smem[0], ids_smem[1]
    length = mine_ref.shape[1]
    for i in range(2):
        left_s[i, 0:length] = mine_ref[i]
        left_s[i, length : 2 * length] = other_ref[i]
        right_s[i, 0:length] = core_columns(core, grads_ref[i])
        right_s[i, length : 2 * length] = core_columns(core, other_grads_ref[i])
    for i in range(2):
        put_matrix(pieces_s, low(dot(left_s[i], right_s[i], 0, 0)), i, 2, feats)
    count, _, half = kept_ref.shape
    chunks = half // 128
    before = outs[0].shape[0] - pieces_s.shape[1]
    rows = before // (count * chunks)
    for s, out in enumerate(outs):
        place = lax.bitwise_xor(chip, s)
        at = pl.ds(pl.multiple_of(place * rows, 16), rows)
        for i in range(count):
            both = low(kept_ref[i, at, :].astype(F32) + got_ref[i, at, :].astype(F32))
            for l in range(chunks):
                row = (i * chunks + l) * rows
                out[row : row + rows] = both[:, l * 128 : (l + 1) * 128]
        out[before:] = pieces_s[place]
    part_ref[...] = dot(grads_ref[0], wg_ref[...], 1, 1)


def input_kernel(
    feats,
    triple_ref,
    gr_ref,
    pair_ref,
    wq_ref,
    wk_ref,
    wv_ref,
    wr_ref,
    part_ref,
    tok_ref,
    gains_ref,
    resid_grad_ref,
    small_ref,
    gain_two_ref,
    grad_ref,
    small_out,
):
    heads = wr_ref.shape[0]
    grad = part_ref[...] + dot(triple_ref[0], wq_ref[...], 1, 1)
    grad = grad + dot(triple_ref[1], wk_ref[...], 1, 1) + dot(triple_ref[2], wv_ref[...], 1, 1)
    gr = gr_ref[...]
    grad = grad + dot(gr[:, 0:heads], wr_ref[...])
    tok = tok_ref[0].astype(F32)
    spread = lax.rsqrt(mean_last(tok * tok) + EPSILON)
    scaled = gains_ref[0:1].astype(F32) * grad
    grad_ref[0] = (
        resid_grad_ref[...]
        + spread * scaled
        - tok * (spread * spread * spread * mean_last(scaled * tok))
    )
    rate_rows = dot(gr, pair_ref[0], 0, 0)
    gain_row = sum_rows(grad * tok * spread)
    small_out[...] = jnp.zeros(small_out.shape, BF16)
    share = tok.shape[1] // feats
    for f in range(feats):
        cols = slice(f * share, (f + 1) * share)
        small_out[f * 16 : f * 16 + 16, 0:share] = low(
            jnp.concatenate(
                [rate_rows[0:heads, cols], gain_row[:, cols], gain_two_ref[:, cols]]
                + [jnp.zeros((14 - heads, share), F32)],
                0,
            )
        )
    at = feats * 16
    small_out[at : at + small_ref.shape[0]] = low(small_ref[...])


def tails_kernel(ids_smem, kept_ref, got_ref, small_ref, *refs):
    outs, tails_s = refs[:-1], refs[-1]
    chips = len(outs)
    inner = low(kept_ref[...].astype(F32) + got_ref[...].astype(F32))
    rows = inner.shape[0] // chips
    extra = small_ref.shape[0] // chips
    for j in range(chips):
        at = 0
        for l in range(2):
            cols = slice(l * 128, (l + 1) * 128)
            tails_s[j, at : at + rows] = inner[j * rows : (j + 1) * rows, cols]
            at += rows
            tails_s[j, at : at + extra] = small_ref[j * extra : (j + 1) * extra, cols]
            at += extra
    for s, out in enumerate(outs):
        out[...] = tails_s[lax.bitwise_xor(ids_smem[1], s)]


def late_weights_kernel(
    feats, ids_smem, mine_ref, other_ref, triple_ref, other_triple_ref, *refs
):
    pieces_s, left_s, right_s = refs[-3:]
    outs = refs[:-3]
    core, chip = ids_smem[0], ids_smem[1]
    length = mine_ref.shape[1]
    left_s[0:length] = mine_ref[0]
    left_s[length : 2 * length] = other_ref[0]
    for i in range(3):
        right_s[i, 0:length] = core_columns(core, triple_ref[i])
        right_s[i, length : 2 * length] = core_columns(core, other_triple_ref[i])
    for i in range(3):
        put_matrix(pieces_s, low(dot(left_s[...], right_s[i], 0, 0)), i, 3, feats)
    for s, out in enumerate(outs):
        out[...] = pieces_s[lax.bitwise_xor(chip, s)]


def sum_at(refs, at):
    value = refs[0][at].astype(F32)
    for ref in refs[1:]:
        value = value + ref[at].astype(F32)
    return low(value)


def cut_feat_kernel(chips, ids_smem, *refs):
    parts, outs = refs[0:chips], refs[chips:]
    rows = outs[0].shape[0]
    for s, out in enumerate(outs):
        at = pl.ds(pl.multiple_of(lax.bitwise_xor(ids_smem[2], s) * rows, 16), rows)
        out[...] = sum_at(parts, (at, slice(None)))


def middle_kernel(chips, ids_smem, *refs):
    pair, tail = refs[0:chips], refs[chips : 2 * chips]
    total_ref, outs = refs[2 * chips], refs[2 * chips + 1 :]
    before = total_ref.shape[0]
    rows = (pair[0].shape[0] - before) // len(outs)
    shared = sum_at(tail, (slice(None), slice(None)))
    for s, out in enumerate(outs):
        at = pl.multiple_of(before + lax.bitwise_xor(ids_smem[2], s) * rows, 16)
        out[0:rows] = sum_at(pair, (pl.ds(at, rows), slice(None)))
        out[rows:] = shared
    total_ref[...] = sum_at(pair, (slice(0, before), slice(None)))


def take_matrices(ids_smem, pieces, outs, start=0):
    core, chip = ids_smem[0], ids_smem[1]
    chunks = outs[0].shape[1] // 256
    rows = outs[0].shape[0] // len(pieces)
    for s, both in enumerate(pieces):
        at = pl.ds(pl.multiple_of(lax.bitwise_xor(chip, s) * rows, 16), rows)
        for i, out in enumerate(outs):
            for l in range(chunks):
                row = start + (i * chunks + l) * rows
                mine = both[0][row : row + rows, :].astype(F32)
                other = both[1][row : row + rows, :].astype(F32)

                @pl.when(core == 0)
                def _(out=out, at=at, l=l, mine=mine, other=other):
                    out[at, l * 128 : (l + 1) * 128] = mine
                    out[at, (chunks + l) * 128 : (chunks + l + 1) * 128] = other

                @pl.when(core != 0)
                def _(out=out, at=at, l=l, mine=mine, other=other):
                    out[at, l * 128 : (l + 1) * 128] = other
                    out[at, (chunks + l) * 128 : (chunks + l + 1) * 128] = mine


def ffn_totals_kernel(chips, ids_smem, *refs):
    pieces = [(refs[s], refs[chips + s]) for s in range(chips)]
    gate_ref, up_ref, down_ref, down_s = refs[2 * chips :]
    take_matrices(ids_smem, pieces, (gate_ref, up_ref, down_s))
    down_ref[...] = jnp.transpose(down_s[...])


def early_totals_kernel(chips, feats, heads, head, ids_smem, *refs):
    pieces = [(refs[s], refs[chips + s]) for s in range(chips)]
    wg_ref, wo_ref, first_ref, second_ref = refs[2 * chips : 2 * chips + 4]
    (rate_ref, norm1_ref, norm2_ref, b1_ref, b2_ref, ig_ref, ib_ref, br_ref, small_s) = refs[
        2 * chips + 4 :
    ]
    core, chip, feat = ids_smem[0], ids_smem[1], ids_smem[2]
    take_matrices(ids_smem, pieces, (wg_ref, wo_ref))
    rows = first_ref.shape[0] // chips
    extra = small_s.shape[0] // chips
    start = 2 * (wg_ref.shape[0] // chips) * (wg_ref.shape[1] // 256)
    for s, both in enumerate(pieces):
        place = lax.bitwise_xor(chip, s)
        at = pl.ds(pl.multiple_of(place * rows, 16), rows)
        at_small = pl.ds(pl.multiple_of(place * extra, 16), extra)
        row = start
        for l in range(2):
            cols = slice(l * 128, (l + 1) * 128)
            mine = both[0][row : row + rows].astype(F32)
            other = both[1][row : row + rows].astype(F32)
            row += rows

            @pl.when(core == 0)
            def _(at=at, cols=cols, mine=mine, other=other):
                first_ref[at, cols] = mine
                second_ref[at, cols] = other

            @pl.when(core != 0)
            def _(at=at, cols=cols, mine=mine, other=other):
                first_ref[at, cols] = other
                second_ref[at, cols] = mine

            small_s[at_small, cols] = both[0][row : row + extra].astype(F32) + both[1][
                row : row + extra
            ].astype(F32)
            row += extra
    share = rate_ref.shape[1]
    block = small_s[pl.ds(pl.multiple_of(feat * 16, 16), 16), :]
    rate_ref[...] = block[0:heads, 0:share]
    norm1_ref[...] = block[heads : heads + 1, 0:share]
    norm2_ref[...] = block[heads + 1 : heads + 2, 0:share]
    at = feats * 16
    b1_ref[...] = small_s[at : at + heads, :]
    packed = small_s[at + 16 : at + 16 + heads, :]
    b2_ref[...] = packed[:, 0:head]
    ig_ref[...] = packed[:, head : 2 * head]
    ib_ref[...] = packed[:, 2 * head : 3 * head]
    br_ref[...] = packed[:, 3 * head : 3 * head + 1]


def late_totals_kernel(chips, ids_smem, *refs):
    pieces = [(refs[s], refs[chips + s]) for s in range(chips)]
    take_matrices(ids_smem, pieces, refs[2 * chips : 2 * chips + 3])


def held(values):
    return pltpu.with_memory_space_constraint(values, pltpu.VMEM)


def call(kernel, outs, inputs, scratch=(), smem=0, us=1.0, plain=(), loose=(), keep=True, mib=24):
    specs, placed = [], []
    for i, x in enumerate(inputs):
        if i < smem:
            specs.append(pl.BlockSpec(memory_space=pltpu.SMEM))
            placed.append(x)
        elif i in loose:
            specs.append(pl.BlockSpec(memory_space=pltpu.HBM))
            placed.append(pltpu.with_memory_space_constraint(x, pltpu.HBM))
        elif i in plain:
            specs.append(pl.BlockSpec(memory_space=pltpu.VMEM))
            placed.append(pltpu.with_memory_space_constraint(x, pltpu.HBM))
        else:
            specs.append(pl.BlockSpec(memory_space=pltpu.VMEM))
            placed.append(held(x))
    kept = [keep] * len(outs) if isinstance(keep, bool) else list(keep)
    return pl.pallas_call(
        kernel,
        out_shape=[
            pltpu.VMEM(s, d) if k else pltpu.HBM(s, d) for (s, d), k in zip(outs, kept)
        ],
        in_specs=specs,
        out_specs=[
            pl.BlockSpec(memory_space=pltpu.HBM if k is None else pltpu.VMEM) for k in kept
        ],
        scratch_shapes=[pltpu.VMEM(*x) if isinstance(x, tuple) else x for x in scratch],
        cost_estimate=pl.CostEstimate(
            flops=int(us * 1e10), bytes_accessed=int(us * 3e7), transcendentals=0
        ),
        compiler_params=pltpu.CompilerParams(vmem_limit_bytes=mib * 2**20),
    )(*placed)


def exchange(values, axis, size, distance):
    return lax.ppermute(values, axis, [(i, i ^ distance) for i in range(size)])


def add_low(left, right):
    return low(left.astype(F32) + right.astype(F32))


def halve(values, axis, size, distance, dim):
    side = lax.bitwise_and(lax.axis_index(axis) // distance, 1)
    half = values.shape[dim] // 2
    kept = lax.dynamic_slice_in_dim(values, side * half, half, dim)
    sent = lax.dynamic_slice_in_dim(values, (1 - side) * half, half, dim)
    return add_low(kept, exchange(sent, axis, size, distance))


def double(values, axis, size, distance, dim):
    side = lax.bitwise_and(lax.axis_index(axis) // distance, 1)
    other = exchange(values, axis, size, distance)
    return jnp.where(
        side == 0,
        jnp.concatenate([values, other], dim),
        jnp.concatenate([other, values], dim),
    )


def distances(size):
    found = []
    step = 1
    while step < size:
        found.append(step)
        step *= 2
    return found


def across_chips(values, rows):
    return [values[0]] + [
        exchange(values[s], "rows", rows, 2 * s) for s in range(1, len(values))
    ]


def across_feats(values, feats):
    return [values[0]] + [exchange(values[s], "feat", feats, s) for s in range(1, feats)]


def other_core(values, rows):
    return exchange(values, "rows", rows, 1)


def sum_low(values):
    values = [v.astype(F32) for v in values]
    while len(values) > 1:
        values = [values[i] + values[i + 1] for i in range(0, len(values), 2)]
    return low(values[0])


def scatter_rows(values, size, dim):
    for d in distances(size):
        values = halve(values, "rows", size, d, dim)
    return values


def gather_rows(values, size, dim):
    for d in reversed(distances(size)):
        values = double(values, "rows", size, d, dim)
    return values


def scatter_feat(values, size, dim):
    me = lax.axis_index("feat")
    total = lax.dynamic_index_in_dim(values, me, dim, keepdims=False).astype(F32)
    for s in range(1, size):
        piece = lax.dynamic_index_in_dim(values, lax.bitwise_xor(me, s), dim, keepdims=False)
        total = total + exchange(piece, "feat", size, s).astype(F32)
    return low(total)


def on_device(
    rows,
    feats,
    tokens,
    cotangent,
    seg_ids,
    pad_mask,
    norm1_gain,
    w_query,
    w_key,
    w_value,
    w_gate,
    w_rate,
    b_rate,
    inner_w1,
    inner_b1,
    inner_w2,
    inner_b2,
    inner_gain,
    inner_bias,
    w_out,
    norm2_gain,
    ffn_gate,
    ffn_up,
    ffn_down,
):
    _, length, width = tokens.shape
    heads, head, inner = inner_w1.shape
    hidden = ffn_gate.shape[1]
    blocks = length // MB
    chips = rows // 2
    gains = jnp.stack([norm1_gain, norm2_gain])
    line = (length, width)
    wide = (heads, length, inner)
    slim = (heads, length, head)
    thin = (heads, length, 1)
    square = (heads, length, length)
    state = (heads, head, inner)
    w2t = jnp.transpose(inner_w2, (0, 2, 1))
    w_rate_t = jnp.transpose(w_rate)
    place = lax.axis_index("rows")
    me = lax.axis_index("feat")
    ids = jnp.stack([lax.bitwise_and(place, 1), lax.shift_right_logical(place, 1), me])
    cots = across_feats([cotangent[0]] * feats, feats)
    kept = [
        (line, F32),
        (line, F32),
        (line, F32),
        ((heads, 2 * length, head), BF16),
        ((length, 128), F32),
        ((16, length), F32),
        ((length, 128), F32),
        (wide, BF16),
        (wide, BF16),
        ((heads, 2 * length, inner), BF16),
        (wide, BF16),
        (slim, F32),
        (slim, F32),
        (thin, F32),
        (slim, F32),
        ((blocks,) + state, BF16),
        (square, BF16),
        (square, BF16),
        (wide, BF16),
        (slim, F32),
        (thin, F32),
    ]
    saved = call(
        forward_kernel,
        [((2,) + line, BF16), (line, BF16)] + kept,
        [
            seg_ids,
            seg_ids,
            pad_mask,
            tokens,
            gains,
            w_query,
            w_key,
            w_value,
            w_gate,
            w_rate_t,
            b_rate[None],
            inner_w1,
            inner_b1,
            w2t,
            inner_b2,
            inner_gain,
            inner_bias,
            w_out,
        ],
        kept
        + [
            (slim, F32),
            (slim, F32),
            (slim, F32),
            (line, F32),
            (state, F32),
            (state, BF16),
            ((heads, 1, inner), F32),
            (state, F32),
            ((heads, 1, head), F32),
            ((heads, inner), F32),
            ((heads, head), F32),
            ((heads, head), F32),
            ((heads, head), F32),
            ((5, width, width), BF16),
            pltpu.SemaphoreType.DMA((5 + len(kept),)),
        ],
        smem=1,
        us=20,
        plain=range(18),
        loose=(5, 6, 7, 8, 17),
        keep=[True, True] + [None] * len(kept),
        mib=48,
    )
    pair, normed_two, resid, gelu_gate, gate_slope = saved[0:5]
    qk, ecol, erow, fcol = saved[5:9]
    rest = saved[9:]
    normed_two, *cots = lax.optimization_barrier([normed_two] + cots)
    blocks_in = [normed_two]
    for s in range(1, feats):
        nearest = s & -s
        blocks_in.append(exchange(blocks_in[s ^ nearest], "feat", feats, nearest))
    acts, ggs, gus, pieces = [], [], [], []
    for s in range(feats):
        act, gg, gu, gx = call(
            ffn_kernel,
            [((length, hidden), BF16)] * 3 + [(line, BF16)],
            [blocks_in[s], cots[s], ffn_gate, ffn_up, ffn_down],
            us=1.5,
        )
        acts.append(act)
        ggs.append(gg)
        gus.append(gu)
        pieces.append(gx if s == 0 else exchange(gx, "feat", feats, s))
    def between(pieces):
        return call(
            partial(between_kernel, feats),
            [(line, F32), (line, F32), ((2,) + line, BF16), ((1, width), F32)],
            pieces + [resid, cotangent, gains, w_out, gelu_gate, gate_slope],
            us=1,
        )

    def inner_backward(grad_inner_out):
        return call(
            backward_kernel,
            [
                ((3,) + line, BF16),
                ((length, 128), BF16),
                ((heads * head, inner), BF16),
                ((heads * head, inner), BF16),
                ((32, inner), F32),
            ],
            [ids, seg_ids, seg_ids, grad_inner_out, qk, ecol, erow, fcol, inner_w1, w2t]
            + [inner_gain]
            + list(rest),
            [
                ((heads, head), F32),
                (wide, F32),
                (slim, F32),
                (wide, F32),
                ((heads, 2 * length, inner), BF16),
                ((heads, 2 * length, head), BF16),
                (wide, BF16),
                (slim, F32),
                ((length, 128), F32),
                (state, F32),
                (state, BF16),
                ((heads, 1, inner), F32),
                (state, F32),
                (state, BF16),
                ((heads, 1, head), F32),
            ],
            smem=2,
            us=22,
        )

    step = 16 * chips
    small_rows = -(-(16 * feats + 32) // step) * step

    def finish(triple, grad_rates, small, part, grad_resid, grad_gain_two):
        return call(
            partial(input_kernel, feats),
            [((1,) + line, F32), ((small_rows, inner), BF16)],
            [triple, grad_rates, pair, w_query, w_key, w_value, w_rate_t, part]
            + [tokens, gains, grad_resid, small, grad_gain_two],
            us=2,
            keep=(False, True),
        )

    if (width // feats) % step or hidden % 256 or width % 256:
        grad_resid, grad_inner_out, grad_pair, grad_gain_two = between(pieces)
        out, grads = plain_totals(
            rows, feats, blocks_in, cots, acts, ggs, gus, ffn_down, pair, grad_pair, w_gate
        )
        triple, grad_rates, kept, sent, small = inner_backward(grad_inner_out)
        grad_tokens, small = finish(triple, grad_rates, small, grads.pop(), grad_resid, grad_gain_two)
        late = plain_late_totals(rows, feats, pair, triple, kept, sent, small, state)
        mixed = low(resid + sum(x.astype(F32) for x in across_feats(out, feats)))
        return arrange(mixed, grad_tokens, grads, late, state)
    ffn = call(
        partial(ffn_weights_kernel, feats),
        [((3, width, hidden // 2), BF16)] * 2 + [(line, BF16)] * feats,
        [ids] + blocks_in + cots + acts + ggs + gus + [ffn_down],
        [((feats * length, width), BF16)] * 2 + [((feats * length, hidden), BF16)] * 3,
        smem=1,
        us=4,
    )
    pieces, ffn_kept = lax.optimization_barrier((pieces, ffn[0]))
    grad_resid, grad_inner_out, grad_pair, grad_gain_two = between(pieces)
    pair_other = other_core(pair, rows)
    half = width // 2
    per = width // (feats * chips) * (half // 128)
    ffn_rows = 3 * (width // chips) * (hidden // 256)
    part, *early = call(
        partial(gate_weights_kernel, feats, chips),
        [(line, F32)] + [((ffn_rows + feats * 2 * per, 128), BF16)] * chips,
        [ids, pair, pair_other, grad_pair, other_core(grad_pair, rows), w_gate]
        + [ffn_kept, other_core(ffn[1], rows)],
        [
            ((chips, feats * 2 * per, 128), BF16),
            ((2, 2 * length, width), BF16),
            ((2, 2 * length, half), BF16),
        ],
        smem=1,
        us=2,
    )
    grad_inner_out, early, out = lax.optimization_barrier((grad_inner_out, early, ffn[2:]))
    early = across_chips(early, rows)
    out = across_feats(out, feats)
    triple, grad_rates, kept, sent, small = inner_backward(grad_inner_out)
    triple_other = other_core(triple, rows)
    got = other_core(sent, rows)
    small, early, out = lax.optimization_barrier((small, early, out))
    grad_tokens, small = finish(
        triple, grad_rates, small, part, grad_resid, grad_gain_two
    )
    mixed = low(resid + sum(x.astype(F32) for x in out))
    tail = 2 * (heads * head + small_rows) // chips
    tails = call(
        tails_kernel,
        [((tail, 128), BF16)] * chips,
        [ids, kept, got, small],
        [((chips, tail, 128), BF16)],
        smem=1,
        us=1,
    )
    tails, triple = lax.optimization_barrier((tails, triple))
    tails = across_chips(tails, rows)
    late = call(
        partial(late_weights_kernel, feats),
        [((feats * 3 * per, 128), BF16)] * chips,
        [ids, pair, pair_other, triple, triple_other],
        [
            ((chips, feats * 3 * per, 128), BF16),
            ((2 * length, width), BF16),
            ((3, 2 * length, half), BF16),
        ],
        smem=1,
        us=2,
    )
    late = across_chips(late, rows)
    ffn_total, *cut = call(
        partial(middle_kernel, chips),
        [((ffn_rows, 128), BF16)] + [((2 * per + tail, 128), BF16)] * feats,
        [ids] + early + tails,
        smem=1,
        us=1,
    )
    ffn_total = across_chips([ffn_total] * chips, rows)
    ffn_total += [other_core(x, rows) for x in ffn_total]
    joined = sum_low(across_feats(cut, feats))
    joined = across_chips([joined] * chips, rows)
    joined += [other_core(x, rows) for x in joined]
    late_cut = call(
        partial(cut_feat_kernel, chips),
        [((3 * per, 128), BF16)] * feats,
        [ids] + late,
        smem=1,
        us=1,
    )
    late_total = sum_low(across_feats(late_cut, feats))
    late = across_chips([late_total] * chips, rows)
    late += [other_core(x, rows) for x in late]
    share = (width // feats, width)
    ffn = call(
        partial(ffn_totals_kernel, chips),
        [((width, hidden), F32)] * 2 + [((hidden, width), F32)],
        [ids] + ffn_total,
        [((width, hidden), F32)],
        smem=1,
        us=3,
        keep=False,
    )
    early = call(
        partial(early_totals_kernel, chips, feats, heads, head),
        [(share, F32)] * 2
        + [((heads * head, inner), F32)] * 2
        + [((heads, width // feats), F32)]
        + [((1, width // feats), F32)] * 2
        + [((heads, inner), F32)]
        + [((heads, head), F32)] * 3
        + [((heads, 1), F32)],
        [ids] + joined,
        [((small_rows, inner), F32)],
        smem=1,
        us=3,
        keep=False,
    )
    late = call(
        partial(late_totals_kernel, chips),
        [(share, F32)] * 3,
        [ids] + late,
        smem=1,
        us=2,
        keep=False,
    )
    return arrange(
        mixed, grad_tokens, list(ffn) + list(early[0:2]), list(late) + list(early[2:]), state
    )


def arrange(mixed, grad_tokens, early, late, state):
    return (
        mixed[None],
        grad_tokens,
        late[6][0],
        late[0],
        late[1],
        late[2],
        early[3],
        jnp.transpose(late[5]),
        late[12][:, 0],
        late[3].reshape(state),
        late[8],
        jnp.transpose(late[4].reshape(state), (0, 2, 1)),
        late[9],
        late[10],
        late[11],
        early[4],
        late[7][0],
        early[0],
        early[1],
        early[2],
    )


def contract(left, right):
    return low(dot(left, right, 0, 0))


def plain_features(values, rows, feats):
    width = values.shape[0]
    values = values.reshape((feats, width // feats, width))
    values = scatter_feat(scatter_rows(values, rows, 1), feats, 0)
    return gather_rows(values, rows, 0).astype(F32)


def plain_totals(
    rows, feats, blocks_in, cots, acts, ggs, gus, ffn_down, pair, grad_pair, w_gate
):
    def joined(parts):
        return jnp.concatenate(parts, 0)

    def over_rows(values):
        return gather_rows(scatter_rows(values, rows, 0), rows, 0).astype(F32)

    x, c, act = joined(blocks_in), joined(cots), joined(acts)
    out = [low(dot(a, ffn_down)) for a in acts]
    grads = [contract(x, joined(ggs)), contract(x, joined(gus)), contract(act, c)]
    grads = [over_rows(g) for g in grads]
    for i in range(2):
        grads.append(plain_features(contract(pair[i], grad_pair[i]), rows, feats))
    grads.append(dot(grad_pair[0], w_gate, 1, 1))
    return out, grads


def plain_late_totals(rows, feats, pair, triple, kept, sent, small, state):
    heads, head, _ = state
    me = lax.axis_index("feat")
    core = lax.bitwise_and(lax.axis_index("rows"), 1)
    late = [plain_features(contract(pair[0], triple[i]), rows, feats) for i in range(3)]
    both = jnp.where(core == 0, jnp.stack([kept, sent]), jnp.stack([sent, kept]))
    both = scatter_rows(both, rows, 1)
    for d in distances(feats):
        both = add_low(both, exchange(both, "feat", feats, d))
    both = gather_rows(both, rows, 1).astype(F32)
    for d in distances(rows):
        small = add_low(small, exchange(small, "rows", rows, d))
    for d in distances(feats):
        small = add_low(small, exchange(small, "feat", feats, d))
    small = small.astype(F32)
    share = pair.shape[2] // feats
    block = lax.dynamic_slice_in_dim(small, me * 16, 16, 0)[:, 0:share]
    at = feats * 16
    packed = small[at + 16 : at + 16 + heads]
    return late + [
        both[0],
        both[1],
        block[0:heads],
        block[heads : heads + 1],
        block[heads + 1 : heads + 2],
        small[at : at + heads],
        packed[:, 0:head],
        packed[:, head : 2 * head],
        packed[:, 2 * head : 3 * head],
        packed[:, 3 * head : 3 * head + 1],
    ]


def solution(mesh):
    batch = ("rows", "feat")
    placed = (
        (P(batch, None, None), P(batch, None, None), P(batch, None), P(batch, None))
        + (P(),) * 15
        + (P(None, "feat"), P(None, "feat"), P("feat", None))
    )
    return jax.shard_map(
        partial(on_device, mesh.shape["rows"], mesh.shape["feat"]),
        mesh=mesh,
        in_specs=placed,
        out_specs=(
            P(batch, None, None),
            P(batch, None, None),
            P("feat"),
            P("feat", None),
            P("feat", None),
            P("feat", None),
            P("feat", None),
            P("feat", None),
            P(),
            P(),
            P(),
            P(),
            P(),
            P(),
            P(),
            P("feat", None),
            P("feat"),
            P(None, "feat"),
            P(None, "feat"),
            P("feat", None),
        ),
        check_vma=False,
    )
```

```python
from functools import partial

import jax
import jax.numpy as jnp
from jax import lax
from jax.experimental import pallas as pl
from jax.experimental.pallas import tpu as pltpu
from jax.sharding import PartitionSpec as P

MB = 16
GROUP = 3
EPSILON = 1e-06
BASE_RATE = 0.1
F32 = jnp.float32
BF16 = jnp.bfloat16


def dot(left, right, left_dim=1, right_dim=0):
    return lax.dot_general(
        left, right, (((left_dim,), (right_dim,)), ((), ())), preferred_element_type=F32
    )


def low(values):
    return values.astype(BF16)


def gelu_parts(values):
    phi = 0.5 + 0.5 * lax.erf(values * 0.7071067811865476)
    density = jnp.exp(-0.5 * values * values) * 0.3989422804014327
    return (values * phi, phi + values * density, density * (2.0 - values * values))


def mean_last(values):
    return jnp.sum(values, -1, keepdims=True) * (1.0 / values.shape[-1])


def sum_rows(values):
    return jnp.sum(values, 0, keepdims=True)


def row_of(ref):
    return ref[...].astype(F32).reshape(1, ref.shape[0])


def column_of(row):
    size = row.shape[1]
    return jnp.transpose(jnp.broadcast_to(row, (size, size)))[:, 0:1]


def segment_masks(seg_row):
    size = seg_row.shape[1]
    rows = lax.broadcasted_iota(jnp.int32, (size, size), 0)
    cols = lax.broadcasted_iota(jnp.int32, (size, size), 1)
    same = column_of(seg_row) == seg_row
    block = MB.bit_length() - 1
    later = lax.shift_right_logical(rows, block) > lax.shift_right_logical(cols, block)
    inclusive = jnp.where(same & (cols <= rows), 1.0, 0.0)
    strict = jnp.where(same & later, 1.0, 0.0)
    return (inclusive, strict)


def forward_kernel(
    seg_smem,
    seg_ref,
    live_ref,
    tok_ref,
    gain1_ref,
    wq_hbm,
    wk_hbm,
    wv_hbm,
    wg_hbm,
    wr_ref,
    br_ref,
    w1_ref,
    b1_ref,
    w2t_ref,
    b2_ref,
    ig_ref,
    ib_ref,
    wo_hbm,
    gain2_ref,
    pair_ref,
    normed_two_ref,
    *refs,
):
    saved = (len(refs) - 15) // 2
    outs, kept, scratch = refs[0:saved], refs[saved : 2 * saved], refs[2 * saved :]
    (
        resid_ref,
        gelu_ref,
        slope_ref,
        qk_ref,
        ecol_ref,
        erow_ref,
        fcol_ref,
        slope1_ref,
        curve1_ref,
        act_ref,
        d1_ref,
        d2_ref,
        n_ref,
        s_ref,
        fit_ref,
        w2s_ref,
        p1_ref,
        p2_ref,
        slopeq_ref,
        nq_ref,
        sq_ref,
    ) = kept
    q_s, k_s, v_s, out_s, w1_s, w1b_s, b1_s, w2_s, b2_s, b1f, b2f, igf, ibf, weights_s, sems = scratch
    length, width = tok_ref.shape[1], tok_ref.shape[2]
    copies = [
        pltpu.make_async_copy(w, weights_s.at[i], sems.at[i])
        for i, w in enumerate((wk_hbm, wv_hbm, wq_hbm, wg_hbm, wo_hbm))
    ]
    for copy in copies:
        copy.start()
    saves = [
        pltpu.make_async_copy(kept[i], outs[i], sems.at[len(copies) + i]) for i in range(saved)
    ]

    def save(*indices):
        for i in indices:
            saves[i].start()

    heads, head = w1_ref.shape[0], w1_ref.shape[1]
    blocks = length // MB
    tok = tok_ref[0].astype(F32)
    spread = lax.rsqrt(mean_last(tok * tok) + EPSILON)
    normed = low(tok * spread * row_of(gain1_ref))
    pair_ref[0] = normed
    seg_row = seg_ref[...].astype(F32)
    live = column_of(live_ref[...].astype(F32))
    rate_pre = dot(normed, wr_ref[...], 1, 1) + br_ref[...].astype(F32)
    sig = jax.nn.sigmoid(rate_pre)
    rates = (BASE_RATE / head) * sig * live
    ecol_ref[...] = jnp.zeros(ecol_ref.shape, F32)
    ecol_ref[:, 0:heads] = rates
    fcol_ref[...] = jnp.zeros(fcol_ref.shape, F32)
    fcol_ref[:, 0:heads] = rates * (1.0 - sig)
    erow_ref[...] = jnp.transpose(ecol_ref[...])[0 : erow_ref.shape[0]]

    def project(i, to):
        copies[i].wait()
        whole = dot(normed, weights_s[i])
        for h in range(heads):
            to[h] = whole[:, h * head : (h + 1) * head]

    project(0, k_s)
    project(1, v_s)
    b1f[...] = b1_ref[...].astype(F32)
    b2f[...] = b2_ref[...].astype(F32)
    igf[...] = ig_ref[...].astype(F32)
    ibf[...] = ib_ref[...].astype(F32)
    for h in range(heads):
        qk_ref[h, length : 2 * length] = low(k_s[h])

    def step(b, carry):
        here = pl.multiple_of(b * MB, MB)
        before = jnp.maximum(here - 1, 0)
        fresh = (b == 0) | (seg_smem[0, here] != seg_smem[0, before])

        ds = pl.ds(here, MB)
        rng = range(heads)
        k = [k_s[h, ds, :] for h in rng]
        v = [v_s[h, ds, :] for h in rng]
        e = [ecol_ref[ds, h : h + 1] for h in rng]
        w1f = [jnp.where(fresh, w1_ref[h].astype(F32), w1_s[h]) for h in rng]
        w2f = [jnp.where(fresh, w2t_ref[h].astype(F32), w2_s[h]) for h in rng]
        w1 = [low(w1f[h]) for h in rng]
        w2 = [low(w2f[h]) for h in rng]
        b1 = [jnp.where(fresh, b1f[h : h + 1], b1_s[h]) for h in rng]
        b2 = [jnp.where(fresh, b2f[h : h + 1], b2_s[h]) for h in rng]
        g = [igf[h : h + 1] for h in rng]
        gb = [ibf[h : h + 1] for h in rng]
        parts = [gelu_parts(dot(low(k[h]), w1[h]) + b1[h]) for h in rng]
        act = [low(parts[h][0]) for h in rng]
        z2 = [dot(act[h], w2[h], 1, 1) + b2[h] for h in rng]
        c = [z - mean_last(z) for z in z2]
        s = [lax.rsqrt(mean_last(x * x) + EPSILON) for x in c]
        n = [c[h] * s[h] for h in rng]
        fit = [g[h] * n[h] + gb[h] - (v[h] - k[h]) for h in rng]
        share = [g[h] * fit[h] for h in rng]
        m1 = [mean_last(share[h]) for h in rng]
        m2 = [mean_last(share[h] * n[h]) for h in rng]
        d2 = [s[h] * (share[h] - m1[h] - n[h] * m2[h]) for h in rng]
        back = [dot(low(d2[h]), w2[h]) for h in rng]
        d1 = [back[h] * parts[h][1] for h in rng]
        d1b = [low(d1[h]) for h in rng]
        ed2 = [d2[h] * e[h] for h in rng]
        up1 = [dot(low(k[h] * e[h]), d1b[h], 0, 0) for h in rng]
        up2 = [dot(low(ed2[h]), act[h], 0, 0) for h in rng]
        for h in rng:
            w1n = w1f[h] - up1[h]
            w1_s[h] = w1n
            w2s_ref[b, h] = w2[h]
            w2_s[h] = w2f[h] - up2[h]
            b1_s[h] = b1[h] - sum_rows(d1[h] * e[h])
            b2_s[h] = b2[h] - sum_rows(ed2[h])
            act_ref[h, pl.ds(length + here, MB), :] = act[h]
            slope1_ref[h, ds, :] = low(parts[h][1])
            curve1_ref[h, ds, :] = low(back[h] * parts[h][2])
            d1_ref[h, ds, :] = d1b[h]
            d2_ref[h, ds, :] = low(d2[h])
            n_ref[h, ds, :] = low(n[h])
            s_ref[ds, h : h + 1] = s[h]
            fit_ref[h, ds, :] = low(fit[h])
        return carry

    save(4, 5, 6)
    lax.fori_loop(0, blocks, step, 0, unroll=4)
    save(7, 8, 10, 11, 12, 13, 14, 15)
    project(2, q_s)
    for h in range(heads):
        qk_ref[h, 0:length] = low(q_s[h])
    save(3)
    inclusive, _ = segment_masks(seg_row)
    for start in range(0, heads, GROUP):
        rng = range(start, start + GROUP)
        every = range(GROUP)
        queries = [qk_ref[h, 0:length] for h in rng]
        keys = [qk_ref[h, length : 2 * length] for h in rng]
        key_act = [act_ref[h, length : 2 * length] for h in rng]
        er = [erow_ref[h : h + 1, :] for h in rng]
        p1 = [(dot(queries[i], keys[i], 1, 1) + 1.0) * inclusive for i in every]
        zq1 = [
            dot(queries[i], w1_ref[h]) + b1f[h : h + 1] - dot(low(p1[i] * er[i]), d1_ref[h])
            for i, h in enumerate(rng)
        ]
        parts = [gelu_parts(x) for x in zq1]
        aq = [low(x[0]) for x in parts]
        p2 = [(dot(aq[i], key_act[i], 1, 1) + 1.0) * inclusive for i in every]
        zq2 = [
            dot(aq[i], w2t_ref[h], 1, 1)
            + b2f[h : h + 1]
            - dot(low(p2[i] * er[i]), d2_ref[h])
            for i, h in enumerate(rng)
        ]
        c = [z - mean_last(z) for z in zq2]
        s = [lax.rsqrt(mean_last(x * x) + EPSILON) for x in c]
        n = [c[i] * s[i] for i in every]
        for i, h in enumerate(rng):
            p1_ref[h] = low(p1[i])
            p2_ref[h] = low(p2[i])
            act_ref[h, 0:length] = aq[i]
            slopeq_ref[h] = low(parts[i][1])
            nq_ref[h] = low(n[i])
            sq_ref[:, h : h + 1] = s[i]
            out_s[:, h * head : (h + 1) * head] = (
                q_s[h] + igf[h : h + 1] * n[i] + ibf[h : h + 1]
            )
    save(9, 16, 17, 18, 19, 20)
    inner_out = out_s[...]
    copies[3].wait()
    gate, slope, _ = gelu_parts(dot(normed, weights_s[3]))
    gelu_ref[...] = gate
    slope_ref[...] = inner_out * slope
    gated = low(inner_out * gate)
    pair_ref[1] = gated
    copies[4].wait()
    resid = tok + dot(gated, weights_s[4])
    resid_ref[...] = resid
    spread_two = lax.rsqrt(mean_last(resid * resid) + EPSILON)
    normed_two_ref[...] = low(resid * spread_two * row_of(gain2_ref))
    save(0, 1, 2)
    for copy in saves:
        copy.wait()


def ffn_kernel(x_ref, c_ref, wg_ref, wu_ref, wd_ref, act_ref, gg_ref, gu_ref, gx_ref):
    x = x_ref[...]
    gate = dot(x, wg_ref[...])
    up = dot(x, wu_ref[...])
    grad_act = dot(c_ref[...], wd_ref[...], 1, 1)
    sigma = jax.nn.sigmoid(gate)
    silu = gate * sigma
    act_ref[...] = low(silu * up)
    gg = low(grad_act * up * sigma * (1.0 + gate * (1.0 - sigma)))
    gu = low(grad_act * silu)
    gg_ref[...] = gg
    gu_ref[...] = gu
    gx_ref[...] = low(dot(gg, wg_ref[...], 1, 1) + dot(gu, wu_ref[...], 1, 1))


def ffn_weights_kernel(parts, ids_smem, *refs):
    x_refs, c_refs, act_refs, gg_refs, gu_refs = (
        refs[i * parts : (i + 1) * parts] for i in range(5)
    )
    wd_ref, kept_ref, sent_ref = refs[5 * parts : 5 * parts + 3]
    out_refs = refs[5 * parts + 3 : 6 * parts + 3]
    x_s, c_s, act_s, gg_s, gu_s = refs[6 * parts + 3 :]
    rows = x_refs[0].shape[0]
    for i in range(parts):
        at = slice(i * rows, (i + 1) * rows)
        x_s[at] = x_refs[i][...]
        c_s[at] = c_refs[i][...]
        act_s[at] = act_refs[i][...]
        gg_s[at] = gg_refs[i][...]
        gu_s[at] = gu_refs[i][...]
        out_refs[i][...] = low(dot(act_refs[i][...], wd_ref[...]))
    half = kept_ref.shape[2]
    core = ids_smem[0]
    for i, (left, right) in enumerate(((x_s, gg_s), (x_s, gu_s), (c_s, act_s))):
        whole = low(dot(left[...], right[...], 0, 0))

        @pl.when(core == 0)
        def _(whole=whole, i=i):
            kept_ref[i] = whole[:, 0:half]
            sent_ref[i] = whole[:, half:]

        @pl.when(core != 0)
        def _(whole=whole, i=i):
            kept_ref[i] = whole[:, half:]
            sent_ref[i] = whole[:, 0:half]


def between_kernel(parts, *refs):
    pieces = refs[0:parts]
    resid_ref, cot_ref, gain2_ref, wo_ref, gelu_ref, slope_ref = refs[parts : parts + 6]
    resid_grad_ref, go_ref, pair_ref, gain_grad_ref = refs[parts + 6 :]
    grad = pieces[0][...].astype(F32)
    for piece in pieces[1:]:
        grad = grad + piece[...].astype(F32)
    resid = resid_ref[...]
    spread = lax.rsqrt(mean_last(resid * resid) + EPSILON)
    scaled = row_of(gain2_ref) * grad
    grad_resid = (
        cot_ref[0].astype(F32)
        + spread * scaled
        - resid * (spread * spread * spread * mean_last(scaled * resid))
    )
    gain_grad_ref[...] = sum_rows(grad * resid * spread)
    resid_grad_ref[...] = grad_resid
    grad_branch = low(grad_resid)
    grad_gated = dot(grad_branch, wo_ref[...], 1, 1)
    go_ref[...] = grad_gated * gelu_ref[...]
    pair_ref[0] = low(grad_gated * slope_ref[...])
    pair_ref[1] = grad_branch


def backward_kernel(
    ids_smem,
    seg_smem,
    seg_ref,
    go_ref,
    qk_ref,
    ecol_ref,
    erow_ref,
    fcol_ref,
    w1_ref,
    w2t_ref,
    ig_ref,
    slope1_ref,
    curve1_ref,
    act_ref,
    d1_ref,
    d2_ref,
    n_ref,
    s_ref,
    fit_ref,
    w2s_ref,
    p1_ref,
    p2_ref,
    slopeq_ref,
    nq_ref,
    sq_ref,
    triple_ref,
    gr_ref,
    kept_ref,
    sent_ref,
    small_ref,
    igf,
    t1_s,
    t2_s,
    ga_s,
    hh1_s,
    hh2_s,
    u_s,
    share_s,
    ge_s,
    gw1_s,
    gw1b_s,
    gb1_s,
    gw2_s,
    gw2b_s,
    gb2_s,
):
    length = go_ref.shape[0]
    heads, head, inner = w1_ref.shape
    blocks = length // MB
    top, bottom = slice(0, length), slice(length, 2 * length)
    igf[...] = ig_ref[...].astype(F32)
    inclusive, strict = segment_masks(seg_ref[...].astype(F32))
    for first in range(0, heads, GROUP):
        rng = range(first, first + GROUP)
        every = range(GROUP)
        g = [igf[h : h + 1] for h in rng]
        weigh = [inclusive * erow_ref[h : h + 1, :] for h in rng]
        n = [nq_ref[h].astype(F32) for h in rng]
        x = [go_ref[:, h * head : (h + 1) * head] * igf[h : h + 1] for h in rng]
        mx = [mean_last(x[i]) for i in every]
        mxn = [mean_last(x[i] * n[i]) for i in every]
        hq2 = [
            low(sq_ref[:, h : h + 1] * (x[i] - mx[i] - n[i] * mxn[i]))
            for i, h in enumerate(rng)
        ]
        aq = [act_ref[h, top] for h in rng]
        ak = [act_ref[h, bottom] for h in rng]
        t2 = [dot(p2_ref[h], hq2[i], 0, 0) for i, h in enumerate(rng)]
        mix = [
            low(-dot(hq2[i], d2_ref[h], 1, 1) * weigh[i]) for i, h in enumerate(rng)
        ]
        gaq = [dot(hq2[i], w2t_ref[h]) + dot(mix[i], ak[i]) for i, h in enumerate(rng)]
        ga = [dot(mix[i], aq[i], 0, 0) for i in every]
        hq1 = [low(gaq[i] * slopeq_ref[h].astype(F32)) for i, h in enumerate(rng)]
        t1 = [dot(p1_ref[h], hq1[i], 0, 0) for i, h in enumerate(rng)]
        for i, h in enumerate(rng):
            hh2_s[h, top] = hq2[i]
            t2_s[h] = t2[i]
            ga_s[h] = ga[i]
            hh1_s[h, top] = hq1[i]
            t1_s[h] = t1[i]
    ge_s[...] = jnp.zeros(ge_s.shape, F32)

    def step(i, carry):
        b = blocks - 1 - i
        here = pl.multiple_of(b * MB, MB)
        after = jnp.minimum(here + MB, length - 1)
        fresh = (i == 0) | (seg_smem[0, after] != seg_smem[0, after - 1])

        ds = pl.ds(here, MB)
        ds_low = pl.ds(length + here, MB)
        rng = range(heads)
        k = [qk_ref[h, ds_low, :] for h in rng]
        act = [act_ref[h, ds_low, :] for h in rng]
        e = [ecol_ref[ds, h : h + 1] for h in rng]
        w2 = [w2s_ref[b, h] for h in rng]
        gw1 = [jnp.where(fresh, 0.0, gw1_s[h]) for h in rng]
        gw2 = [jnp.where(fresh, 0.0, gw2_s[h]) for h in rng]
        gw1b = [low(x) for x in gw1]
        gw2b = [low(x) for x in gw2]
        gb1 = [jnp.where(fresh, 0.0, gb1_s[h]) for h in rng]
        gb2 = [jnp.where(fresh, 0.0, gb2_s[h]) for h in rng]
        d1 = [d1_ref[h, ds, :].astype(F32) for h in rng]
        d2 = [d2_ref[h, ds, :].astype(F32) for h in rng]
        n = [n_ref[h, ds, :].astype(F32) for h in rng]
        s = [s_ref[ds, h : h + 1] for h in rng]
        fit = [fit_ref[h, ds, :].astype(F32) for h in rng]
        slope = [slope1_ref[h, ds, :].astype(F32) for h in rng]
        curve = [curve1_ref[h, ds, :].astype(F32) for h in rng]
        g = [igf[h : h + 1] for h in rng]
        share = [g[h] * fit[h] for h in rng]
        t1 = [t1_s[h, ds, :] + dot(k[h], gw1b[h]) + gb1[h] for h in rng]
        t2 = [t2_s[h, ds, :] + dot(act[h], gw2b[h], 1, 1) + gb2[h] for h in rng]
        g1 = [-e[h] * t1[h] for h in rng]
        u = [low(g1[h] * slope[h]) for h in rng]
        ed2 = [low(-e[h] * d2[h]) for h in rng]
        ga = [ga_s[h, ds, :] + dot(ed2[h], gw2b[h]) for h in rng]
        g2 = [dot(u[h], w2[h], 1, 1) - e[h] * t2[h] for h in rng]
        y = [s[h] * g2[h] for h in rng]
        my = [mean_last(y[h]) for h in rng]
        myn = [mean_last(y[h] * n[h]) for h in rng]
        msn = [mean_last(share[h] * n[h]) for h in rng]
        mgd = [mean_last(g2[h] * d2[h]) for h in rng]
        gshare = [y[h] - my[h] - n[h] * myn[h] for h in rng]
        gn = [g[h] * (g[h] * gshare[h]) - y[h] * msn[h] - share[h] * myn[h] for h in rng]
        mn = [mean_last(gn[h]) for h in rng]
        mnn = [mean_last(gn[h] * n[h]) for h in rng]
        h2 = [
            low(s[h] * (gn[h] - mn[h] - n[h] * (mnn[h] + mgd[h]))) for h in rng
        ]
        ga = [ga[h] + dot(h2[h], w2[h]) for h in rng]
        h1f = [ga[h] * slope[h] + g1[h] * curve[h] for h in rng]
        h1 = [low(x) for x in h1f]
        up1 = [dot(k[h], h1[h], 0, 0) for h in rng]
        up2 = [
            dot(low(d2[h]), u[h], 0, 0) + dot(h2[h], act[h], 0, 0) for h in rng
        ]
        for h in rng:
            w1n = gw1[h] + up1[h]
            w2n = gw2[h] + up2[h]
            gw1_s[h] = w1n
            gw2_s[h] = w2n
            gb1_s[h] = gb1[h] + sum_rows(h1f[h])
            gb2_s[h] = gb2[h] + sum_rows(h2[h].astype(F32))
            u_s[h, ds, :] = u[h]
            hh1_s[h, ds_low, :] = h1[h]
            hh2_s[h, ds_low, :] = h2[h]
            share_s[h, ds, :] = gshare[h]
            ge_s[ds, h : h + 1] = -jnp.sum(d1[h] * t1[h], -1, keepdims=True) - jnp.sum(
                d2[h] * t2[h], -1, keepdims=True
            )
        return carry

    lax.fori_loop(0, blocks, step, 0, unroll=4)
    small_ref[...] = jnp.zeros(small_ref.shape, F32)
    core = ids_smem[0]
    pad = small_ref.shape[0] // 2
    for start in range(0, heads, GROUP):
        rng = range(start, start + GROUP)
        every = range(GROUP)
        cols = [slice(h * head, (h + 1) * head) for h in rng]
        g = [igf[h : h + 1] for h in rng]
        er = [erow_ref[h : h + 1, :] for h in rng]
        hh1 = [hh1_s[h] for h in rng]
        hh2 = [hh2_s[h] for h in rng]
        qk = [qk_ref[h] for h in rng]
        keys = [qk_ref[h, bottom] for h in rng]
        share = [share_s[h] for h in rng]
        go = [go_ref[:, cols[i]] for i in every]
        both = [dot(hh1[i], d1_ref[h], 1, 1) for i, h in enumerate(rng)]
        direct = [dot(hh1[i], w1_ref[h], 1, 1) for i, h in enumerate(rng)]
        mixq = [low(-both[i][top] * (inclusive * er[i])) for i in every]
        mixk = [low(-both[i][bottom] * (strict * er[i])) for i in every]
        first = [low(dot(qk[i], hh1[i], 0, 0)) for i in every]
        second = [
            low(dot(hh2[i], act_ref[h], 0, 0) + dot(d2_ref[h], u_s[h], 0, 0))
            for i, h in enumerate(rng)
        ]
        gq = [low(go[i] + direct[i][top] + dot(mixq[i], keys[i])) for i in every]
        spread = [
            dot(mixq[i], qk_ref[h, top], 0, 0) + dot(mixk[i], keys[i], 0, 0)
            for i, h in enumerate(rng)
        ]
        gk = [
            low(g[i] * share[i] + direct[i][bottom] + dot(mixk[i], keys[i]) + spread[i])
            for i in every
        ]
        for i, h in enumerate(rng):
            triple_ref[0, :, cols[i]] = gq[i]
            triple_ref[1, :, cols[i]] = gk[i]
            triple_ref[2, :, cols[i]] = low(-g[i] * share[i])
            kept_ref[cols[i]] = jnp.where(core == 0, first[i], second[i])
            sent_ref[cols[i]] = jnp.where(core == 0, second[i], first[i])
            small_ref[h : h + 1] = sum_rows(hh1[i].astype(F32))
            row = slice(pad + h, pad + h + 1)
            small_ref[row, 0:head] = sum_rows(hh2[i].astype(F32))
            small_ref[row, head : 2 * head] = sum_rows(
                go[i] * nq_ref[h].astype(F32)
                + share[i] * (fit_ref[h].astype(F32) + g[i] * n_ref[h].astype(F32))
            )
            small_ref[row, 2 * head : 3 * head] = sum_rows(go[i]) + g[i] * sum_rows(share[i])
    grad_rates = ge_s[...] * fcol_ref[...]
    gr_ref[...] = low(grad_rates)
    total = jnp.broadcast_to(sum_rows(grad_rates), (grad_rates.shape[1], grad_rates.shape[1]))
    small_ref[pad : pad + heads, 3 * head : 3 * head + 1] = jnp.transpose(total)[0:heads, 0:1]


def put_matrix(to_ref, values, index, count, feats):
    chips = to_ref.shape[0]
    rows = values.shape[0] // (feats * chips)
    chunks = values.shape[1] // 128
    for f in range(feats):
        for l in range(chunks):
            row = ((f * count + index) * chunks + l) * rows
            for j in range(chips):
                at = (f * chips + j) * rows
                to_ref[j, row : row + rows, :] = values[at : at + rows, l * 128 : (l + 1) * 128]


def core_columns(core, values):
    half = values.shape[1] // 2
    return jnp.where(core == 0, values[:, 0:half], values[:, half:])


def put_halves(ids_smem, kept_ref, sent_ref, put):
    core, chip = ids_smem[0], ids_smem[1]
    first, second = 1 + core, 2 - core
    put(kept_ref.at[0], chip)
    put(kept_ref.at[1], lax.bitwise_xor(chip, second))
    put(sent_ref.at[0], lax.bitwise_xor(chip, first))
    put(sent_ref.at[1], lax.bitwise_xor(chip, 3))


def gate_weights_kernel(
    feats,
    ids_smem,
    mine_ref,
    other_ref,
    grads_ref,
    other_grads_ref,
    wg_ref,
    kept_ref,
    got_ref,
    part_ref,
    kept_out,
    sent_out,
    pieces_s,
    left_s,
    right_s,
):
    core = ids_smem[0]
    length = mine_ref.shape[1]
    for i in range(2):
        left_s[i, 0:length] = mine_ref[i]
        left_s[i, length : 2 * length] = other_ref[i]
        right_s[i, 0:length] = core_columns(core, grads_ref[i])
        right_s[i, length : 2 * length] = core_columns(core, other_grads_ref[i])
    for i in range(2):
        put_matrix(pieces_s, low(dot(left_s[i], right_s[i], 0, 0)), i, 2, feats)
    count, _, half = kept_ref.shape
    chunks = half // 128
    before = kept_out.shape[1] - pieces_s.shape[1]
    rows = before // (count * chunks)

    def put(out, place):
        at = pl.ds(pl.multiple_of(place * rows, rows), rows)
        for i in range(count):
            both = low(kept_ref[i, at, :].astype(F32) + got_ref[i, at, :].astype(F32))
            for l in range(chunks):
                row = (i * chunks + l) * rows
                out[row : row + rows] = both[:, l * 128 : (l + 1) * 128]
        out[before:] = pieces_s[place]

    put_halves(ids_smem, kept_out, sent_out, put)
    part_ref[...] = dot(grads_ref[0], wg_ref[...], 1, 1)


def input_kernel(
    feats,
    triple_ref,
    gr_ref,
    pair_ref,
    wq_ref,
    wk_ref,
    wv_ref,
    wr_ref,
    part_ref,
    tok_ref,
    gain1_ref,
    resid_grad_ref,
    small_ref,
    gain_two_ref,
    grad_ref,
    small_out,
):
    heads = wr_ref.shape[0]
    grad = part_ref[...] + dot(triple_ref[0], wq_ref[...], 1, 1)
    grad = grad + dot(triple_ref[1], wk_ref[...], 1, 1) + dot(triple_ref[2], wv_ref[...], 1, 1)
    gr = gr_ref[...]
    grad = grad + dot(gr[:, 0:heads], wr_ref[...])
    tok = tok_ref[0].astype(F32)
    spread = lax.rsqrt(mean_last(tok * tok) + EPSILON)
    scaled = row_of(gain1_ref) * grad
    grad_ref[0] = (
        resid_grad_ref[...]
        + spread * scaled
        - tok * (spread * spread * spread * mean_last(scaled * tok))
    )
    rate_rows = dot(gr, pair_ref[0], 0, 0)
    gain_row = sum_rows(grad * tok * spread)
    small_out[...] = jnp.zeros(small_out.shape, BF16)
    share = tok.shape[1] // feats
    for f in range(feats):
        cols = slice(f * share, (f + 1) * share)
        small_out[f * 16 : f * 16 + 16, 0:share] = low(
            jnp.concatenate(
                [rate_rows[0:heads, cols], gain_row[:, cols], gain_two_ref[:, cols]]
                + [jnp.zeros((14 - heads, share), F32)],
                0,
            )
        )
    at = feats * 16
    small_out[at : at + small_ref.shape[0]] = low(small_ref[...])


def tails_kernel(ids_smem, kept_ref, got_ref, kept_out, sent_out, tails_s):
    chips = tails_s.shape[0]
    inner = low(kept_ref[...].astype(F32) + got_ref[...].astype(F32))
    rows = inner.shape[0] // chips
    for j in range(chips):
        for l in range(2):
            tails_s[j, l * rows : (l + 1) * rows] = inner[
                j * rows : (j + 1) * rows, l * 128 : (l + 1) * 128
            ]

    def put(out, place):
        out[...] = tails_s[place]

    put_halves(ids_smem, kept_out, sent_out, put)


def late_weights_kernel(
    feats,
    ids_smem,
    mine_ref,
    other_ref,
    triple_ref,
    other_triple_ref,
    small_ref,
    kept_out,
    sent_out,
    pieces_s,
    left_s,
    right_s,
):
    core = ids_smem[0]
    length = mine_ref.shape[1]
    left_s[0:length] = mine_ref[0]
    left_s[length : 2 * length] = other_ref[0]
    for i in range(3):
        right_s[i, 0:length] = core_columns(core, triple_ref[i])
        right_s[i, length : 2 * length] = core_columns(core, other_triple_ref[i])
    for i in range(3):
        put_matrix(pieces_s, low(dot(left_s[...], right_s[i], 0, 0)), i, 3, feats)
    chips, most, _ = pieces_s.shape
    extra = small_ref.shape[0] // chips
    for j in range(chips):
        for l in range(2):
            at = most - (2 - l) * extra
            pieces_s[j, at : at + extra] = small_ref[
                j * extra : (j + 1) * extra, l * 128 : (l + 1) * 128
            ]

    def put(out, place):
        out[...] = pieces_s[place]

    put_halves(ids_smem, kept_out, sent_out, put)


def mixed_kernel(feats, resid_ref, *refs):
    kept_ref, got_ref, mixed_ref, stay_ref, go_ref = refs[feats:]
    total = resid_ref[...]
    for ref in refs[0:feats]:
        total = total + ref[...].astype(F32)
    mixed_ref[0] = low(total)
    add_kernel(kept_ref, got_ref, stay_ref, go_ref)


def add_kernel(kept_ref, got_ref, stay_ref, go_ref):
    stay_ref[...] = low(kept_ref[0].astype(F32) + got_ref[0].astype(F32))
    go_ref[...] = low(kept_ref[1].astype(F32) + got_ref[1].astype(F32))


def sum_at(refs, at):
    value = refs[0][at].astype(F32)
    for ref in refs[1:]:
        value = value + ref[at].astype(F32)
    return low(value)


def cut_feat_kernel(common, ids_smem, *refs):
    parts, outs = refs[0:2], refs[2:]
    rows = outs[0].shape[0] - common
    shared = sum_at(parts, (slice(rows * len(outs), rows * len(outs) + common), slice(None)))
    for s, out in enumerate(outs):
        at = pl.ds(pl.multiple_of(lax.bitwise_xor(ids_smem[2], s) * rows, 16), rows)
        out[0:rows] = sum_at(parts, (at, slice(None)))
        out[rows:] = shared


def sum_kernel(*refs):
    values = [ref[...].astype(F32) for ref in refs[:-1]]
    while len(values) > 1:
        values = [values[i] + values[i + 1] for i in range(0, len(values), 2)]
    refs[-1][...] = low(values[0])


def join_kernel(*refs):
    total_ref, out_ref = refs[-2:]
    rows = refs[0].shape[0]
    sum_kernel(*refs[:-2], out_ref.at[0:rows])
    out_ref[rows:] = total_ref[...]


def middle_kernel(ids_smem, *refs):
    pair, tail = refs[0:2], refs[2:4]
    total_ref, outs = refs[4], refs[5:]
    before = total_ref.shape[0]
    rows = (pair[0].shape[0] - before) // len(outs)
    shared = sum_at(tail, (slice(None), slice(None)))
    for s, out in enumerate(outs):
        at = pl.multiple_of(before + lax.bitwise_xor(ids_smem[2], s) * rows, 16)
        out[0:rows] = sum_at(pair, (pl.ds(at, rows), slice(None)))
        out[rows:] = shared
    total_ref[...] = sum_at(pair, (slice(0, before), slice(None)))


def take_matrices(ids_smem, pieces, outs, start=0, order=None):
    core, chip = ids_smem[0], ids_smem[1]
    chunks = outs[0].shape[1] // 256
    rows = outs[0].shape[0] // len(pieces)
    for s, both in enumerate(pieces):
        ats = [
            pl.ds(pl.multiple_of(lax.bitwise_xor(chip, d) * rows, 16), rows)
            for d in (order[s] if order else (s, s))
        ]
        for i, out in enumerate(outs):
            for l in range(chunks):
                row = start + (i * chunks + l) * rows
                mine = both[0][row : row + rows, :].astype(F32)
                other = both[1][row : row + rows, :].astype(F32)
                low_cols = slice(l * 128, (l + 1) * 128)
                high_cols = slice((chunks + l) * 128, (chunks + l + 1) * 128)

                @pl.when(core == 0)
                def _(out=out, ats=ats, mine=mine, other=other, a=low_cols, b=high_cols):
                    out[ats[0], a] = mine
                    out[ats[1], b] = other

                @pl.when(core != 0)
                def _(out=out, ats=ats, mine=mine, other=other, a=low_cols, b=high_cols):
                    out[ats[0], b] = mine
                    out[ats[1], a] = other


def early_totals_kernel(ids_smem, *refs):
    core, chip = ids_smem[0], ids_smem[1]
    first, second = 1 + core, 2 - core
    pieces = [(refs[s], refs[4 + s]) for s in range(4)]
    order = [(0, 0), (second, first), (first, second), (3, 3)]
    gate_ref, up_ref, down_ref, wg_ref, wo_ref, first_ref, second_ref, down_s = refs[8:]
    take_matrices(ids_smem, pieces, (wg_ref, wo_ref), order=order)
    rows = first_ref.shape[0] // 4
    start = 2 * (wg_ref.shape[0] // 4) * (wg_ref.shape[1] // 256)
    for s, both in enumerate(pieces):
        ats = [
            pl.ds(pl.multiple_of(lax.bitwise_xor(chip, d) * rows, 16), rows) for d in order[s]
        ]
        for l in range(2):
            cols = slice(l * 128, (l + 1) * 128)
            row = start + l * rows
            mine = both[0][row : row + rows].astype(F32)
            other = both[1][row : row + rows].astype(F32)

            @pl.when(core == 0)
            def _(ats=ats, cols=cols, mine=mine, other=other):
                first_ref[ats[0], cols] = mine
                second_ref[ats[1], cols] = other

            @pl.when(core != 0)
            def _(ats=ats, cols=cols, mine=mine, other=other):
                first_ref[ats[1], cols] = other
                second_ref[ats[0], cols] = mine

    take_matrices(ids_smem, pieces, (gate_ref, up_ref, down_s), start + 2 * rows, order)
    down_ref[...] = jnp.transpose(down_s[...])


def late_totals_kernel(chips, feats, heads, head, ids_smem, *refs):
    pieces = [(refs[s], refs[chips + s]) for s in range(chips)]
    matrices = refs[2 * chips : 2 * chips + 3]
    (rate_ref, norm1_ref, norm2_ref, b1_ref, b2_ref, ig_ref, ib_ref, br_ref, small_s) = refs[
        2 * chips + 3 :
    ]
    chip, feat = ids_smem[1], ids_smem[2]
    take_matrices(ids_smem, pieces, matrices)
    extra = small_s.shape[0] // chips
    most = refs[0].shape[0]
    for s, both in enumerate(pieces):
        at = pl.ds(pl.multiple_of(lax.bitwise_xor(chip, s) * extra, 16), extra)
        for l in range(2):
            row = most - (2 - l) * extra
            small_s[at, l * 128 : (l + 1) * 128] = both[0][row : row + extra].astype(
                F32
            ) + both[1][row : row + extra].astype(F32)
    share = rate_ref.shape[1]
    block = small_s[pl.ds(pl.multiple_of(feat * 16, 16), 16), :]
    rate_ref[...] = block[0:heads, 0:share]
    norm1_ref[...] = block[heads : heads + 1, 0:share]
    norm2_ref[...] = block[heads + 1 : heads + 2, 0:share]
    at = feats * 16
    b1_ref[...] = small_s[at : at + heads, :]
    packed = small_s[at + 16 : at + 16 + heads, :]
    b2_ref[...] = packed[:, 0:head]
    ig_ref[...] = packed[:, head : 2 * head]
    ib_ref[...] = packed[:, 2 * head : 3 * head]
    br_ref[...] = jnp.transpose(small_s[at + 16 : at + 32, 128:])[3 * head - 128 : 3 * head - 127, 0:heads]


def held(values):
    return pltpu.with_memory_space_constraint(values, pltpu.VMEM)


def in_order():
    last = []

    def ordered(kernel, outs, inputs, scratch=(), **options):
        inputs = list(inputs)
        at = options.get("smem", 0)
        if last:
            inputs[at], _ = lax.optimization_barrier((inputs[at], last.pop()))
        found = call(kernel, outs, inputs, scratch, **options)
        last.append(found[0])
        return found

    return ordered


def call(
    kernel, outs, inputs, scratch=(), smem=0, cover=True, plain=(), loose=(), keep=True, mib=24
):
    specs, placed = [], []
    for i, x in enumerate(inputs):
        if i < smem:
            specs.append(pl.BlockSpec(memory_space=pltpu.SMEM))
            placed.append(x)
        elif i in loose:
            specs.append(pl.BlockSpec(memory_space=pltpu.HBM))
            placed.append(pltpu.with_memory_space_constraint(x, pltpu.HBM))
        elif i in plain:
            specs.append(pl.BlockSpec(memory_space=pltpu.VMEM))
            placed.append(pltpu.with_memory_space_constraint(x, pltpu.HBM))
        else:
            specs.append(pl.BlockSpec(memory_space=pltpu.VMEM))
            placed.append(held(x))
    kept = [keep] * len(outs) if isinstance(keep, bool) else list(keep)
    return pl.pallas_call(
        kernel,
        out_shape=[
            pltpu.VMEM(s, d) if k else pltpu.HBM(s, d) for (s, d), k in zip(outs, kept)
        ],
        in_specs=specs,
        out_specs=[
            pl.BlockSpec(memory_space=pltpu.HBM if k is None else pltpu.VMEM) for k in kept
        ],
        scratch_shapes=[pltpu.VMEM(*x) if isinstance(x, tuple) else x for x in scratch],
        cost_estimate=pl.CostEstimate(
            flops=int(2e10 if cover else 1e6), bytes_accessed=int(2e7 if cover else 1e3), transcendentals=0
        ),
        compiler_params=pltpu.CompilerParams(vmem_limit_bytes=mib * 2**20),
    )(*placed)


def exchange(values, axis, size, distance):
    return lax.ppermute(values, axis, [(i, i ^ distance) for i in range(size)])


def add_low(left, right):
    return low(left.astype(F32) + right.astype(F32))


def halve(values, axis, size, distance, dim):
    side = lax.bitwise_and(lax.axis_index(axis) // distance, 1)
    half = values.shape[dim] // 2
    kept = lax.dynamic_slice_in_dim(values, side * half, half, dim)
    sent = lax.dynamic_slice_in_dim(values, (1 - side) * half, half, dim)
    return add_low(kept, exchange(sent, axis, size, distance))


def double(values, axis, size, distance, dim):
    side = lax.bitwise_and(lax.axis_index(axis) // distance, 1)
    other = exchange(values, axis, size, distance)
    return jnp.where(
        side == 0,
        jnp.concatenate([values, other], dim),
        jnp.concatenate([other, values], dim),
    )


def distances(size):
    found = []
    step = 1
    while step < size:
        found.append(step)
        step *= 2
    return found


def across_chips(values, rows):
    return [values[0]] + [
        exchange(values[s], "rows", rows, 2 * s) for s in range(1, len(values))
    ]


def across_feats(values, feats):
    return [values[0]] + [exchange(values[s], "feat", feats, s) for s in range(1, feats)]


def first_axis(values, rows):
    return lax.ppermute(values, "rows", [(i, i ^ (2 << (i & 1))) for i in range(rows)])


def second_axis(values, rows):
    return lax.ppermute(values, "rows", [(i, i ^ (4 >> (i & 1))) for i in range(rows)])


def halved(launch, kept, got, rows, cover):
    stay, go = launch(add_kernel, [(kept.shape[1:], BF16)] * 2, [kept, got], cover=cover)
    return stay, second_axis(go, rows)


def other_core(values, rows):
    return exchange(values, "rows", rows, 1)


def scatter_rows(values, size, dim):
    for d in distances(size):
        values = halve(values, "rows", size, d, dim)
    return values


def gather_rows(values, size, dim):
    for d in reversed(distances(size)):
        values = double(values, "rows", size, d, dim)
    return values


def scatter_feat(values, size, dim):
    me = lax.axis_index("feat")
    total = lax.dynamic_index_in_dim(values, me, dim, keepdims=False).astype(F32)
    for s in range(1, size):
        piece = lax.dynamic_index_in_dim(values, lax.bitwise_xor(me, s), dim, keepdims=False)
        total = total + exchange(piece, "feat", size, s).astype(F32)
    return low(total)


def on_device(
    rows,
    feats,
    tokens,
    cotangent,
    seg_ids,
    pad_mask,
    norm1_gain,
    w_query,
    w_key,
    w_value,
    w_gate,
    w_rate,
    b_rate,
    inner_w1,
    inner_b1,
    inner_w2,
    inner_b2,
    inner_gain,
    inner_bias,
    w_out,
    norm2_gain,
    ffn_gate,
    ffn_up,
    ffn_down,
):
    launch = in_order()
    _, length, width = tokens.shape
    heads, head, inner = inner_w1.shape
    hidden = ffn_gate.shape[1]
    blocks = length // MB
    chips = rows // 2
    line = (length, width)
    wide = (heads, length, inner)
    slim = (heads, length, head)
    square = (heads, length, length)
    state = (heads, head, inner)
    w2t = jnp.transpose(inner_w2, (0, 2, 1))
    w_rate_t = jnp.transpose(w_rate)
    place = lax.axis_index("rows")
    me = lax.axis_index("feat")
    ids = jnp.stack([lax.bitwise_and(place, 1), lax.shift_right_logical(place, 1), me])
    cots = across_feats([cotangent[0]] * feats, feats)
    kept = [
        (line, F32),
        (line, F32),
        (line, F32),
        ((heads, 2 * length, head), BF16),
        ((length, 128), F32),
        ((16, length), F32),
        ((length, 128), F32),
        (wide, BF16),
        (wide, BF16),
        ((heads, 2 * length, inner), BF16),
        (wide, BF16),
        (slim, BF16),
        (slim, BF16),
        ((length, 128), F32),
        (slim, BF16),
        ((blocks,) + state, BF16),
        (square, BF16),
        (square, BF16),
        (wide, BF16),
        (slim, BF16),
        ((length, 128), F32),
    ]
    saved = launch(
        forward_kernel,
        [((2,) + line, BF16), (line, BF16)] + kept,
        [
            seg_ids,
            seg_ids,
            pad_mask,
            tokens,
            norm1_gain,
            w_query,
            w_key,
            w_value,
            w_gate,
            w_rate_t,
            b_rate[None],
            inner_w1,
            inner_b1,
            w2t,
            inner_b2,
            inner_gain,
            inner_bias,
            w_out,
            norm2_gain,
        ],
        kept
        + [
            (slim, F32),
            (slim, F32),
            (slim, F32),
            (line, F32),
            (state, F32),
            (state, BF16),
            ((heads, 1, inner), F32),
            (state, F32),
            ((heads, 1, head), F32),
            ((heads, inner), F32),
            ((heads, head), F32),
            ((heads, head), F32),
            ((heads, head), F32),
            ((5, width, width), BF16),
            pltpu.SemaphoreType.DMA((5 + len(kept),)),
        ],
        smem=1,
        plain=range(19),
        loose=(5, 6, 7, 8, 17),
        keep=[True, True] + [None] * len(kept),
        mib=48,
    )
    pair, normed_two, resid, gelu_gate, gate_slope = saved[0:5]
    qk, ecol, erow, fcol = saved[5:9]
    rest = saved[9:]
    normed_two, *cots = lax.optimization_barrier([normed_two] + cots)
    blocks_in = [normed_two]
    acts, ggs, gus, pieces = [], [], [], []
    for s in range(1, feats):
        if s & (s - 1) == 0:
            blocks_in.append(exchange(normed_two, "feat", feats, s))
        else:
            blocks_in.append(None)
    for s in range(feats):
        if blocks_in[s] is None:
            nearest = s & -s
            held_back, _ = lax.optimization_barrier((blocks_in[s ^ nearest], pieces[1]))
            blocks_in[s] = exchange(held_back, "feat", feats, nearest)
        act, gg, gu, gx = launch(
            ffn_kernel,
            [((length, hidden), BF16)] * 3 + [(line, BF16)],
            [blocks_in[s], cots[s], ffn_gate, ffn_up, ffn_down],
        )
        acts.append(act)
        ggs.append(gg)
        gus.append(gu)
        pieces.append(gx)
    if feats > 2:
        pieces[1], _ = lax.optimization_barrier((pieces[1], acts[2]))
    pieces = across_feats(pieces, feats)

    def between(pieces):
        return launch(
            partial(between_kernel, feats),
            [(line, F32), (line, F32), ((2,) + line, BF16), ((1, width), F32)],
            pieces + [resid, cotangent, norm2_gain, w_out, gelu_gate, gate_slope],
        )

    def inner_backward(grad_inner_out):
        return launch(
            backward_kernel,
            [
                ((3,) + line, BF16),
                ((length, 128), BF16),
                ((heads * head, inner), BF16),
                ((heads * head, inner), BF16),
                ((32, inner), F32),
            ],
            [ids, seg_ids, seg_ids, grad_inner_out, qk, ecol, erow, fcol, inner_w1, w2t]
            + [inner_gain]
            + list(rest),
            [
                ((heads, head), F32),
                (wide, F32),
                (slim, F32),
                (wide, F32),
                ((heads, 2 * length, inner), BF16),
                ((heads, 2 * length, head), BF16),
                (wide, BF16),
                (slim, F32),
                ((length, 128), F32),
                (state, F32),
                (state, BF16),
                ((heads, 1, inner), F32),
                (state, F32),
                (state, BF16),
                ((heads, 1, head), F32),
            ],
            smem=2,
        )

    step = 16 * chips
    small_rows = -(-(16 * feats + 32) // step) * step

    def finish(triple, grad_rates, small, part, grad_resid, grad_gain_two):
        return launch(
            partial(input_kernel, feats),
            [((1,) + line, F32), ((small_rows, inner), BF16)],
            [triple, grad_rates, pair, w_query, w_key, w_value, w_rate_t, part]
            + [tokens, norm1_gain, grad_resid, small, grad_gain_two],
            keep=(False, True),
            cover=False,
        )

    if chips != 4 or (width // feats) % step or hidden % 256 or width % 256:
        grad_resid, grad_inner_out, grad_pair, grad_gain_two = between(pieces)
        out, grads = plain_totals(
            rows, feats, blocks_in, cots, acts, ggs, gus, ffn_down, pair, grad_pair, w_gate
        )
        triple, grad_rates, kept, sent, small = inner_backward(grad_inner_out)
        out = across_feats(out, feats)
        mixed = low(resid + sum(x.astype(F32) for x in out))[None]
        grad_tokens, small = finish(
            triple, grad_rates, small, grads.pop(), grad_resid, grad_gain_two
        )
        late = plain_late_totals(rows, feats, pair, triple, kept, sent, small, state)
        return arrange(mixed, grad_tokens, grads, late, state)
    ffn = launch(
        partial(ffn_weights_kernel, feats),
        [((3, width, hidden // 2), BF16)] * 2 + [(line, BF16)] * feats,
        [ids] + blocks_in + cots + acts + ggs + gus + [ffn_down],
        [((feats * length, width), BF16)] * 2 + [((feats * length, hidden), BF16)] * 3,
        smem=1,
    )
    grad_resid, grad_inner_out, grad_pair, grad_gain_two = between(pieces)
    ffn_sent, _ = lax.optimization_barrier((ffn[1], grad_pair))
    pair_other = other_core(pair, rows)
    half = width // 2
    per = width // (feats * chips) * (half // 128)
    ffn_rows = 3 * (width // chips) * (hidden // 256)
    part, early, early_sent = launch(
        partial(gate_weights_kernel, feats),
        [(line, F32)] + [((2, ffn_rows + feats * 2 * per, 128), BF16)] * 2,
        [ids, pair, pair_other, grad_pair, other_core(grad_pair, rows), w_gate]
        + [ffn[0], other_core(ffn_sent, rows)],
        [
            ((chips, feats * 2 * per, 128), BF16),
            ((2, 2 * length, width), BF16),
            ((2, 2 * length, half), BF16),
        ],
        smem=1,
    )
    early_got = first_axis(early_sent, rows)
    out, _ = lax.optimization_barrier((ffn[2:], part))
    out = across_feats(out, feats)
    triple, grad_rates, kept, sent, small = inner_backward(grad_inner_out)
    triple_other = other_core(triple, rows)
    inner_got = other_core(sent, rows)
    mixed, early, early_sent = launch(
        partial(mixed_kernel, feats),
        [((1,) + line, BF16)] + [(early.shape[1:], BF16)] * 2,
        [resid] + out + [early, early_got],
        keep=(False, True, True),
    )
    early_got = second_axis(early_sent, rows)
    tail = 2 * heads * head // chips
    tails, tails_sent = launch(
        tails_kernel,
        [((2, tail, 128), BF16)] * 2,
        [ids, kept, inner_got],
        [((chips, tail, 128), BF16)],
        smem=1,
        cover=False,
    )
    tails_got = first_axis(tails_sent, rows)
    grad_tokens, small = finish(triple, grad_rates, small, part, grad_resid, grad_gain_two)
    tails, tails_got = halved(launch, tails, tails_got, rows, False)
    early_got, small = lax.optimization_barrier((early_got, small))
    common = 2 * small_rows // chips
    late, late_sent = launch(
        partial(late_weights_kernel, feats),
        [((2, feats * 3 * per + common, 128), BF16)] * 2,
        [ids, pair, pair_other, triple, triple_other, small],
        [
            ((chips, feats * 3 * per + common, 128), BF16),
            ((2 * length, width), BF16),
            ((3, 2 * length, half), BF16),
        ],
        smem=1,
    )
    late_got = first_axis(late_sent, rows)
    ffn_total, *cut = launch(
        middle_kernel,
        [((ffn_rows, 128), BF16)] + [((2 * per + tail, 128), BF16)] * feats,
        [ids, early, early_got, tails, tails_got],
        smem=1,
    )
    cut = across_feats(cut, feats)
    late, late_got = halved(launch, late, late_got, rows, True)
    (joined,) = launch(
        join_kernel, [((2 * per + tail + ffn_rows, 128), BF16)], cut + [ffn_total]
    )
    late_cut = launch(
        partial(cut_feat_kernel, common),
        [((3 * per + common, 128), BF16)] * feats,
        [ids, late, late_got],
        smem=1,
        cover=False,
    )
    joined, late_cut = lax.optimization_barrier((joined, late_cut))
    late_cut = across_feats(late_cut, feats)
    near = second_axis(joined, rows)
    joined = [joined, near, first_axis(joined, rows), first_axis(near, rows)]
    (late_total,) = launch(sum_kernel, [((3 * per + common, 128), BF16)], late_cut)
    late = across_chips([late_total] * chips, rows)
    late += [other_core(x, rows) for x in late]
    joined += [other_core(x, rows) for x in joined]
    share = (width // feats, width)
    late = launch(
        partial(late_totals_kernel, chips, feats, heads, head),
        [(share, F32)] * 3
        + [((heads, width // feats), F32)]
        + [((1, width // feats), F32)] * 2
        + [((heads, inner), F32)]
        + [((heads, head), F32)] * 3
        + [((1, heads), F32)],
        [ids] + late,
        [((small_rows, inner), F32)],
        smem=1,
        keep=False,
    )
    early = launch(
        early_totals_kernel,
        [((width, hidden), F32)] * 2
        + [((hidden, width), F32)]
        + [(share, F32)] * 2
        + [((heads * head, inner), F32)] * 2,
        [ids] + joined,
        [((width, hidden), F32)],
        smem=1,
        keep=False,
    )
    early, late = list(early), list(late)
    return arrange(mixed, grad_tokens, early[0:5], late[0:3] + early[5:7] + late[3:], state)


def arrange(mixed, grad_tokens, early, late, state):
    return (
        mixed,
        grad_tokens,
        late[6][0],
        late[0],
        late[1],
        late[2],
        early[3],
        jnp.transpose(late[5]),
        late[12][0],
        late[3].reshape(state),
        late[8],
        jnp.transpose(late[4].reshape(state), (0, 2, 1)),
        late[9],
        late[10],
        late[11],
        early[4],
        late[7][0],
        early[0],
        early[1],
        early[2],
    )


def contract(left, right):
    return low(dot(left, right, 0, 0))


def plain_features(values, rows, feats):
    width = values.shape[0]
    values = values.reshape((feats, width // feats, width))
    values = scatter_feat(scatter_rows(values, rows, 1), feats, 0)
    return gather_rows(values, rows, 0).astype(F32)


def plain_totals(
    rows, feats, blocks_in, cots, acts, ggs, gus, ffn_down, pair, grad_pair, w_gate
):
    def joined(parts):
        return jnp.concatenate(parts, 0)

    def over_rows(values):
        return gather_rows(scatter_rows(values, rows, 0), rows, 0).astype(F32)

    x, c, act = joined(blocks_in), joined(cots), joined(acts)
    out = [low(dot(a, ffn_down)) for a in acts]
    grads = [contract(x, joined(ggs)), contract(x, joined(gus)), contract(act, c)]
    grads = [over_rows(g) for g in grads]
    for i in range(2):
        grads.append(plain_features(contract(pair[i], grad_pair[i]), rows, feats))
    grads.append(dot(grad_pair[0], w_gate, 1, 1))
    return out, grads


def plain_late_totals(rows, feats, pair, triple, kept, sent, small, state):
    heads, head, _ = state
    me = lax.axis_index("feat")
    core = lax.bitwise_and(lax.axis_index("rows"), 1)
    late = [plain_features(contract(pair[0], triple[i]), rows, feats) for i in range(3)]
    both = jnp.where(core == 0, jnp.stack([kept, sent]), jnp.stack([sent, kept]))
    both = scatter_rows(both, rows, 1)
    for d in distances(feats):
        both = add_low(both, exchange(both, "feat", feats, d))
    both = gather_rows(both, rows, 1).astype(F32)
    for d in distances(rows):
        small = add_low(small, exchange(small, "rows", rows, d))
    for d in distances(feats):
        small = add_low(small, exchange(small, "feat", feats, d))
    small = small.astype(F32)
    share = pair.shape[2] // feats
    block = lax.dynamic_slice_in_dim(small, me * 16, 16, 0)[:, 0:share]
    at = feats * 16
    packed = small[at + 16 : at + 16 + heads]
    return late + [
        both[0],
        both[1],
        block[0:heads],
        block[heads : heads + 1],
        block[heads + 1 : heads + 2],
        small[at : at + heads],
        packed[:, 0:head],
        packed[:, head : 2 * head],
        packed[:, 2 * head : 3 * head],
        packed[:, 3 * head : 3 * head + 1].reshape(1, heads),
    ]


def solution(mesh):
    batch = ("rows", "feat")
    placed = (
        (P(batch, None, None), P(batch, None, None), P(batch, None), P(batch, None))
        + (P(),) * 15
        + (P(None, "feat"), P(None, "feat"), P("feat", None))
    )
    return jax.shard_map(
        partial(on_device, mesh.shape["rows"], mesh.shape["feat"]),
        mesh=mesh,
        in_specs=placed,
        out_specs=(
            P(batch, None, None),
            P(batch, None, None),
            P("feat"),
            P("feat", None),
            P("feat", None),
            P("feat", None),
            P("feat", None),
            P("feat", None),
            P(),
            P(),
            P(),
            P(),
            P(),
            P(),
            P(),
            P("feat", None),
            P("feat"),
            P(None, "feat"),
            P(None, "feat"),
            P("feat", None),
        ),
        check_vma=False,
    )
```

```python
from functools import partial

import jax
import jax.numpy as jnp
from jax import lax
from jax.experimental import pallas as pl
from jax.experimental.pallas import tpu as pltpu
from jax.sharding import PartitionSpec as P

MB = 16
FORWARD_HEADS = 6
BACKWARD_HEADS = 3
EPSILON = 1e-06
BASE_RATE = 0.1
F32 = jnp.float32
BF16 = jnp.bfloat16


def dot(left, right, left_dim=1, right_dim=0):
    return lax.dot_general(
        left, right, (((left_dim,), (right_dim,)), ((), ())), preferred_element_type=F32
    )


def low(values):
    return values.astype(BF16)


def gelu_parts(values):
    phi = 0.5 + 0.5 * lax.erf(values * 0.7071067811865476)
    density = jnp.exp(-0.5 * values * values) * 0.3989422804014327
    return (values * phi, phi + values * density, density * (2.0 - values * values))


def mean_last(values):
    return jnp.sum(values, -1, keepdims=True) * (1.0 / values.shape[-1])


def sum_rows(values):
    return jnp.sum(values, 0, keepdims=True)


def row_of(ref):
    return ref[...].astype(F32).reshape(1, ref.shape[0])


def column_of(row):
    size = row.shape[1]
    return jnp.transpose(jnp.broadcast_to(row, (size, size)))[:, 0:1]


def segment_masks(seg_row):
    size = seg_row.shape[1]
    rows = lax.broadcasted_iota(jnp.int32, (size, size), 0)
    cols = lax.broadcasted_iota(jnp.int32, (size, size), 1)
    same = column_of(seg_row) == seg_row
    block = MB.bit_length() - 1
    later = lax.shift_right_logical(rows, block) > lax.shift_right_logical(cols, block)
    inclusive = jnp.where(same & (cols <= rows), 1.0, 0.0)
    strict = jnp.where(same & later, 1.0, 0.0)
    return (inclusive, strict)


def forward_kernel(
    seg_smem,
    seg_ref,
    live_ref,
    tok_ref,
    gain1_ref,
    wq_hbm,
    wk_hbm,
    wv_hbm,
    wg_hbm,
    wr_ref,
    br_ref,
    w1_ref,
    b1_ref,
    w2t_ref,
    b2_ref,
    ig_ref,
    ib_ref,
    wo_hbm,
    gain2_ref,
    pair_ref,
    normed_two_ref,
    *refs,
):
    saved = (len(refs) - 15) // 2
    outs, kept, scratch = refs[0:saved], refs[saved : 2 * saved], refs[2 * saved :]
    (
        resid_ref,
        gelu_ref,
        slope_ref,
        qk_ref,
        ecol_ref,
        erow_ref,
        fcol_ref,
        slope1_ref,
        curve1_ref,
        act_ref,
        d1_ref,
        d2_ref,
        n_ref,
        s_ref,
        fit_ref,
        w2s_ref,
        p1_ref,
        p2_ref,
        slopeq_ref,
        nq_ref,
        sq_ref,
    ) = kept
    q_s, k_s, v_s, out_s, base_s, mix_s, w2_s, b2_s = scratch[0:8]
    b1f, b2f, igf, ibf, weights_s, sems, state_sems = scratch[8:]
    length, width = tok_ref.shape[1], tok_ref.shape[2]
    copies = [
        pltpu.make_async_copy(w, weights_s.at[i], sems.at[i])
        for i, w in enumerate((wk_hbm, wv_hbm, wq_hbm, wg_hbm, wo_hbm))
    ]
    for copy in copies:
        copy.start()
    saves = {
        i: pltpu.make_async_copy(kept[i], outs[i], sems.at[len(copies) + i])
        for i in range(saved)
        if i != 15
    }

    def save(*indices):
        for i in indices:
            saves[i].start()

    heads, head = w1_ref.shape[0], w1_ref.shape[1]
    blocks = length // MB
    tok = tok_ref[0].astype(F32)
    spread = lax.rsqrt(mean_last(tok * tok) + EPSILON)
    normed = low(tok * spread * row_of(gain1_ref))
    pair_ref[0] = normed
    seg_row = seg_ref[...].astype(F32)
    live = column_of(live_ref[...].astype(F32))
    rate_pre = dot(normed, wr_ref[...], 1, 1) + br_ref[...].astype(F32)
    sig = jax.nn.sigmoid(rate_pre)
    rates = (BASE_RATE / head) * sig * live
    ecol_ref[...] = jnp.zeros(ecol_ref.shape, F32)
    ecol_ref[:, 0:heads] = rates
    fcol_ref[...] = jnp.zeros(fcol_ref.shape, F32)
    fcol_ref[:, 0:heads] = rates * (1.0 - sig)
    erow_ref[...] = jnp.transpose(ecol_ref[...])[0 : erow_ref.shape[0]]

    def project(i, to):
        copies[i].wait()
        whole = dot(normed, weights_s[i])
        for h in range(heads):
            to[h] = whole[:, h * head : (h + 1) * head]

    project(0, k_s)
    project(1, v_s)
    b1f[...] = b1_ref[...].astype(F32)
    b2f[...] = b2_ref[...].astype(F32)
    igf[...] = ig_ref[...].astype(F32)
    ibf[...] = ib_ref[...].astype(F32)
    for h in range(heads):
        qk_ref[h, length : 2 * length] = low(k_s[h])

    d1_ref[...] = jnp.zeros(d1_ref.shape, BF16)
    inclusive, strict = segment_masks(seg_row)
    for h in range(heads):
        keys = qk_ref[h, length : 2 * length]
        mix_s[h] = low((dot(keys, keys, 1, 1) + 1.0) * (strict * erow_ref[h : h + 1, :]))
        base_s[h] = dot(keys, w1_ref[h]) + b1f[h : h + 1]

    def step(b, carry):
        here = pl.multiple_of(b * MB, MB)
        before = jnp.maximum(here - 1, 0)
        fresh = (b == 0) | (seg_smem[0, here] != seg_smem[0, before])

        ds = pl.ds(here, MB)
        rng = range(heads)
        k = [k_s[h, ds, :] for h in rng]
        v = [v_s[h, ds, :] for h in rng]
        e = [ecol_ref[ds, h : h + 1] for h in rng]
        w2f = [jnp.where(fresh, w2t_ref[h].astype(F32), w2_s[h]) for h in rng]
        w2 = [low(w2f[h]) for h in rng]
        b2 = [jnp.where(fresh, b2f[h : h + 1], b2_s[h]) for h in rng]
        g = [igf[h : h + 1] for h in rng]
        gb = [ibf[h : h + 1] for h in rng]
        parts = [gelu_parts(base_s[h, ds, :] - dot(mix_s[h, ds, :], d1_ref[h])) for h in rng]
        act = [low(parts[h][0]) for h in rng]
        z2 = [dot(act[h], w2[h], 1, 1) + b2[h] for h in rng]
        c = [z - mean_last(z) for z in z2]
        s = [lax.rsqrt(mean_last(x * x) + EPSILON) for x in c]
        n = [c[h] * s[h] for h in rng]
        fit = [g[h] * n[h] + gb[h] - (v[h] - k[h]) for h in rng]
        share = [g[h] * fit[h] for h in rng]
        m1 = [mean_last(share[h]) for h in rng]
        m2 = [mean_last(share[h] * n[h]) for h in rng]
        d2 = [s[h] * (share[h] - m1[h] - n[h] * m2[h]) for h in rng]
        back = [dot(low(d2[h]), w2[h]) for h in rng]
        d1 = [back[h] * parts[h][1] for h in rng]
        d1b = [low(d1[h]) for h in rng]
        ed2 = [d2[h] * e[h] for h in rng]
        up2 = [dot(low(ed2[h]), act[h], 0, 0) for h in rng]
        for h in rng:
            w2s_ref[b, h] = w2[h]
            w2_s[h] = w2f[h] - up2[h]
            b2_s[h] = b2[h] - sum_rows(ed2[h])
            act_ref[h, pl.ds(length + here, MB), :] = act[h]
            slope1_ref[h, ds, :] = low(parts[h][1])
            curve1_ref[h, ds, :] = low(back[h] * parts[h][2])
            d1_ref[h, ds, :] = d1b[h]
            d2_ref[h, ds, :] = low(d2[h])
            n_ref[h, ds, :] = low(n[h])
            s_ref[ds, h : h + 1] = s[h]
            fit_ref[h, ds, :] = low(fit[h])
        pltpu.make_async_copy(w2s_ref.at[b], outs[15].at[b], state_sems.at[b]).start()
        return carry

    save(4, 5, 6)
    lax.fori_loop(0, blocks, step, 0, unroll=4)
    save(7, 8, 10, 11, 12, 13, 14)
    project(2, q_s)
    for h in range(heads):
        qk_ref[h, 0:length] = low(q_s[h])
    save(3)
    for start in range(0, heads, FORWARD_HEADS):
        rng = range(start, start + FORWARD_HEADS)
        every = range(FORWARD_HEADS)
        queries = [qk_ref[h, 0:length] for h in rng]
        keys = [qk_ref[h, length : 2 * length] for h in rng]
        key_act = [act_ref[h, length : 2 * length] for h in rng]
        er = [erow_ref[h : h + 1, :] for h in rng]
        p1 = [(dot(queries[i], keys[i], 1, 1) + 1.0) * inclusive for i in every]
        zq1 = [
            dot(queries[i], w1_ref[h]) + b1f[h : h + 1] - dot(low(p1[i] * er[i]), d1_ref[h])
            for i, h in enumerate(rng)
        ]
        parts = [gelu_parts(x) for x in zq1]
        aq = [low(x[0]) for x in parts]
        p2 = [(dot(aq[i], key_act[i], 1, 1) + 1.0) * inclusive for i in every]
        zq2 = [
            dot(aq[i], w2t_ref[h], 1, 1)
            + b2f[h : h + 1]
            - dot(low(p2[i] * er[i]), d2_ref[h])
            for i, h in enumerate(rng)
        ]
        c = [z - mean_last(z) for z in zq2]
        s = [lax.rsqrt(mean_last(x * x) + EPSILON) for x in c]
        n = [c[i] * s[i] for i in every]
        for i, h in enumerate(rng):
            p1_ref[h] = low(p1[i])
            p2_ref[h] = low(p2[i])
            act_ref[h, 0:length] = aq[i]
            slopeq_ref[h] = low(parts[i][1])
            nq_ref[h] = low(n[i])
            sq_ref[:, h : h + 1] = s[i]
            out_s[:, h * head : (h + 1) * head] = (
                q_s[h] + igf[h : h + 1] * n[i] + ibf[h : h + 1]
            )
    save(9, 16, 17, 18, 19, 20)
    inner_out = out_s[...]
    copies[3].wait()
    gate, slope, _ = gelu_parts(dot(normed, weights_s[3]))
    gelu_ref[...] = gate
    slope_ref[...] = inner_out * slope
    gated = low(inner_out * gate)
    pair_ref[1] = gated
    copies[4].wait()
    resid = tok + dot(gated, weights_s[4])
    resid_ref[...] = resid
    spread_two = lax.rsqrt(mean_last(resid * resid) + EPSILON)
    normed_two_ref[...] = low(resid * spread_two * row_of(gain2_ref))
    save(0, 1, 2)
    for copy in saves.values():
        copy.wait()
    for b in range(blocks):
        pltpu.make_async_copy(w2s_ref.at[b], outs[15].at[b], state_sems.at[b]).wait()


def ffn_kernel(x_ref, c_ref, wg_ref, wu_ref, wd_ref, act_ref, gg_ref, gu_ref, gx_ref):
    x = x_ref[...]
    gate = dot(x, wg_ref[...])
    up = dot(x, wu_ref[...])
    grad_act = dot(c_ref[...], wd_ref[...], 1, 1)
    sigma = jax.nn.sigmoid(gate)
    silu = gate * sigma
    act_ref[...] = low(silu * up)
    gg = low(grad_act * up * sigma * (1.0 + gate * (1.0 - sigma)))
    gu = low(grad_act * silu)
    gg_ref[...] = gg
    gu_ref[...] = gu
    gx_ref[...] = low(dot(gg, wg_ref[...], 1, 1) + dot(gu, wu_ref[...], 1, 1))


def ffn_weights_kernel(parts, ids_smem, *refs):
    x_refs, c_refs, act_refs, gg_refs, gu_refs = (
        refs[i * parts : (i + 1) * parts] for i in range(5)
    )
    wd_ref, kept_ref, sent_ref = refs[5 * parts : 5 * parts + 3]
    out_refs = refs[5 * parts + 3 : 6 * parts + 3]
    x_s, c_s, act_s, gg_s, gu_s = refs[6 * parts + 3 :]
    rows = x_refs[0].shape[0]
    for i in range(parts):
        at = slice(i * rows, (i + 1) * rows)
        x_s[at] = x_refs[i][...]
        c_s[at] = c_refs[i][...]
        act_s[at] = act_refs[i][...]
        gg_s[at] = gg_refs[i][...]
        gu_s[at] = gu_refs[i][...]
        out_refs[i][...] = low(dot(act_refs[i][...], wd_ref[...]))
    half = kept_ref.shape[2]
    core = ids_smem[0]
    for i, (left, right) in enumerate(((x_s, gg_s), (x_s, gu_s), (c_s, act_s))):
        whole = low(dot(left[...], right[...], 0, 0))

        @pl.when(core == 0)
        def _(whole=whole, i=i):
            kept_ref[i] = whole[:, 0:half]
            sent_ref[i] = whole[:, half:]

        @pl.when(core != 0)
        def _(whole=whole, i=i):
            kept_ref[i] = whole[:, half:]
            sent_ref[i] = whole[:, 0:half]


def between_kernel(parts, *refs):
    pieces = refs[0:parts]
    resid_ref, cot_ref, gain2_ref, wo_ref, gelu_ref, slope_ref = refs[parts : parts + 6]
    resid_grad_ref, go_ref, pair_ref, gain_grad_ref = refs[parts + 6 :]
    grad = pieces[0][...].astype(F32)
    for piece in pieces[1:]:
        grad = grad + piece[...].astype(F32)
    resid = resid_ref[...]
    spread = lax.rsqrt(mean_last(resid * resid) + EPSILON)
    scaled = row_of(gain2_ref) * grad
    grad_resid = (
        cot_ref[0].astype(F32)
        + spread * scaled
        - resid * (spread * spread * spread * mean_last(scaled * resid))
    )
    gain_grad_ref[...] = sum_rows(grad * resid * spread)
    resid_grad_ref[...] = grad_resid
    grad_branch = low(grad_resid)
    grad_gated = dot(grad_branch, wo_ref[...], 1, 1)
    go_ref[...] = grad_gated * gelu_ref[...]
    pair_ref[0] = low(grad_gated * slope_ref[...])
    pair_ref[1] = grad_branch


def backward_kernel(
    ids_smem,
    seg_smem,
    seg_ref,
    go_ref,
    qk_ref,
    ecol_ref,
    erow_ref,
    fcol_ref,
    w1_ref,
    w2t_ref,
    ig_ref,
    slope1_ref,
    curve1_ref,
    act_ref,
    d1_ref,
    d2_ref,
    n_ref,
    s_ref,
    fit_ref,
    w2s_ref,
    p1_ref,
    p2_ref,
    slopeq_ref,
    nq_ref,
    sq_ref,
    triple_ref,
    gr_ref,
    kept_ref,
    sent_ref,
    small_ref,
    igf,
    t1_s,
    t2_s,
    ga_s,
    hh1_s,
    hh2_s,
    u_s,
    share_s,
    ge_s,
    mix_s,
    gw2_s,
    gb2_s,
):
    length = go_ref.shape[0]
    heads, head, inner = w1_ref.shape
    blocks = length // MB
    top, bottom = slice(0, length), slice(length, 2 * length)
    igf[...] = ig_ref[...].astype(F32)
    inclusive, strict = segment_masks(seg_ref[...].astype(F32))
    for first in range(0, heads, BACKWARD_HEADS):
        rng = range(first, first + BACKWARD_HEADS)
        every = range(BACKWARD_HEADS)
        g = [igf[h : h + 1] for h in rng]
        weigh = [inclusive * erow_ref[h : h + 1, :] for h in rng]
        n = [nq_ref[h].astype(F32) for h in rng]
        x = [go_ref[:, h * head : (h + 1) * head] * igf[h : h + 1] for h in rng]
        mx = [mean_last(x[i]) for i in every]
        mxn = [mean_last(x[i] * n[i]) for i in every]
        hq2 = [
            low(sq_ref[:, h : h + 1] * (x[i] - mx[i] - n[i] * mxn[i]))
            for i, h in enumerate(rng)
        ]
        aq = [act_ref[h, top] for h in rng]
        ak = [act_ref[h, bottom] for h in rng]
        t2 = [dot(p2_ref[h], hq2[i], 0, 0) for i, h in enumerate(rng)]
        mix = [
            low(-dot(hq2[i], d2_ref[h], 1, 1) * weigh[i]) for i, h in enumerate(rng)
        ]
        gaq = [dot(hq2[i], w2t_ref[h]) + dot(mix[i], ak[i]) for i, h in enumerate(rng)]
        ga = [dot(mix[i], aq[i], 0, 0) for i in every]
        hq1 = [low(gaq[i] * slopeq_ref[h].astype(F32)) for i, h in enumerate(rng)]
        t1 = [dot(p1_ref[h], hq1[i], 0, 0) for i, h in enumerate(rng)]
        for i, h in enumerate(rng):
            hh2_s[h, top] = hq2[i]
            t2_s[h] = t2[i]
            ga_s[h] = ga[i]
            hh1_s[h, top] = hq1[i]
            t1_s[h] = t1[i]
    ge_s[...] = jnp.zeros(ge_s.shape, F32)
    earlier = jnp.transpose(strict)
    for h in range(heads):
        keys = qk_ref[h, bottom]
        mix_s[h] = low((dot(keys, keys, 1, 1) + 1.0) * earlier)
    hh1_s[:, bottom, :] = jnp.zeros(hh1_s[:, bottom, :].shape, BF16)

    def step(i, carry):
        b = blocks - 1 - i
        here = pl.multiple_of(b * MB, MB)
        after = jnp.minimum(here + MB, length - 1)
        fresh = (i == 0) | (seg_smem[0, after] != seg_smem[0, after - 1])

        ds = pl.ds(here, MB)
        ds_low = pl.ds(length + here, MB)
        rng = range(heads)
        act = [act_ref[h, ds_low, :] for h in rng]
        e = [ecol_ref[ds, h : h + 1] for h in rng]
        w2 = [w2s_ref[b, h] for h in rng]
        gw2 = [jnp.where(fresh, 0.0, gw2_s[h]) for h in rng]
        gw2b = [low(x) for x in gw2]
        gb2 = [jnp.where(fresh, 0.0, gb2_s[h]) for h in rng]
        d1 = [d1_ref[h, ds, :].astype(F32) for h in rng]
        d2 = [d2_ref[h, ds, :].astype(F32) for h in rng]
        n = [n_ref[h, ds, :].astype(F32) for h in rng]
        s = [s_ref[ds, h : h + 1] for h in rng]
        fit = [fit_ref[h, ds, :].astype(F32) for h in rng]
        slope = [slope1_ref[h, ds, :].astype(F32) for h in rng]
        curve = [curve1_ref[h, ds, :].astype(F32) for h in rng]
        g = [igf[h : h + 1] for h in rng]
        share = [g[h] * fit[h] for h in rng]
        t1 = [t1_s[h, ds, :] + dot(mix_s[h, ds, :], hh1_s[h, bottom]) for h in rng]
        t2 = [t2_s[h, ds, :] + dot(act[h], gw2b[h], 1, 1) + gb2[h] for h in rng]
        g1 = [-e[h] * t1[h] for h in rng]
        u = [low(g1[h] * slope[h]) for h in rng]
        ed2 = [low(-e[h] * d2[h]) for h in rng]
        ga = [ga_s[h, ds, :] + dot(ed2[h], gw2b[h]) for h in rng]
        g2 = [dot(u[h], w2[h], 1, 1) - e[h] * t2[h] for h in rng]
        y = [s[h] * g2[h] for h in rng]
        my = [mean_last(y[h]) for h in rng]
        myn = [mean_last(y[h] * n[h]) for h in rng]
        msn = [mean_last(share[h] * n[h]) for h in rng]
        mgd = [mean_last(g2[h] * d2[h]) for h in rng]
        gshare = [y[h] - my[h] - n[h] * myn[h] for h in rng]
        gn = [g[h] * (g[h] * gshare[h]) - y[h] * msn[h] - share[h] * myn[h] for h in rng]
        mn = [mean_last(gn[h]) for h in rng]
        mnn = [mean_last(gn[h] * n[h]) for h in rng]
        h2 = [
            low(s[h] * (gn[h] - mn[h] - n[h] * (mnn[h] + mgd[h]))) for h in rng
        ]
        ga = [ga[h] + dot(h2[h], w2[h]) for h in rng]
        h1f = [ga[h] * slope[h] + g1[h] * curve[h] for h in rng]
        h1 = [low(x) for x in h1f]
        up2 = [
            dot(low(d2[h]), u[h], 0, 0) + dot(h2[h], act[h], 0, 0) for h in rng
        ]
        for h in rng:
            w2n = gw2[h] + up2[h]
            gw2_s[h] = w2n
            gb2_s[h] = gb2[h] + sum_rows(h2[h].astype(F32))
            u_s[h, ds, :] = u[h]
            hh1_s[h, ds_low, :] = h1[h]
            hh2_s[h, ds_low, :] = h2[h]
            share_s[h, ds, :] = gshare[h]
            ge_s[ds, h : h + 1] = -jnp.sum(d1[h] * t1[h], -1, keepdims=True) - jnp.sum(
                d2[h] * t2[h], -1, keepdims=True
            )
        return carry

    lax.fori_loop(0, blocks, step, 0, unroll=4)
    small_ref[...] = jnp.zeros(small_ref.shape, F32)
    core = ids_smem[0]
    pad = small_ref.shape[0] // 2
    for start in range(0, heads, BACKWARD_HEADS):
        rng = range(start, start + BACKWARD_HEADS)
        every = range(BACKWARD_HEADS)
        cols = [slice(h * head, (h + 1) * head) for h in rng]
        g = [igf[h : h + 1] for h in rng]
        er = [erow_ref[h : h + 1, :] for h in rng]
        hh1 = [hh1_s[h] for h in rng]
        hh2 = [hh2_s[h] for h in rng]
        qk = [qk_ref[h] for h in rng]
        keys = [qk_ref[h, bottom] for h in rng]
        share = [share_s[h] for h in rng]
        go = [go_ref[:, cols[i]] for i in every]
        both = [dot(hh1[i], d1_ref[h], 1, 1) for i, h in enumerate(rng)]
        direct = [dot(hh1[i], w1_ref[h], 1, 1) for i, h in enumerate(rng)]
        mixq = [low(-both[i][top] * (inclusive * er[i])) for i in every]
        mixk = [low(-both[i][bottom] * (strict * er[i])) for i in every]
        first = [low(dot(qk[i], hh1[i], 0, 0)) for i in every]
        second = [
            low(dot(hh2[i], act_ref[h], 0, 0) + dot(d2_ref[h], u_s[h], 0, 0))
            for i, h in enumerate(rng)
        ]
        gq = [low(go[i] + direct[i][top] + dot(mixq[i], keys[i])) for i in every]
        spread = [
            dot(mixq[i], qk_ref[h, top], 0, 0) + dot(mixk[i], keys[i], 0, 0)
            for i, h in enumerate(rng)
        ]
        gk = [
            low(g[i] * share[i] + direct[i][bottom] + dot(mixk[i], keys[i]) + spread[i])
            for i in every
        ]
        for i, h in enumerate(rng):
            triple_ref[0, :, cols[i]] = gq[i]
            triple_ref[1, :, cols[i]] = gk[i]
            triple_ref[2, :, cols[i]] = low(-g[i] * share[i])
            kept_ref[cols[i]] = jnp.where(core == 0, first[i], second[i])
            sent_ref[cols[i]] = jnp.where(core == 0, second[i], first[i])
            small_ref[h : h + 1] = sum_rows(hh1[i].astype(F32))
            row = slice(pad + h, pad + h + 1)
            small_ref[row, 0:head] = sum_rows(hh2[i].astype(F32))
            small_ref[row, head : 2 * head] = sum_rows(
                go[i] * nq_ref[h].astype(F32)
                + share[i] * (fit_ref[h].astype(F32) + g[i] * n_ref[h].astype(F32))
            )
            small_ref[row, 2 * head : 3 * head] = sum_rows(go[i]) + g[i] * sum_rows(share[i])
    grad_rates = ge_s[...] * fcol_ref[...]
    gr_ref[...] = low(grad_rates)
    total = jnp.broadcast_to(sum_rows(grad_rates), (grad_rates.shape[1], grad_rates.shape[1]))
    small_ref[pad : pad + heads, 3 * head : 3 * head + 1] = jnp.transpose(total)[0:heads, 0:1]


def put_matrix(to_ref, values, index, count, feats):
    chips = to_ref.shape[0]
    rows = values.shape[0] // (feats * chips)
    chunks = values.shape[1] // 128
    for f in range(feats):
        for l in range(chunks):
            row = ((f * count + index) * chunks + l) * rows
            for j in range(chips):
                at = (f * chips + j) * rows
                to_ref[j, row : row + rows, :] = values[at : at + rows, l * 128 : (l + 1) * 128]


def core_columns(core, values):
    half = values.shape[1] // 2
    return jnp.where(core == 0, values[:, 0:half], values[:, half:])


def put_halves(ids_smem, kept_ref, sent_ref, put):
    core, chip = ids_smem[0], ids_smem[1]
    first, second = 1 + core, 2 - core
    put(kept_ref.at[0], chip)
    put(kept_ref.at[1], lax.bitwise_xor(chip, second))
    put(sent_ref.at[0], lax.bitwise_xor(chip, first))
    put(sent_ref.at[1], lax.bitwise_xor(chip, 3))


def gate_weights_kernel(
    feats,
    ids_smem,
    mine_ref,
    other_ref,
    grads_ref,
    other_grads_ref,
    wg_ref,
    kept_ref,
    got_ref,
    part_ref,
    kept_out,
    sent_out,
    pieces_s,
    left_s,
    right_s,
):
    core = ids_smem[0]
    length = mine_ref.shape[1]
    for i in range(2):
        left_s[i, 0:length] = mine_ref[i]
        left_s[i, length : 2 * length] = other_ref[i]
        right_s[i, 0:length] = core_columns(core, grads_ref[i])
        right_s[i, length : 2 * length] = core_columns(core, other_grads_ref[i])
    for i in range(2):
        put_matrix(pieces_s, low(dot(left_s[i], right_s[i], 0, 0)), i, 2, feats)
    count, _, half = kept_ref.shape
    chunks = half // 128
    before = kept_out.shape[1] - pieces_s.shape[1]
    rows = before // (count * chunks)

    def put(out, place):
        at = pl.ds(pl.multiple_of(place * rows, rows), rows)
        for i in range(count):
            both = low(kept_ref[i, at, :].astype(F32) + got_ref[i, at, :].astype(F32))
            for l in range(chunks):
                row = (i * chunks + l) * rows
                out[row : row + rows] = both[:, l * 128 : (l + 1) * 128]
        out[before:] = pieces_s[place]

    put_halves(ids_smem, kept_out, sent_out, put)
    part_ref[...] = dot(grads_ref[0], wg_ref[...], 1, 1)


def input_kernel(
    feats,
    triple_ref,
    gr_ref,
    pair_ref,
    wq_ref,
    wk_ref,
    wv_ref,
    wr_ref,
    part_ref,
    tok_ref,
    gain1_ref,
    resid_grad_ref,
    small_ref,
    gain_two_ref,
    grad_ref,
    small_out,
):
    heads = wr_ref.shape[0]
    grad = part_ref[...] + dot(triple_ref[0], wq_ref[...], 1, 1)
    grad = grad + dot(triple_ref[1], wk_ref[...], 1, 1) + dot(triple_ref[2], wv_ref[...], 1, 1)
    gr = gr_ref[...]
    grad = grad + dot(gr[:, 0:heads], wr_ref[...])
    tok = tok_ref[0].astype(F32)
    spread = lax.rsqrt(mean_last(tok * tok) + EPSILON)
    scaled = row_of(gain1_ref) * grad
    grad_ref[0] = (
        resid_grad_ref[...]
        + spread * scaled
        - tok * (spread * spread * spread * mean_last(scaled * tok))
    )
    rate_rows = dot(gr, pair_ref[0], 0, 0)
    gain_row = sum_rows(grad * tok * spread)
    small_out[...] = jnp.zeros(small_out.shape, BF16)
    share = tok.shape[1] // feats
    for f in range(feats):
        cols = slice(f * share, (f + 1) * share)
        small_out[f * 16 : f * 16 + 16, 0:share] = low(
            jnp.concatenate(
                [rate_rows[0:heads, cols], gain_row[:, cols], gain_two_ref[:, cols]]
                + [jnp.zeros((14 - heads, share), F32)],
                0,
            )
        )
    at = feats * 16
    small_out[at : at + small_ref.shape[0]] = low(small_ref[...])


def tails_kernel(ids_smem, kept_ref, got_ref, kept_out, sent_out, tails_s):
    chips = tails_s.shape[0]
    inner = low(kept_ref[...].astype(F32) + got_ref[...].astype(F32))
    rows = inner.shape[0] // chips
    for j in range(chips):
        for l in range(2):
            tails_s[j, l * rows : (l + 1) * rows] = inner[
                j * rows : (j + 1) * rows, l * 128 : (l + 1) * 128
            ]

    def put(out, place):
        out[...] = tails_s[place]

    put_halves(ids_smem, kept_out, sent_out, put)


def late_weights_kernel(
    feats,
    ids_smem,
    mine_ref,
    other_ref,
    triple_ref,
    other_triple_ref,
    small_ref,
    kept_out,
    sent_out,
    pieces_s,
    left_s,
    right_s,
):
    core = ids_smem[0]
    length = mine_ref.shape[1]
    left_s[0:length] = mine_ref[0]
    left_s[length : 2 * length] = other_ref[0]
    for i in range(3):
        right_s[i, 0:length] = core_columns(core, triple_ref[i])
        right_s[i, length : 2 * length] = core_columns(core, other_triple_ref[i])
    for i in range(3):
        put_matrix(pieces_s, low(dot(left_s[...], right_s[i], 0, 0)), i, 3, feats)
    chips, most, _ = pieces_s.shape
    extra = small_ref.shape[0] // chips
    for j in range(chips):
        for l in range(2):
            at = most - (2 - l) * extra
            pieces_s[j, at : at + extra] = small_ref[
                j * extra : (j + 1) * extra, l * 128 : (l + 1) * 128
            ]

    def put(out, place):
        out[...] = pieces_s[place]

    put_halves(ids_smem, kept_out, sent_out, put)


def mixed_kernel(feats, resid_ref, *refs):
    kept_ref, got_ref, mixed_ref, stay_ref, go_ref = refs[feats:]
    total = resid_ref[...]
    for ref in refs[0:feats]:
        total = total + ref[...].astype(F32)
    mixed_ref[0] = low(total)
    add_kernel(kept_ref, got_ref, stay_ref, go_ref)


def add_kernel(kept_ref, got_ref, stay_ref, go_ref):
    stay_ref[...] = low(kept_ref[0].astype(F32) + got_ref[0].astype(F32))
    go_ref[...] = low(kept_ref[1].astype(F32) + got_ref[1].astype(F32))


def sum_at(refs, at):
    value = refs[0][at].astype(F32)
    for ref in refs[1:]:
        value = value + ref[at].astype(F32)
    return low(value)


def cut_feat_kernel(common, ids_smem, *refs):
    parts, outs = refs[0:2], refs[2:]
    rows = outs[0].shape[0] - common
    shared = sum_at(parts, (slice(rows * len(outs), rows * len(outs) + common), slice(None)))
    for s, out in enumerate(outs):
        at = pl.ds(pl.multiple_of(lax.bitwise_xor(ids_smem[2], s) * rows, 16), rows)
        out[0:rows] = sum_at(parts, (at, slice(None)))
        out[rows:] = shared


def sum_kernel(*refs):
    values = [ref[...].astype(F32) for ref in refs[:-1]]
    while len(values) > 1:
        values = [values[i] + values[i + 1] for i in range(0, len(values), 2)]
    refs[-1][...] = low(values[0])


def join_kernel(*refs):
    total_ref, out_ref = refs[-2:]
    rows = refs[0].shape[0]
    sum_kernel(*refs[:-2], out_ref.at[0:rows])
    out_ref[rows:] = total_ref[...]


def middle_kernel(ids_smem, *refs):
    pair, tail = refs[0:2], refs[2:4]
    total_ref, outs = refs[4], refs[5:]
    before = total_ref.shape[0]
    rows = (pair[0].shape[0] - before) // len(outs)
    shared = sum_at(tail, (slice(None), slice(None)))
    for s, out in enumerate(outs):
        at = pl.multiple_of(before + lax.bitwise_xor(ids_smem[2], s) * rows, 16)
        out[0:rows] = sum_at(pair, (pl.ds(at, rows), slice(None)))
        out[rows:] = shared
    total_ref[...] = sum_at(pair, (slice(0, before), slice(None)))


def take_matrices(ids_smem, pieces, outs, start=0, order=None):
    core, chip = ids_smem[0], ids_smem[1]
    chunks = outs[0].shape[1] // 256
    rows = outs[0].shape[0] // len(pieces)
    for s, both in enumerate(pieces):
        ats = [
            pl.ds(pl.multiple_of(lax.bitwise_xor(chip, d) * rows, 16), rows)
            for d in (order[s] if order else (s, s))
        ]
        for i, out in enumerate(outs):
            for l in range(chunks):
                row = start + (i * chunks + l) * rows
                mine = both[0][row : row + rows, :].astype(F32)
                other = both[1][row : row + rows, :].astype(F32)
                low_cols = slice(l * 128, (l + 1) * 128)
                high_cols = slice((chunks + l) * 128, (chunks + l + 1) * 128)

                @pl.when(core == 0)
                def _(out=out, ats=ats, mine=mine, other=other, a=low_cols, b=high_cols):
                    out[ats[0], a] = mine
                    out[ats[1], b] = other

                @pl.when(core != 0)
                def _(out=out, ats=ats, mine=mine, other=other, a=low_cols, b=high_cols):
                    out[ats[0], b] = mine
                    out[ats[1], a] = other


def early_totals_kernel(ids_smem, *refs):
    core, chip = ids_smem[0], ids_smem[1]
    first, second = 1 + core, 2 - core
    pieces = [(refs[s], refs[4 + s]) for s in range(4)]
    order = [(0, 0), (second, first), (first, second), (3, 3)]
    outs, kept, down_s, sems = refs[8:15], refs[15:22], refs[22], refs[23]
    gate_ref, up_ref, down_ref, wg_ref, wo_ref, first_ref, second_ref = kept
    saves = [pltpu.make_async_copy(kept[i], outs[i], sems.at[i]) for i in range(7)]
    rows = first_ref.shape[0] // 4
    start = 2 * (wg_ref.shape[0] // 4) * (wg_ref.shape[1] // 256)
    take_matrices(ids_smem, pieces, (gate_ref, up_ref, down_s), start + 2 * rows, order)
    saves[0].start()
    saves[1].start()
    down_ref[...] = jnp.transpose(down_s[...])
    saves[2].start()
    for s, both in enumerate(pieces):
        ats = [
            pl.ds(pl.multiple_of(lax.bitwise_xor(chip, d) * rows, 16), rows) for d in order[s]
        ]
        for l in range(2):
            cols = slice(l * 128, (l + 1) * 128)
            row = start + l * rows
            mine = both[0][row : row + rows].astype(F32)
            other = both[1][row : row + rows].astype(F32)

            @pl.when(core == 0)
            def _(ats=ats, cols=cols, mine=mine, other=other):
                first_ref[ats[0], cols] = mine
                second_ref[ats[1], cols] = other

            @pl.when(core != 0)
            def _(ats=ats, cols=cols, mine=mine, other=other):
                first_ref[ats[1], cols] = other
                second_ref[ats[0], cols] = mine

    saves[5].start()
    saves[6].start()
    take_matrices(ids_smem, pieces, (wg_ref, wo_ref), order=order)
    saves[3].start()
    saves[4].start()
    for copy in saves:
        copy.wait()


def late_totals_kernel(chips, feats, heads, head, ids_smem, *refs):
    pieces = [(refs[s], refs[chips + s]) for s in range(chips)]
    matrices = refs[2 * chips : 2 * chips + 3]
    (rate_ref, norm1_ref, norm2_ref, b1_ref, b2_ref, ig_ref, ib_ref, br_ref, small_s) = refs[
        2 * chips + 3 :
    ]
    chip, feat = ids_smem[1], ids_smem[2]
    take_matrices(ids_smem, pieces, matrices)
    extra = small_s.shape[0] // chips
    most = refs[0].shape[0]
    for s, both in enumerate(pieces):
        at = pl.ds(pl.multiple_of(lax.bitwise_xor(chip, s) * extra, 16), extra)
        for l in range(2):
            row = most - (2 - l) * extra
            small_s[at, l * 128 : (l + 1) * 128] = both[0][row : row + extra].astype(
                F32
            ) + both[1][row : row + extra].astype(F32)
    share = rate_ref.shape[1]
    block = small_s[pl.ds(pl.multiple_of(feat * 16, 16), 16), :]
    rate_ref[...] = block[0:heads, 0:share]
    norm1_ref[...] = block[heads : heads + 1, 0:share]
    norm2_ref[...] = block[heads + 1 : heads + 2, 0:share]
    at = feats * 16
    b1_ref[...] = small_s[at : at + heads, :]
    packed = small_s[at + 16 : at + 16 + heads, :]
    b2_ref[...] = packed[:, 0:head]
    ig_ref[...] = packed[:, head : 2 * head]
    ib_ref[...] = packed[:, 2 * head : 3 * head]
    br_ref[...] = jnp.transpose(small_s[at + 16 : at + 32, 128:])[3 * head - 128 : 3 * head - 127, 0:heads]


def held(values):
    return pltpu.with_memory_space_constraint(values, pltpu.VMEM)


def in_order():
    last = []

    def ordered(kernel, outs, inputs, scratch=(), **options):
        inputs = list(inputs)
        at = options.get("smem", 0)
        if last:
            inputs[at], _ = lax.optimization_barrier((inputs[at], last.pop()))
        found = call(kernel, outs, inputs, scratch, **options)
        last.append(found[0])
        return found

    return ordered


def call(
    kernel, outs, inputs, scratch=(), smem=0, cover=1, plain=(), loose=(), keep=True, mib=24
):
    specs, placed = [], []
    for i, x in enumerate(inputs):
        if i < smem:
            specs.append(pl.BlockSpec(memory_space=pltpu.SMEM))
            placed.append(x)
        elif i in loose:
            specs.append(pl.BlockSpec(memory_space=pltpu.HBM))
            placed.append(pltpu.with_memory_space_constraint(x, pltpu.HBM))
        elif i in plain:
            specs.append(pl.BlockSpec(memory_space=pltpu.VMEM))
            placed.append(pltpu.with_memory_space_constraint(x, pltpu.HBM))
        else:
            specs.append(pl.BlockSpec(memory_space=pltpu.VMEM))
            placed.append(held(x))
    kept = [keep] * len(outs) if isinstance(keep, bool) else list(keep)
    return pl.pallas_call(
        kernel,
        out_shape=[
            pltpu.VMEM(s, d) if k else pltpu.HBM(s, d) for (s, d), k in zip(outs, kept)
        ],
        in_specs=specs,
        out_specs=[
            pl.BlockSpec(memory_space=pltpu.HBM if k is None else pltpu.VMEM) for k in kept
        ],
        scratch_shapes=[pltpu.VMEM(*x) if isinstance(x, tuple) else x for x in scratch],
        cost_estimate=pl.CostEstimate(
            flops=int(2e10 * cover + 1e6), bytes_accessed=int(2e7 * cover + 1e3), transcendentals=0
        ),
        compiler_params=pltpu.CompilerParams(vmem_limit_bytes=mib * 2**20),
    )(*placed)


def exchange(values, axis, size, distance):
    return lax.ppermute(values, axis, [(i, i ^ distance) for i in range(size)])


def add_low(left, right):
    return low(left.astype(F32) + right.astype(F32))


def halve(values, axis, size, distance, dim):
    side = lax.bitwise_and(lax.axis_index(axis) // distance, 1)
    half = values.shape[dim] // 2
    kept = lax.dynamic_slice_in_dim(values, side * half, half, dim)
    sent = lax.dynamic_slice_in_dim(values, (1 - side) * half, half, dim)
    return add_low(kept, exchange(sent, axis, size, distance))


def double(values, axis, size, distance, dim):
    side = lax.bitwise_and(lax.axis_index(axis) // distance, 1)
    other = exchange(values, axis, size, distance)
    return jnp.where(
        side == 0,
        jnp.concatenate([values, other], dim),
        jnp.concatenate([other, values], dim),
    )


def distances(size):
    found = []
    step = 1
    while step < size:
        found.append(step)
        step *= 2
    return found


def across_chips(values, rows):
    return [values[0]] + [
        exchange(values[s], "rows", rows, 2 * s) for s in range(1, len(values))
    ]


def across_feats(values, feats):
    return [values[0]] + [exchange(values[s], "feat", feats, s) for s in range(1, feats)]


def first_axis(values, rows):
    return lax.ppermute(values, "rows", [(i, i ^ (2 << (i & 1))) for i in range(rows)])


def second_axis(values, rows):
    return lax.ppermute(values, "rows", [(i, i ^ (4 >> (i & 1))) for i in range(rows)])


def halved(launch, kept, got, rows, cover):
    stay, go = launch(add_kernel, [(kept.shape[1:], BF16)] * 2, [kept, got], cover=cover)
    return stay, second_axis(go, rows)


def other_core(values, rows):
    return exchange(values, "rows", rows, 1)


def scatter_rows(values, size, dim):
    for d in distances(size):
        values = halve(values, "rows", size, d, dim)
    return values


def gather_rows(values, size, dim):
    for d in reversed(distances(size)):
        values = double(values, "rows", size, d, dim)
    return values


def scatter_feat(values, size, dim):
    me = lax.axis_index("feat")
    total = lax.dynamic_index_in_dim(values, me, dim, keepdims=False).astype(F32)
    for s in range(1, size):
        piece = lax.dynamic_index_in_dim(values, lax.bitwise_xor(me, s), dim, keepdims=False)
        total = total + exchange(piece, "feat", size, s).astype(F32)
    return low(total)


def on_device(
    rows,
    feats,
    tokens,
    cotangent,
    seg_ids,
    pad_mask,
    norm1_gain,
    w_query,
    w_key,
    w_value,
    w_gate,
    w_rate,
    b_rate,
    inner_w1,
    inner_b1,
    inner_w2,
    inner_b2,
    inner_gain,
    inner_bias,
    w_out,
    norm2_gain,
    ffn_gate,
    ffn_up,
    ffn_down,
):
    launch = in_order()
    _, length, width = tokens.shape
    heads, head, inner = inner_w1.shape
    hidden = ffn_gate.shape[1]
    blocks = length // MB
    chips = rows // 2
    line = (length, width)
    wide = (heads, length, inner)
    slim = (heads, length, head)
    square = (heads, length, length)
    state = (heads, head, inner)
    w2t = jnp.transpose(inner_w2, (0, 2, 1))
    w_rate_t = jnp.transpose(w_rate)
    place = lax.axis_index("rows")
    me = lax.axis_index("feat")
    ids = jnp.stack([lax.bitwise_and(place, 1), lax.shift_right_logical(place, 1), me])
    cots = across_feats([cotangent[0]] * feats, feats)
    kept = [
        (line, F32),
        (line, F32),
        (line, F32),
        ((heads, 2 * length, head), BF16),
        ((length, 128), F32),
        ((16, length), F32),
        ((length, 128), F32),
        (wide, BF16),
        (wide, BF16),
        ((heads, 2 * length, inner), BF16),
        (wide, BF16),
        (slim, BF16),
        (slim, BF16),
        ((length, 128), F32),
        (slim, BF16),
        ((blocks,) + state, BF16),
        (square, BF16),
        (square, BF16),
        (wide, BF16),
        (slim, BF16),
        ((length, 128), F32),
    ]
    saved = launch(
        forward_kernel,
        [((2,) + line, BF16), (line, BF16)] + kept,
        [
            seg_ids,
            seg_ids,
            pad_mask,
            tokens,
            norm1_gain,
            w_query,
            w_key,
            w_value,
            w_gate,
            w_rate_t,
            b_rate[None],
            inner_w1,
            inner_b1,
            w2t,
            inner_b2,
            inner_gain,
            inner_bias,
            w_out,
            norm2_gain,
        ],
        kept
        + [
            (slim, F32),
            (slim, F32),
            (slim, F32),
            (line, F32),
            (wide, F32),
            (square, BF16),
            (state, F32),
            ((heads, 1, head), F32),
            ((heads, inner), F32),
            ((heads, head), F32),
            ((heads, head), F32),
            ((heads, head), F32),
            ((5, width, width), BF16),
            pltpu.SemaphoreType.DMA((5 + len(kept),)),
            pltpu.SemaphoreType.DMA((blocks,)),
        ],
        smem=1,
        plain=range(19),
        loose=(5, 6, 7, 8, 17),
        keep=[True, True] + [None] * len(kept),
        mib=48,
    )
    pair, normed_two, resid, gelu_gate, gate_slope = saved[0:5]
    qk, ecol, erow, fcol = saved[5:9]
    rest = saved[9:]
    normed_two, *cots = lax.optimization_barrier([normed_two] + cots)
    blocks_in = [normed_two]
    acts, ggs, gus, pieces = [], [], [], []
    for s in range(1, feats):
        if s & (s - 1) == 0:
            blocks_in.append(exchange(normed_two, "feat", feats, s))
        else:
            blocks_in.append(None)
    for s in range(feats):
        if blocks_in[s] is None:
            nearest = s & -s
            held_back, _ = lax.optimization_barrier((blocks_in[s ^ nearest], pieces[1]))
            blocks_in[s] = exchange(held_back, "feat", feats, nearest)
        act, gg, gu, gx = launch(
            ffn_kernel,
            [((length, hidden), BF16)] * 3 + [(line, BF16)],
            [blocks_in[s], cots[s], ffn_gate, ffn_up, ffn_down],
        )
        acts.append(act)
        ggs.append(gg)
        gus.append(gu)
        pieces.append(gx)
    if feats > 2:
        pieces[1], _ = lax.optimization_barrier((pieces[1], acts[3]))
    pieces = across_feats(pieces, feats)

    def between(pieces):
        return launch(
            partial(between_kernel, feats),
            [(line, F32), (line, F32), ((2,) + line, BF16), ((1, width), F32)],
            pieces + [resid, cotangent, norm2_gain, w_out, gelu_gate, gate_slope],
        )

    def inner_backward(grad_inner_out):
        return launch(
            backward_kernel,
            [
                ((3,) + line, BF16),
                ((length, 128), BF16),
                ((heads * head, inner), BF16),
                ((heads * head, inner), BF16),
                ((32, inner), F32),
            ],
            [ids, seg_ids, seg_ids, grad_inner_out, qk, ecol, erow, fcol, inner_w1, w2t]
            + [inner_gain]
            + list(rest),
            [
                ((heads, head), F32),
                (wide, F32),
                (slim, F32),
                (wide, F32),
                ((heads, 2 * length, inner), BF16),
                ((heads, 2 * length, head), BF16),
                (wide, BF16),
                (slim, F32),
                ((length, 128), F32),
                (square, BF16),
                (state, F32),
                ((heads, 1, head), F32),
            ],
            smem=2,
        )

    step = 16 * chips
    small_rows = -(-(16 * feats + 32) // step) * step

    def finish(triple, grad_rates, small, part, grad_resid, grad_gain_two):
        return launch(
            partial(input_kernel, feats),
            [((1,) + line, F32), ((small_rows, inner), BF16)],
            [triple, grad_rates, pair, w_query, w_key, w_value, w_rate_t, part]
            + [tokens, norm1_gain, grad_resid, small, grad_gain_two],
            keep=(False, True),
            cover=0,
        )

    if chips != 4 or (width // feats) % step or hidden % 256 or width % 256:
        grad_resid, grad_inner_out, grad_pair, grad_gain_two = between(pieces)
        out, grads = plain_totals(
            rows, feats, blocks_in, cots, acts, ggs, gus, ffn_down, pair, grad_pair, w_gate
        )
        triple, grad_rates, kept, sent, small = inner_backward(grad_inner_out)
        out = across_feats(out, feats)
        mixed = low(resid + sum(x.astype(F32) for x in out))[None]
        grad_tokens, small = finish(
            triple, grad_rates, small, grads.pop(), grad_resid, grad_gain_two
        )
        late = plain_late_totals(rows, feats, pair, triple, kept, sent, small, state)
        return arrange(mixed, grad_tokens, grads, late, state)
    ffn = launch(
        partial(ffn_weights_kernel, feats),
        [((3, width, hidden // 2), BF16)] * 2 + [(line, BF16)] * feats,
        [ids] + blocks_in + cots + acts + ggs + gus + [ffn_down],
        [((feats * length, width), BF16)] * 2 + [((feats * length, hidden), BF16)] * 3,
        smem=1,
    )
    grad_resid, grad_inner_out, grad_pair, grad_gain_two = between(pieces)
    ffn_sent, _ = lax.optimization_barrier((ffn[1], grad_pair))
    pair_other = other_core(pair, rows)
    half = width // 2
    per = width // (feats * chips) * (half // 128)
    ffn_rows = 3 * (width // chips) * (hidden // 256)
    part, early, early_sent = launch(
        partial(gate_weights_kernel, feats),
        [(line, F32)] + [((2, ffn_rows + feats * 2 * per, 128), BF16)] * 2,
        [ids, pair, pair_other, grad_pair, other_core(grad_pair, rows), w_gate]
        + [ffn[0], other_core(ffn_sent, rows)],
        [
            ((chips, feats * 2 * per, 128), BF16),
            ((2, 2 * length, width), BF16),
            ((2, 2 * length, half), BF16),
        ],
        smem=1,
    )
    early_got = first_axis(early_sent, rows)
    out, _ = lax.optimization_barrier((ffn[2:], part))
    out = across_feats(out, feats)
    triple, grad_rates, kept, sent, small = inner_backward(grad_inner_out)
    triple_other = other_core(triple, rows)
    inner_got = other_core(sent, rows)
    mixed, early, early_sent = launch(
        partial(mixed_kernel, feats),
        [((1,) + line, BF16)] + [(early.shape[1:], BF16)] * 2,
        [resid] + out + [early, early_got],
        keep=(False, True, True),
    )
    tail = 2 * heads * head // chips
    tails, tails_sent = launch(
        tails_kernel,
        [((2, tail, 128), BF16)] * 2,
        [ids, kept, inner_got],
        [((chips, tail, 128), BF16)],
        smem=1,
        cover=0,
    )
    tails_got = first_axis(tails_sent, rows)
    early_sent, _ = lax.optimization_barrier((early_sent, tails_sent))
    early_got = second_axis(early_sent, rows)
    grad_tokens, small = finish(triple, grad_rates, small, part, grad_resid, grad_gain_two)
    tails, tails_got = halved(launch, tails, tails_got, rows, 0)
    common = 2 * small_rows // chips
    late, late_sent = launch(
        partial(late_weights_kernel, feats),
        [((2, feats * 3 * per + common, 128), BF16)] * 2,
        [ids, pair, pair_other, triple, triple_other, small],
        [
            ((chips, feats * 3 * per + common, 128), BF16),
            ((2 * length, width), BF16),
            ((3, 2 * length, half), BF16),
        ],
        smem=1,
        cover=2,
    )
    late_got = first_axis(late_sent, rows)
    ffn_total, *cut = launch(
        middle_kernel,
        [((ffn_rows, 128), BF16)] + [((2 * per + tail, 128), BF16)] * feats,
        [ids, early, early_got, tails, tails_got],
        smem=1,
    )
    cut = across_feats(cut, feats)
    late, late_got = halved(launch, late, late_got, rows, 1)
    (joined,) = launch(
        join_kernel, [((2 * per + tail + ffn_rows, 128), BF16)], cut + [ffn_total]
    )
    late_cut = launch(
        partial(cut_feat_kernel, common),
        [((3 * per + common, 128), BF16)] * feats,
        [ids, late, late_got],
        smem=1,
        cover=0,
    )
    joined, late_cut = lax.optimization_barrier((joined, late_cut))
    late_cut = across_feats(late_cut, feats)
    near = second_axis(joined, rows)
    joined = [joined, near, first_axis(joined, rows), first_axis(near, rows)]
    (late_total,) = launch(sum_kernel, [((3 * per + common, 128), BF16)], late_cut)
    late = across_chips([late_total] * chips, rows)
    late += [other_core(x, rows) for x in late]
    joined += [other_core(x, rows) for x in joined]
    share = (width // feats, width)
    late = launch(
        partial(late_totals_kernel, chips, feats, heads, head),
        [(share, F32)] * 3
        + [((heads, width // feats), F32)]
        + [((1, width // feats), F32)] * 2
        + [((heads, inner), F32)]
        + [((heads, head), F32)] * 3
        + [((1, heads), F32)],
        [ids] + late,
        [((small_rows, inner), F32)],
        smem=1,
        keep=False,
    )
    kept = (
        [((width, hidden), F32)] * 2
        + [((hidden, width), F32)]
        + [(share, F32)] * 2
        + [((heads * head, inner), F32)] * 2
    )
    early = launch(
        early_totals_kernel,
        kept,
        [ids] + joined,
        kept + [((width, hidden), F32), pltpu.SemaphoreType.DMA((len(kept),))],
        smem=1,
        keep=[None] * len(kept),
    )
    early, late = list(early), list(late)
    return arrange(mixed, grad_tokens, early[0:5], late[0:3] + early[5:7] + late[3:], state)


def arrange(mixed, grad_tokens, early, late, state):
    return (
        mixed,
        grad_tokens,
        late[6][0],
        late[0],
        late[1],
        late[2],
        early[3],
        jnp.transpose(late[5]),
        late[12][0],
        late[3].reshape(state),
        late[8],
        jnp.transpose(late[4].reshape(state), (0, 2, 1)),
        late[9],
        late[10],
        late[11],
        early[4],
        late[7][0],
        early[0],
        early[1],
        early[2],
    )


def contract(left, right):
    return low(dot(left, right, 0, 0))


def plain_features(values, rows, feats):
    width = values.shape[0]
    values = values.reshape((feats, width // feats, width))
    values = scatter_feat(scatter_rows(values, rows, 1), feats, 0)
    return gather_rows(values, rows, 0).astype(F32)


def plain_totals(
    rows, feats, blocks_in, cots, acts, ggs, gus, ffn_down, pair, grad_pair, w_gate
):
    def joined(parts):
        return jnp.concatenate(parts, 0)

    def over_rows(values):
        return gather_rows(scatter_rows(values, rows, 0), rows, 0).astype(F32)

    x, c, act = joined(blocks_in), joined(cots), joined(acts)
    out = [low(dot(a, ffn_down)) for a in acts]
    grads = [contract(x, joined(ggs)), contract(x, joined(gus)), contract(act, c)]
    grads = [over_rows(g) for g in grads]
    for i in range(2):
        grads.append(plain_features(contract(pair[i], grad_pair[i]), rows, feats))
    grads.append(dot(grad_pair[0], w_gate, 1, 1))
    return out, grads


def plain_late_totals(rows, feats, pair, triple, kept, sent, small, state):
    heads, head, _ = state
    me = lax.axis_index("feat")
    core = lax.bitwise_and(lax.axis_index("rows"), 1)
    late = [plain_features(contract(pair[0], triple[i]), rows, feats) for i in range(3)]
    both = jnp.where(core == 0, jnp.stack([kept, sent]), jnp.stack([sent, kept]))
    both = scatter_rows(both, rows, 1)
    for d in distances(feats):
        both = add_low(both, exchange(both, "feat", feats, d))
    both = gather_rows(both, rows, 1).astype(F32)
    for d in distances(rows):
        small = add_low(small, exchange(small, "rows", rows, d))
    for d in distances(feats):
        small = add_low(small, exchange(small, "feat", feats, d))
    small = small.astype(F32)
    share = pair.shape[2] // feats
    block = lax.dynamic_slice_in_dim(small, me * 16, 16, 0)[:, 0:share]
    at = feats * 16
    packed = small[at + 16 : at + 16 + heads]
    return late + [
        both[0],
        both[1],
        block[0:heads],
        block[heads : heads + 1],
        block[heads + 1 : heads + 2],
        small[at : at + heads],
        packed[:, 0:head],
        packed[:, head : 2 * head],
        packed[:, 2 * head : 3 * head],
        packed[:, 3 * head : 3 * head + 1].reshape(1, heads),
    ]


def solution(mesh):
    batch = ("rows", "feat")
    placed = (
        (P(batch, None, None), P(batch, None, None), P(batch, None), P(batch, None))
        + (P(),) * 15
        + (P(None, "feat"), P(None, "feat"), P("feat", None))
    )
    return jax.shard_map(
        partial(on_device, mesh.shape["rows"], mesh.shape["feat"]),
        mesh=mesh,
        in_specs=placed,
        out_specs=(
            P(batch, None, None),
            P(batch, None, None),
            P("feat"),
            P("feat", None),
            P("feat", None),
            P("feat", None),
            P("feat", None),
            P("feat", None),
            P(),
            P(),
            P(),
            P(),
            P(),
            P(),
            P(),
            P("feat", None),
            P("feat"),
            P(None, "feat"),
            P(None, "feat"),
            P("feat", None),
        ),
        check_vma=False,
    )
```

```python
from functools import partial

import jax
import jax.numpy as jnp
from jax import lax
from jax.experimental import pallas as pl
from jax.experimental.pallas import tpu as pltpu
from jax.sharding import PartitionSpec as P

MB = 16
FORWARD_HEADS = 6
BACKWARD_HEADS = 3
EPSILON = 1e-06
BASE_RATE = 0.1
F32 = jnp.float32
BF16 = jnp.bfloat16


def dot(left, right, left_dim=1, right_dim=0):
    return lax.dot_general(
        left, right, (((left_dim,), (right_dim,)), ((), ())), preferred_element_type=F32
    )


def low(values):
    return values.astype(BF16)


def gelu_parts(values):
    phi = 0.5 + 0.5 * lax.erf(values * 0.7071067811865476)
    density = jnp.exp(-0.5 * values * values) * 0.3989422804014327
    return (values * phi, phi + values * density, density * (2.0 - values * values))


def mean_last(values):
    return jnp.sum(values, -1, keepdims=True) * (1.0 / values.shape[-1])


def sum_rows(values):
    return jnp.sum(values, 0, keepdims=True)


def row_of(ref):
    return ref[...].astype(F32).reshape(1, ref.shape[0])


def column_of(row):
    size = row.shape[1]
    return jnp.transpose(jnp.broadcast_to(row, (size, size)))[:, 0:1]


def segment_masks(seg_row):
    size = seg_row.shape[1]
    rows = lax.broadcasted_iota(jnp.int32, (size, size), 0)
    cols = lax.broadcasted_iota(jnp.int32, (size, size), 1)
    same = column_of(seg_row) == seg_row
    block = MB.bit_length() - 1
    later = lax.shift_right_logical(rows, block) > lax.shift_right_logical(cols, block)
    inclusive = jnp.where(same & (cols <= rows), 1.0, 0.0)
    strict = jnp.where(same & later, 1.0, 0.0)
    return (inclusive, strict)


def forward_kernel(
    seg_smem,
    seg_ref,
    live_ref,
    tok_ref,
    gain1_ref,
    wq_hbm,
    wk_hbm,
    wv_hbm,
    wg_hbm,
    wr_ref,
    br_ref,
    w1_ref,
    b1_ref,
    w2t_ref,
    b2_ref,
    ig_ref,
    ib_ref,
    wo_hbm,
    gain2_ref,
    pair_ref,
    normed_two_ref,
    *refs,
):
    saved = (len(refs) - 15) // 2
    outs, kept, scratch = refs[0:saved], refs[saved : 2 * saved], refs[2 * saved :]
    (
        resid_ref,
        gelu_ref,
        slope_ref,
        qk_ref,
        ecol_ref,
        erow_ref,
        fcol_ref,
        slope1_ref,
        curve1_ref,
        act_ref,
        d1_ref,
        d2_ref,
        n_ref,
        s_ref,
        fit_ref,
        w2s_ref,
        p1_ref,
        p2_ref,
        slopeq_ref,
        nq_ref,
        sq_ref,
    ) = kept
    q_s, k_s, v_s, out_s, base_s, mix_s, w2_s, b2_s = scratch[0:8]
    b1f, b2f, igf, ibf, weights_s, sems, state_sems = scratch[8:]
    length, width = tok_ref.shape[1], tok_ref.shape[2]
    copies = [
        pltpu.make_async_copy(w, weights_s.at[i], sems.at[i])
        for i, w in enumerate((wk_hbm, wv_hbm, wq_hbm, wg_hbm, wo_hbm))
    ]
    for copy in copies:
        copy.start()
    saves = {
        i: pltpu.make_async_copy(kept[i], outs[i], sems.at[len(copies) + i])
        for i in range(saved)
        if i != 15
    }

    def save(*indices):
        for i in indices:
            saves[i].start()

    heads, head = w1_ref.shape[0], w1_ref.shape[1]
    blocks = length // MB
    tok = tok_ref[0].astype(F32)
    spread = lax.rsqrt(mean_last(tok * tok) + EPSILON)
    normed = low(tok * spread * row_of(gain1_ref))
    pair_ref[0] = normed
    seg_row = seg_ref[...].astype(F32)
    live = column_of(live_ref[...].astype(F32))
    rate_pre = dot(normed, wr_ref[...], 1, 1) + br_ref[...].astype(F32)
    sig = jax.nn.sigmoid(rate_pre)
    rates = (BASE_RATE / head) * sig * live
    ecol_ref[...] = jnp.zeros(ecol_ref.shape, F32)
    ecol_ref[:, 0:heads] = rates
    fcol_ref[...] = jnp.zeros(fcol_ref.shape, F32)
    fcol_ref[:, 0:heads] = rates * (1.0 - sig)
    erow_ref[...] = jnp.transpose(ecol_ref[...])[0 : erow_ref.shape[0]]

    def project(i, to):
        copies[i].wait()
        whole = dot(normed, weights_s[i])
        for h in range(heads):
            to[h] = whole[:, h * head : (h + 1) * head]

    project(0, k_s)
    project(1, v_s)
    b1f[...] = b1_ref[...].astype(F32)
    b2f[...] = b2_ref[...].astype(F32)
    igf[...] = ig_ref[...].astype(F32)
    ibf[...] = ib_ref[...].astype(F32)
    for h in range(heads):
        qk_ref[h, length : 2 * length] = low(k_s[h])

    d1_ref[...] = jnp.zeros(d1_ref.shape, BF16)
    inclusive, strict = segment_masks(seg_row)
    for h in range(heads):
        keys = qk_ref[h, length : 2 * length]
        mix_s[h] = low((dot(keys, keys, 1, 1) + 1.0) * (strict * erow_ref[h : h + 1, :]))
        base_s[h] = dot(keys, w1_ref[h]) + b1f[h : h + 1]

    def step(b, carry):
        here = pl.multiple_of(b * MB, MB)
        before = jnp.maximum(here - 1, 0)
        fresh = (b == 0) | (seg_smem[0, here] != seg_smem[0, before])

        ds = pl.ds(here, MB)
        rng = range(heads)
        k = [k_s[h, ds, :] for h in rng]
        v = [v_s[h, ds, :] for h in rng]
        e = [ecol_ref[ds, h : h + 1] for h in rng]
        w2f = [jnp.where(fresh, w2t_ref[h].astype(F32), w2_s[h]) for h in rng]
        w2 = [low(w2f[h]) for h in rng]
        b2 = [jnp.where(fresh, b2f[h : h + 1], b2_s[h]) for h in rng]
        g = [igf[h : h + 1] for h in rng]
        gb = [ibf[h : h + 1] for h in rng]
        parts = [gelu_parts(base_s[h, ds, :] - dot(mix_s[h, ds, :], d1_ref[h])) for h in rng]
        act = [low(parts[h][0]) for h in rng]
        z2 = [dot(act[h], w2[h], 1, 1) + b2[h] for h in rng]
        c = [z - mean_last(z) for z in z2]
        s = [lax.rsqrt(mean_last(x * x) + EPSILON) for x in c]
        n = [c[h] * s[h] for h in rng]
        fit = [g[h] * n[h] + gb[h] - (v[h] - k[h]) for h in rng]
        share = [g[h] * fit[h] for h in rng]
        m1 = [mean_last(share[h]) for h in rng]
        m2 = [mean_last(share[h] * n[h]) for h in rng]
        d2 = [s[h] * (share[h] - m1[h] - n[h] * m2[h]) for h in rng]
        back = [dot(low(d2[h]), w2[h]) for h in rng]
        d1 = [back[h] * parts[h][1] for h in rng]
        d1b = [low(d1[h]) for h in rng]
        ed2 = [d2[h] * e[h] for h in rng]
        up2 = [dot(low(ed2[h]), act[h], 0, 0) for h in rng]
        for h in rng:
            w2s_ref[b, h] = w2[h]
            w2_s[h] = w2f[h] - up2[h]
            b2_s[h] = b2[h] - sum_rows(ed2[h])
            act_ref[h, pl.ds(length + here, MB), :] = act[h]
            slope1_ref[h, ds, :] = low(parts[h][1])
            curve1_ref[h, ds, :] = low(back[h] * parts[h][2])
            d1_ref[h, ds, :] = d1b[h]
            d2_ref[h, ds, :] = low(d2[h])
            n_ref[h, ds, :] = low(n[h])
            s_ref[ds, h : h + 1] = s[h]
            fit_ref[h, ds, :] = low(fit[h])
        pltpu.make_async_copy(w2s_ref.at[b], outs[15].at[b], state_sems.at[b]).start()
        return carry

    save(4, 5, 6)
    lax.fori_loop(0, blocks, step, 0, unroll=4)
    save(7, 8, 10, 11, 12, 13, 14)
    project(2, q_s)
    for h in range(heads):
        qk_ref[h, 0:length] = low(q_s[h])
    save(3)
    for start in range(0, heads, FORWARD_HEADS):
        rng = range(start, start + FORWARD_HEADS)
        every = range(FORWARD_HEADS)
        queries = [qk_ref[h, 0:length] for h in rng]
        keys = [qk_ref[h, length : 2 * length] for h in rng]
        key_act = [act_ref[h, length : 2 * length] for h in rng]
        er = [erow_ref[h : h + 1, :] for h in rng]
        p1 = [(dot(queries[i], keys[i], 1, 1) + 1.0) * inclusive for i in every]
        zq1 = [
            dot(queries[i], w1_ref[h]) + b1f[h : h + 1] - dot(low(p1[i] * er[i]), d1_ref[h])
            for i, h in enumerate(rng)
        ]
        parts = [gelu_parts(x) for x in zq1]
        aq = [low(x[0]) for x in parts]
        p2 = [(dot(aq[i], key_act[i], 1, 1) + 1.0) * inclusive for i in every]
        zq2 = [
            dot(aq[i], w2t_ref[h], 1, 1)
            + b2f[h : h + 1]
            - dot(low(p2[i] * er[i]), d2_ref[h])
            for i, h in enumerate(rng)
        ]
        c = [z - mean_last(z) for z in zq2]
        s = [lax.rsqrt(mean_last(x * x) + EPSILON) for x in c]
        n = [c[i] * s[i] for i in every]
        for i, h in enumerate(rng):
            p1_ref[h] = low(p1[i])
            p2_ref[h] = low(p2[i])
            act_ref[h, 0:length] = aq[i]
            slopeq_ref[h] = low(parts[i][1])
            nq_ref[h] = low(n[i])
            sq_ref[:, h : h + 1] = s[i]
            out_s[:, h * head : (h + 1) * head] = (
                q_s[h] + igf[h : h + 1] * n[i] + ibf[h : h + 1]
            )
    save(9, 16, 17, 18, 19, 20)
    inner_out = out_s[...]
    copies[3].wait()
    gate, slope, _ = gelu_parts(dot(normed, weights_s[3]))
    gelu_ref[...] = gate
    slope_ref[...] = inner_out * slope
    gated = low(inner_out * gate)
    pair_ref[1] = gated
    copies[4].wait()
    resid = tok + dot(gated, weights_s[4])
    resid_ref[...] = resid
    spread_two = lax.rsqrt(mean_last(resid * resid) + EPSILON)
    normed_two_ref[...] = low(resid * spread_two * row_of(gain2_ref))
    save(0, 1, 2)
    for copy in saves.values():
        copy.wait()
    for b in range(blocks):
        pltpu.make_async_copy(w2s_ref.at[b], outs[15].at[b], state_sems.at[b]).wait()


def ffn_kernel(x_ref, c_ref, wg_ref, wu_ref, wd_ref, act_ref, gg_ref, gu_ref, gx_ref):
    x = x_ref[...]
    gate = dot(x, wg_ref[...])
    up = dot(x, wu_ref[...])
    grad_act = dot(c_ref[...], wd_ref[...], 1, 1)
    sigma = jax.nn.sigmoid(gate)
    silu = gate * sigma
    act_ref[...] = low(silu * up)
    gg = low(grad_act * up * sigma * (1.0 + gate * (1.0 - sigma)))
    gu = low(grad_act * silu)
    gg_ref[...] = gg
    gu_ref[...] = gu
    gx_ref[...] = low(dot(gg, wg_ref[...], 1, 1) + dot(gu, wu_ref[...], 1, 1))


def ffn_weights_kernel(parts, ids_smem, *refs):
    x_refs, c_refs, act_refs, gg_refs, gu_refs = (
        refs[i * parts : (i + 1) * parts] for i in range(5)
    )
    wd_ref, kept_ref, sent_ref = refs[5 * parts : 5 * parts + 3]
    out_refs = refs[5 * parts + 3 : 6 * parts + 3]
    x_s, c_s, act_s, gg_s, gu_s = refs[6 * parts + 3 :]
    rows = x_refs[0].shape[0]
    for i in range(parts):
        at = slice(i * rows, (i + 1) * rows)
        x_s[at] = x_refs[i][...]
        c_s[at] = c_refs[i][...]
        act_s[at] = act_refs[i][...]
        gg_s[at] = gg_refs[i][...]
        gu_s[at] = gu_refs[i][...]
        out_refs[i][...] = low(dot(act_refs[i][...], wd_ref[...]))
    half = kept_ref.shape[2]
    core = ids_smem[0]
    for i, (left, right) in enumerate(((x_s, gg_s), (x_s, gu_s), (c_s, act_s))):
        whole = low(dot(left[...], right[...], 0, 0))

        @pl.when(core == 0)
        def _(whole=whole, i=i):
            kept_ref[i] = whole[:, 0:half]
            sent_ref[i] = whole[:, half:]

        @pl.when(core != 0)
        def _(whole=whole, i=i):
            kept_ref[i] = whole[:, half:]
            sent_ref[i] = whole[:, 0:half]


def between_kernel(parts, *refs):
    pieces = refs[0:parts]
    resid_ref, cot_ref, gain2_ref, wo_ref, gelu_ref, slope_ref = refs[parts : parts + 6]
    resid_grad_ref, go_ref, pair_ref, gain_grad_ref = refs[parts + 6 :]
    grad = pieces[0][...].astype(F32)
    for piece in pieces[1:]:
        grad = grad + piece[...].astype(F32)
    resid = resid_ref[...]
    spread = lax.rsqrt(mean_last(resid * resid) + EPSILON)
    scaled = row_of(gain2_ref) * grad
    grad_resid = (
        cot_ref[0].astype(F32)
        + spread * scaled
        - resid * (spread * spread * spread * mean_last(scaled * resid))
    )
    gain_grad_ref[...] = sum_rows(grad * resid * spread)
    resid_grad_ref[...] = grad_resid
    grad_branch = low(grad_resid)
    grad_gated = dot(grad_branch, wo_ref[...], 1, 1)
    go_ref[...] = grad_gated * gelu_ref[...]
    pair_ref[0] = low(grad_gated * slope_ref[...])
    pair_ref[1] = grad_branch


def backward_kernel(
    ids_smem,
    seg_smem,
    seg_ref,
    go_ref,
    qk_ref,
    ecol_ref,
    erow_ref,
    fcol_ref,
    w1_ref,
    w2t_ref,
    ig_ref,
    slope1_ref,
    curve1_ref,
    act_ref,
    d1_ref,
    d2_ref,
    n_ref,
    s_ref,
    fit_ref,
    w2s_ref,
    p1_ref,
    p2_ref,
    slopeq_ref,
    nq_ref,
    sq_ref,
    triple_ref,
    gr_ref,
    kept_ref,
    sent_ref,
    small_ref,
    igf,
    t1_s,
    t2_s,
    ga_s,
    hh1_s,
    hh2_s,
    u_s,
    share_s,
    ge_s,
    mix_s,
    gw2_s,
    gb2_s,
):
    length = go_ref.shape[0]
    heads, head, inner = w1_ref.shape
    blocks = length // MB
    top, bottom = slice(0, length), slice(length, 2 * length)
    igf[...] = ig_ref[...].astype(F32)
    inclusive, strict = segment_masks(seg_ref[...].astype(F32))
    for first in range(0, heads, BACKWARD_HEADS):
        rng = range(first, first + BACKWARD_HEADS)
        every = range(BACKWARD_HEADS)
        g = [igf[h : h + 1] for h in rng]
        weigh = [inclusive * erow_ref[h : h + 1, :] for h in rng]
        n = [nq_ref[h].astype(F32) for h in rng]
        x = [go_ref[:, h * head : (h + 1) * head] * igf[h : h + 1] for h in rng]
        mx = [mean_last(x[i]) for i in every]
        mxn = [mean_last(x[i] * n[i]) for i in every]
        hq2 = [
            low(sq_ref[:, h : h + 1] * (x[i] - mx[i] - n[i] * mxn[i]))
            for i, h in enumerate(rng)
        ]
        aq = [act_ref[h, top] for h in rng]
        ak = [act_ref[h, bottom] for h in rng]
        t2 = [dot(p2_ref[h], hq2[i], 0, 0) for i, h in enumerate(rng)]
        mix = [
            low(-dot(hq2[i], d2_ref[h], 1, 1) * weigh[i]) for i, h in enumerate(rng)
        ]
        gaq = [dot(hq2[i], w2t_ref[h]) + dot(mix[i], ak[i]) for i, h in enumerate(rng)]
        ga = [dot(mix[i], aq[i], 0, 0) for i in every]
        hq1 = [low(gaq[i] * slopeq_ref[h].astype(F32)) for i, h in enumerate(rng)]
        t1 = [dot(p1_ref[h], hq1[i], 0, 0) for i, h in enumerate(rng)]
        for i, h in enumerate(rng):
            hh2_s[h, top] = hq2[i]
            t2_s[h] = t2[i]
            ga_s[h] = ga[i]
            hh1_s[h, top] = hq1[i]
            t1_s[h] = t1[i]
    ge_s[...] = jnp.zeros(ge_s.shape, F32)
    earlier = jnp.transpose(strict)
    for h in range(heads):
        keys = qk_ref[h, bottom]
        mix_s[h] = low((dot(keys, keys, 1, 1) + 1.0) * earlier)
    hh1_s[:, bottom, :] = jnp.zeros(hh1_s[:, bottom, :].shape, BF16)

    def step(i, carry):
        b = blocks - 1 - i
        here = pl.multiple_of(b * MB, MB)
        after = jnp.minimum(here + MB, length - 1)
        fresh = (i == 0) | (seg_smem[0, after] != seg_smem[0, after - 1])

        ds = pl.ds(here, MB)
        ds_low = pl.ds(length + here, MB)
        rng = range(heads)
        act = [act_ref[h, ds_low, :] for h in rng]
        e = [ecol_ref[ds, h : h + 1] for h in rng]
        w2 = [w2s_ref[b, h] for h in rng]
        gw2 = [jnp.where(fresh, 0.0, gw2_s[h]) for h in rng]
        gw2b = [low(x) for x in gw2]
        gb2 = [jnp.where(fresh, 0.0, gb2_s[h]) for h in rng]
        d1 = [d1_ref[h, ds, :].astype(F32) for h in rng]
        d2 = [d2_ref[h, ds, :].astype(F32) for h in rng]
        n = [n_ref[h, ds, :].astype(F32) for h in rng]
        s = [s_ref[ds, h : h + 1] for h in rng]
        fit = [fit_ref[h, ds, :].astype(F32) for h in rng]
        slope = [slope1_ref[h, ds, :].astype(F32) for h in rng]
        curve = [curve1_ref[h, ds, :].astype(F32) for h in rng]
        g = [igf[h : h + 1] for h in rng]
        share = [g[h] * fit[h] for h in rng]
        t1 = [t1_s[h, ds, :] + dot(mix_s[h, ds, :], hh1_s[h, bottom]) for h in rng]
        t2 = [t2_s[h, ds, :] + dot(act[h], gw2b[h], 1, 1) + gb2[h] for h in rng]
        g1 = [-e[h] * t1[h] for h in rng]
        u = [low(g1[h] * slope[h]) for h in rng]
        ed2 = [low(-e[h] * d2[h]) for h in rng]
        ga = [ga_s[h, ds, :] + dot(ed2[h], gw2b[h]) for h in rng]
        g2 = [dot(u[h], w2[h], 1, 1) - e[h] * t2[h] for h in rng]
        y = [s[h] * g2[h] for h in rng]
        my = [mean_last(y[h]) for h in rng]
        myn = [mean_last(y[h] * n[h]) for h in rng]
        msn = [mean_last(share[h] * n[h]) for h in rng]
        mgd = [mean_last(g2[h] * d2[h]) for h in rng]
        gshare = [y[h] - my[h] - n[h] * myn[h] for h in rng]
        gn = [g[h] * (g[h] * gshare[h]) - y[h] * msn[h] - share[h] * myn[h] for h in rng]
        mn = [mean_last(gn[h]) for h in rng]
        mnn = [mean_last(gn[h] * n[h]) for h in rng]
        h2 = [
            low(s[h] * (gn[h] - mn[h] - n[h] * (mnn[h] + mgd[h]))) for h in rng
        ]
        ga = [ga[h] + dot(h2[h], w2[h]) for h in rng]
        h1f = [ga[h] * slope[h] + g1[h] * curve[h] for h in rng]
        h1 = [low(x) for x in h1f]
        up2 = [
            dot(low(d2[h]), u[h], 0, 0) + dot(h2[h], act[h], 0, 0) for h in rng
        ]
        for h in rng:
            w2n = gw2[h] + up2[h]
            gw2_s[h] = w2n
            gb2_s[h] = gb2[h] + sum_rows(h2[h].astype(F32))
            u_s[h, ds, :] = u[h]
            hh1_s[h, ds_low, :] = h1[h]
            hh2_s[h, ds_low, :] = h2[h]
            share_s[h, ds, :] = gshare[h]
            ge_s[ds, h : h + 1] = -jnp.sum(d1[h] * t1[h], -1, keepdims=True) - jnp.sum(
                d2[h] * t2[h], -1, keepdims=True
            )
        return carry

    lax.fori_loop(0, blocks, step, 0, unroll=4)
    small_ref[...] = jnp.zeros(small_ref.shape, F32)
    core = ids_smem[0]
    pad = small_ref.shape[0] // 2
    for start in range(0, heads, BACKWARD_HEADS):
        rng = range(start, start + BACKWARD_HEADS)
        every = range(BACKWARD_HEADS)
        cols = [slice(h * head, (h + 1) * head) for h in rng]
        g = [igf[h : h + 1] for h in rng]
        er = [erow_ref[h : h + 1, :] for h in rng]
        hh1 = [hh1_s[h] for h in rng]
        hh2 = [hh2_s[h] for h in rng]
        qk = [qk_ref[h] for h in rng]
        keys = [qk_ref[h, bottom] for h in rng]
        share = [share_s[h] for h in rng]
        go = [go_ref[:, cols[i]] for i in every]
        both = [dot(hh1[i], d1_ref[h], 1, 1) for i, h in enumerate(rng)]
        direct = [dot(hh1[i], w1_ref[h], 1, 1) for i, h in enumerate(rng)]
        mixq = [low(-both[i][top] * (inclusive * er[i])) for i in every]
        mixk = [low(-both[i][bottom] * (strict * er[i])) for i in every]
        first = [low(dot(qk[i], hh1[i], 0, 0)) for i in every]
        second = [
            low(dot(hh2[i], act_ref[h], 0, 0) + dot(d2_ref[h], u_s[h], 0, 0))
            for i, h in enumerate(rng)
        ]
        gq = [low(go[i] + direct[i][top] + dot(mixq[i], keys[i])) for i in every]
        spread = [
            dot(mixq[i], qk_ref[h, top], 0, 0) + dot(mixk[i], keys[i], 0, 0)
            for i, h in enumerate(rng)
        ]
        gk = [
            low(g[i] * share[i] + direct[i][bottom] + dot(mixk[i], keys[i]) + spread[i])
            for i in every
        ]
        for i, h in enumerate(rng):
            triple_ref[0, :, cols[i]] = gq[i]
            triple_ref[1, :, cols[i]] = gk[i]
            triple_ref[2, :, cols[i]] = low(-g[i] * share[i])
            kept_ref[cols[i]] = jnp.where(core == 0, first[i], second[i])
            sent_ref[cols[i]] = jnp.where(core == 0, second[i], first[i])
            small_ref[h : h + 1] = sum_rows(hh1[i].astype(F32))
            row = slice(pad + h, pad + h + 1)
            small_ref[row, 0:head] = sum_rows(hh2[i].astype(F32))
            small_ref[row, head : 2 * head] = sum_rows(
                go[i] * nq_ref[h].astype(F32)
                + share[i] * (fit_ref[h].astype(F32) + g[i] * n_ref[h].astype(F32))
            )
            small_ref[row, 2 * head : 3 * head] = sum_rows(go[i]) + g[i] * sum_rows(share[i])
    grad_rates = ge_s[...] * fcol_ref[...]
    gr_ref[...] = low(grad_rates)
    total = jnp.broadcast_to(sum_rows(grad_rates), (grad_rates.shape[1], grad_rates.shape[1]))
    total = jnp.transpose(total)[0:heads, 0:1]
    high = low(total).astype(F32)
    slot = lax.broadcasted_iota(jnp.int32, (heads, head), 1)
    mine = ids_smem[3]
    small_ref[pad : pad + heads, 3 * head : 4 * head] = jnp.where(
        slot == mine, high, 0.0
    ) + jnp.where(slot == mine + head // 2, total - high, 0.0)


def put_matrix(to_ref, values, index, count, feats):
    chips = to_ref.shape[0]
    rows = values.shape[0] // (feats * chips)
    chunks = values.shape[1] // 128
    for f in range(feats):
        for l in range(chunks):
            row = ((f * count + index) * chunks + l) * rows
            for j in range(chips):
                at = (f * chips + j) * rows
                to_ref[j, row : row + rows, :] = values[at : at + rows, l * 128 : (l + 1) * 128]


def core_columns(core, values):
    half = values.shape[1] // 2
    return jnp.where(core == 0, values[:, 0:half], values[:, half:])


def put_halves(ids_smem, kept_ref, sent_ref, put):
    core, chip = ids_smem[0], ids_smem[1]
    first, second = 1 + core, 2 - core
    put(kept_ref.at[0], chip)
    put(kept_ref.at[1], lax.bitwise_xor(chip, second))
    put(sent_ref.at[0], lax.bitwise_xor(chip, first))
    put(sent_ref.at[1], lax.bitwise_xor(chip, 3))


def gate_weights_kernel(
    feats,
    ids_smem,
    mine_ref,
    other_ref,
    grads_ref,
    other_grads_ref,
    wg_ref,
    kept_ref,
    got_ref,
    part_ref,
    kept_out,
    sent_out,
    pieces_s,
    left_s,
    right_s,
):
    core = ids_smem[0]
    length = mine_ref.shape[1]
    for i in range(2):
        left_s[i, 0:length] = mine_ref[i]
        left_s[i, length : 2 * length] = other_ref[i]
        right_s[i, 0:length] = core_columns(core, grads_ref[i])
        right_s[i, length : 2 * length] = core_columns(core, other_grads_ref[i])
    for i in range(2):
        put_matrix(pieces_s, low(dot(left_s[i], right_s[i], 0, 0)), i, 2, feats)
    count, _, half = kept_ref.shape
    chunks = half // 128
    before = kept_out.shape[1] - pieces_s.shape[1]
    rows = before // (count * chunks)

    def put(out, place):
        at = pl.ds(pl.multiple_of(place * rows, rows), rows)
        for i in range(count):
            both = low(kept_ref[i, at, :].astype(F32) + got_ref[i, at, :].astype(F32))
            for l in range(chunks):
                row = (i * chunks + l) * rows
                out[row : row + rows] = both[:, l * 128 : (l + 1) * 128]
        out[before:] = pieces_s[place]

    put_halves(ids_smem, kept_out, sent_out, put)
    part_ref[...] = dot(grads_ref[0], wg_ref[...], 1, 1)


def input_kernel(
    feats,
    triple_ref,
    gr_ref,
    pair_ref,
    wq_ref,
    wk_ref,
    wv_ref,
    wr_ref,
    part_ref,
    tok_ref,
    gain1_ref,
    resid_grad_ref,
    small_ref,
    gain_two_ref,
    grad_ref,
    small_out,
):
    heads = wr_ref.shape[0]
    grad = part_ref[...] + dot(triple_ref[0], wq_ref[...], 1, 1)
    grad = grad + dot(triple_ref[1], wk_ref[...], 1, 1) + dot(triple_ref[2], wv_ref[...], 1, 1)
    gr = gr_ref[...]
    grad = grad + dot(gr[:, 0:heads], wr_ref[...])
    tok = tok_ref[0].astype(F32)
    spread = lax.rsqrt(mean_last(tok * tok) + EPSILON)
    scaled = row_of(gain1_ref) * grad
    grad_ref[0] = (
        resid_grad_ref[...]
        + spread * scaled
        - tok * (spread * spread * spread * mean_last(scaled * tok))
    )
    rate_rows = dot(gr, pair_ref[0], 0, 0)
    gain_row = sum_rows(grad * tok * spread)
    small_out[...] = jnp.zeros(small_out.shape, BF16)
    share = tok.shape[1] // feats
    for f in range(feats):
        cols = slice(f * share, (f + 1) * share)
        small_out[f * 16 : f * 16 + 16, 0:share] = low(
            jnp.concatenate(
                [rate_rows[0:heads, cols], gain_row[:, cols], gain_two_ref[:, cols]]
                + [jnp.zeros((14 - heads, share), F32)],
                0,
            )
        )
    at = feats * 16
    small_out[at : at + small_ref.shape[0]] = low(small_ref[...])


def tails_kernel(ids_smem, kept_ref, got_ref, kept_out, sent_out, tails_s):
    chips = tails_s.shape[0]
    inner = low(kept_ref[...].astype(F32) + got_ref[...].astype(F32))
    rows = inner.shape[0] // chips
    for j in range(chips):
        for l in range(2):
            tails_s[j, l * rows : (l + 1) * rows] = inner[
                j * rows : (j + 1) * rows, l * 128 : (l + 1) * 128
            ]

    def put(out, place):
        out[...] = tails_s[place]

    put_halves(ids_smem, kept_out, sent_out, put)


def late_weights_kernel(
    feats,
    ids_smem,
    mine_ref,
    other_ref,
    triple_ref,
    other_triple_ref,
    small_ref,
    kept_out,
    sent_out,
    pieces_s,
    left_s,
    right_s,
):
    core = ids_smem[0]
    length = mine_ref.shape[1]
    left_s[0:length] = mine_ref[0]
    left_s[length : 2 * length] = other_ref[0]
    for i in range(3):
        right_s[i, 0:length] = core_columns(core, triple_ref[i])
        right_s[i, length : 2 * length] = core_columns(core, other_triple_ref[i])
    for i in range(3):
        put_matrix(pieces_s, low(dot(left_s[...], right_s[i], 0, 0)), i, 3, feats)
    chips, most, _ = pieces_s.shape
    extra = small_ref.shape[0] // chips
    for j in range(chips):
        for l in range(2):
            at = most - (2 - l) * extra
            pieces_s[j, at : at + extra] = small_ref[
                j * extra : (j + 1) * extra, l * 128 : (l + 1) * 128
            ]

    def put(out, place):
        out[...] = pieces_s[place]

    put_halves(ids_smem, kept_out, sent_out, put)


def mixed_kernel(feats, resid_ref, *refs):
    kept_ref, got_ref, mixed_ref, stay_ref, go_ref = refs[feats:]
    total = resid_ref[...]
    for ref in refs[0:feats]:
        total = total + ref[...].astype(F32)
    mixed_ref[0] = low(total)
    add_kernel(kept_ref, got_ref, stay_ref, go_ref)


def add_kernel(kept_ref, got_ref, stay_ref, go_ref):
    stay_ref[...] = low(kept_ref[0].astype(F32) + got_ref[0].astype(F32))
    go_ref[...] = low(kept_ref[1].astype(F32) + got_ref[1].astype(F32))


def sum_at(refs, at):
    value = refs[0][at].astype(F32)
    for ref in refs[1:]:
        value = value + ref[at].astype(F32)
    return low(value)


def cut_feat_kernel(common, ids_smem, *refs):
    parts, outs = refs[0:2], refs[2:]
    rows = outs[0].shape[0] - common
    shared = sum_at(parts, (slice(rows * len(outs), rows * len(outs) + common), slice(None)))
    for s, out in enumerate(outs):
        at = pl.ds(pl.multiple_of(lax.bitwise_xor(ids_smem[2], s) * rows, 16), rows)
        out[0:rows] = sum_at(parts, (at, slice(None)))
        out[rows:] = shared


def sum_kernel(*refs):
    values = [ref[...].astype(F32) for ref in refs[:-1]]
    while len(values) > 1:
        values = [values[i] + values[i + 1] for i in range(0, len(values), 2)]
    refs[-1][...] = low(values[0])


def join_kernel(*refs):
    total_ref, out_ref = refs[-2:]
    rows = refs[0].shape[0]
    sum_kernel(*refs[:-2], out_ref.at[0:rows])
    out_ref[rows:] = total_ref[...]


def middle_kernel(ids_smem, *refs):
    pair, tail = refs[0:2], refs[2:4]
    total_ref, outs = refs[4], refs[5:]
    before = total_ref.shape[0]
    rows = (pair[0].shape[0] - before) // len(outs)
    shared = sum_at(tail, (slice(None), slice(None)))
    for s, out in enumerate(outs):
        at = pl.multiple_of(before + lax.bitwise_xor(ids_smem[2], s) * rows, 16)
        out[0:rows] = sum_at(pair, (pl.ds(at, rows), slice(None)))
        out[rows:] = shared
    total_ref[...] = sum_at(pair, (slice(0, before), slice(None)))


def take_matrices(ids_smem, pieces, outs, start=0, order=None):
    core, chip = ids_smem[0], ids_smem[1]
    chunks = outs[0].shape[1] // 256
    rows = outs[0].shape[0] // len(pieces)
    for s, both in enumerate(pieces):
        ats = [
            pl.ds(pl.multiple_of(lax.bitwise_xor(chip, d) * rows, 16), rows)
            for d in (order[s] if order else (s, s))
        ]
        for i, out in enumerate(outs):
            for l in range(chunks):
                row = start + (i * chunks + l) * rows
                mine = both[0][row : row + rows, :].astype(F32)
                other = both[1][row : row + rows, :].astype(F32)
                low_cols = slice(l * 128, (l + 1) * 128)
                high_cols = slice((chunks + l) * 128, (chunks + l + 1) * 128)

                @pl.when(core == 0)
                def _(out=out, ats=ats, mine=mine, other=other, a=low_cols, b=high_cols):
                    out[ats[0], a] = mine
                    out[ats[1], b] = other

                @pl.when(core != 0)
                def _(out=out, ats=ats, mine=mine, other=other, a=low_cols, b=high_cols):
                    out[ats[0], b] = mine
                    out[ats[1], a] = other


def early_totals_kernel(ids_smem, *refs):
    core, chip = ids_smem[0], ids_smem[1]
    first, second = 1 + core, 2 - core
    pieces = [(refs[s], refs[4 + s]) for s in range(4)]
    order = [(0, 0), (second, first), (first, second), (3, 3)]
    outs, kept, down_s, sems = refs[8:15], refs[15:22], refs[22], refs[23]
    gate_ref, up_ref, down_ref, wg_ref, wo_ref, first_ref, second_ref = kept
    saves = [pltpu.make_async_copy(kept[i], outs[i], sems.at[i]) for i in range(7)]
    rows = first_ref.shape[0] // 4
    start = 2 * (wg_ref.shape[0] // 4) * (wg_ref.shape[1] // 256)
    take_matrices(ids_smem, pieces, (gate_ref, up_ref, down_s), start + 2 * rows, order)
    saves[0].start()
    saves[1].start()
    down_ref[...] = jnp.transpose(down_s[...])
    saves[2].start()
    for s, both in enumerate(pieces):
        ats = [
            pl.ds(pl.multiple_of(lax.bitwise_xor(chip, d) * rows, 16), rows) for d in order[s]
        ]
        for l in range(2):
            cols = slice(l * 128, (l + 1) * 128)
            row = start + l * rows
            mine = both[0][row : row + rows].astype(F32)
            other = both[1][row : row + rows].astype(F32)

            @pl.when(core == 0)
            def _(ats=ats, cols=cols, mine=mine, other=other):
                first_ref[ats[0], cols] = mine
                second_ref[ats[1], cols] = other

            @pl.when(core != 0)
            def _(ats=ats, cols=cols, mine=mine, other=other):
                first_ref[ats[1], cols] = other
                second_ref[ats[0], cols] = mine

    saves[5].start()
    saves[6].start()
    take_matrices(ids_smem, pieces, (wg_ref, wo_ref), order=order)
    saves[3].start()
    saves[4].start()
    for copy in saves:
        copy.wait()


def late_totals_kernel(chips, feats, heads, head, ids_smem, *refs):
    pieces = [(refs[s], refs[chips + s]) for s in range(chips)]
    matrices = refs[2 * chips : 2 * chips + 3]
    (rate_ref, norm1_ref, norm2_ref, b1_ref, b2_ref, ig_ref, ib_ref, br_ref, small_s) = refs[
        2 * chips + 3 :
    ]
    chip, feat = ids_smem[1], ids_smem[2]
    take_matrices(ids_smem, pieces, matrices)
    extra = small_s.shape[0] // chips
    most = refs[0].shape[0]
    for s, both in enumerate(pieces):
        at = pl.ds(pl.multiple_of(lax.bitwise_xor(chip, s) * extra, 16), extra)
        for l in range(2):
            row = most - (2 - l) * extra
            small_s[at, l * 128 : (l + 1) * 128] = both[0][row : row + extra].astype(
                F32
            ) + both[1][row : row + extra].astype(F32)
    share = rate_ref.shape[1]
    block = small_s[pl.ds(pl.multiple_of(feat * 16, 16), 16), :]
    rate_ref[...] = block[0:heads, 0:share]
    norm1_ref[...] = block[heads : heads + 1, 0:share]
    norm2_ref[...] = block[heads + 1 : heads + 2, 0:share]
    at = feats * 16
    b1_ref[...] = small_s[at : at + heads, :]
    packed = small_s[at + 16 : at + 16 + heads, :]
    b2_ref[...] = packed[:, 0:head]
    ig_ref[...] = packed[:, head : 2 * head]
    ib_ref[...] = packed[:, 2 * head : 3 * head]
    turned = jnp.transpose(small_s[at + 16 : at + 32, 128:])
    br_ref[...] = sum_rows(turned[3 * head - 128 :])[:, 0:heads]


def held(values):
    return pltpu.with_memory_space_constraint(values, pltpu.VMEM)


def in_order():
    last = []

    def ordered(kernel, outs, inputs, scratch=(), **options):
        inputs = list(inputs)
        at = options.get("smem", 0)
        if last:
            inputs[at], _ = lax.optimization_barrier((inputs[at], last.pop()))
        found = call(kernel, outs, inputs, scratch, **options)
        last.append(found[0])
        return found

    return ordered


def call(
    kernel, outs, inputs, scratch=(), smem=0, cover=1, plain=(), loose=(), keep=True, mib=24
):
    specs, placed = [], []
    for i, x in enumerate(inputs):
        if i < smem:
            specs.append(pl.BlockSpec(memory_space=pltpu.SMEM))
            placed.append(x)
        elif i in loose:
            specs.append(pl.BlockSpec(memory_space=pltpu.HBM))
            placed.append(pltpu.with_memory_space_constraint(x, pltpu.HBM))
        elif i in plain:
            specs.append(pl.BlockSpec(memory_space=pltpu.VMEM))
            placed.append(pltpu.with_memory_space_constraint(x, pltpu.HBM))
        else:
            specs.append(pl.BlockSpec(memory_space=pltpu.VMEM))
            placed.append(held(x))
    kept = [keep] * len(outs) if isinstance(keep, bool) else list(keep)
    return pl.pallas_call(
        kernel,
        out_shape=[
            pltpu.VMEM(s, d) if k else pltpu.HBM(s, d) for (s, d), k in zip(outs, kept)
        ],
        in_specs=specs,
        out_specs=[
            pl.BlockSpec(memory_space=pltpu.HBM if k is None else pltpu.VMEM) for k in kept
        ],
        scratch_shapes=[pltpu.VMEM(*x) if isinstance(x, tuple) else x for x in scratch],
        cost_estimate=pl.CostEstimate(
            flops=int(2e10 * cover + 1e6), bytes_accessed=int(2e7 * cover + 1e3), transcendentals=0
        ),
        compiler_params=pltpu.CompilerParams(vmem_limit_bytes=mib * 2**20),
    )(*placed)


def exchange(values, axis, size, distance):
    return lax.ppermute(values, axis, [(i, i ^ distance) for i in range(size)])


def add_low(left, right):
    return low(left.astype(F32) + right.astype(F32))


def halve(values, axis, size, distance, dim):
    side = lax.bitwise_and(lax.axis_index(axis) // distance, 1)
    half = values.shape[dim] // 2
    kept = lax.dynamic_slice_in_dim(values, side * half, half, dim)
    sent = lax.dynamic_slice_in_dim(values, (1 - side) * half, half, dim)
    return add_low(kept, exchange(sent, axis, size, distance))


def double(values, axis, size, distance, dim):
    side = lax.bitwise_and(lax.axis_index(axis) // distance, 1)
    other = exchange(values, axis, size, distance)
    return jnp.where(
        side == 0,
        jnp.concatenate([values, other], dim),
        jnp.concatenate([other, values], dim),
    )


def distances(size):
    found = []
    step = 1
    while step < size:
        found.append(step)
        step *= 2
    return found


def across_chips(values, rows):
    return [values[0]] + [
        exchange(values[s], "rows", rows, 2 * s) for s in range(1, len(values))
    ]


def across_feats(values, feats):
    return [values[0]] + [exchange(values[s], "feat", feats, s) for s in range(1, feats)]


def first_axis(values, rows):
    return lax.ppermute(values, "rows", [(i, i ^ (2 << (i & 1))) for i in range(rows)])


def second_axis(values, rows):
    return lax.ppermute(values, "rows", [(i, i ^ (4 >> (i & 1))) for i in range(rows)])


def halved(launch, kept, got, rows, cover):
    stay, go = launch(add_kernel, [(kept.shape[1:], BF16)] * 2, [kept, got], cover=cover)
    return stay, second_axis(go, rows)


def other_core(values, rows):
    return exchange(values, "rows", rows, 1)


def scatter_rows(values, size, dim):
    for d in distances(size):
        values = halve(values, "rows", size, d, dim)
    return values


def gather_rows(values, size, dim):
    for d in reversed(distances(size)):
        values = double(values, "rows", size, d, dim)
    return values


def scatter_feat(values, size, dim):
    me = lax.axis_index("feat")
    total = lax.dynamic_index_in_dim(values, me, dim, keepdims=False).astype(F32)
    for s in range(1, size):
        piece = lax.dynamic_index_in_dim(values, lax.bitwise_xor(me, s), dim, keepdims=False)
        total = total + exchange(piece, "feat", size, s).astype(F32)
    return low(total)


def on_device(
    rows,
    feats,
    tokens,
    cotangent,
    seg_ids,
    pad_mask,
    norm1_gain,
    w_query,
    w_key,
    w_value,
    w_gate,
    w_rate,
    b_rate,
    inner_w1,
    inner_b1,
    inner_w2,
    inner_b2,
    inner_gain,
    inner_bias,
    w_out,
    norm2_gain,
    ffn_gate,
    ffn_up,
    ffn_down,
):
    launch = in_order()
    _, length, width = tokens.shape
    heads, head, inner = inner_w1.shape
    hidden = ffn_gate.shape[1]
    blocks = length // MB
    chips = rows // 2
    line = (length, width)
    wide = (heads, length, inner)
    slim = (heads, length, head)
    square = (heads, length, length)
    state = (heads, head, inner)
    w2t = jnp.transpose(inner_w2, (0, 2, 1))
    w_rate_t = jnp.transpose(w_rate)
    place = lax.axis_index("rows")
    me = lax.axis_index("feat")
    slot = lax.bitwise_and(place * feats + me, head // 2 - 1)
    ids = jnp.stack(
        [lax.bitwise_and(place, 1), lax.shift_right_logical(place, 1), me, slot]
    )
    cots = across_feats([cotangent[0]] * feats, feats)
    kept = [
        (line, F32),
        (line, F32),
        (line, F32),
        ((heads, 2 * length, head), BF16),
        ((length, 128), F32),
        ((16, length), F32),
        ((length, 128), F32),
        (wide, BF16),
        (wide, BF16),
        ((heads, 2 * length, inner), BF16),
        (wide, BF16),
        (slim, BF16),
        (slim, BF16),
        ((length, 128), F32),
        (slim, BF16),
        ((blocks,) + state, BF16),
        (square, BF16),
        (square, BF16),
        (wide, BF16),
        (slim, BF16),
        ((length, 128), F32),
    ]
    saved = launch(
        forward_kernel,
        [((2,) + line, BF16), (line, BF16)] + kept,
        [
            seg_ids,
            seg_ids,
            pad_mask,
            tokens,
            norm1_gain,
            w_query,
            w_key,
            w_value,
            w_gate,
            w_rate_t,
            b_rate[None],
            inner_w1,
            inner_b1,
            w2t,
            inner_b2,
            inner_gain,
            inner_bias,
            w_out,
            norm2_gain,
        ],
        kept
        + [
            (slim, F32),
            (slim, F32),
            (slim, F32),
            (line, F32),
            (wide, F32),
            (square, BF16),
            (state, F32),
            ((heads, 1, head), F32),
            ((heads, inner), F32),
            ((heads, head), F32),
            ((heads, head), F32),
            ((heads, head), F32),
            ((5, width, width), BF16),
            pltpu.SemaphoreType.DMA((5 + len(kept),)),
            pltpu.SemaphoreType.DMA((blocks,)),
        ],
        smem=1,
        plain=range(19),
        loose=(5, 6, 7, 8, 17),
        keep=[True, True] + [None] * len(kept),
        mib=48,
    )
    pair, normed_two, resid, gelu_gate, gate_slope = saved[0:5]
    qk, ecol, erow, fcol = saved[5:9]
    rest = saved[9:]
    normed_two, *cots = lax.optimization_barrier([normed_two] + cots)
    blocks_in = [normed_two]
    acts, ggs, gus, pieces = [], [], [], []
    for s in range(1, feats):
        if s & (s - 1) == 0:
            blocks_in.append(exchange(normed_two, "feat", feats, s))
        else:
            blocks_in.append(None)
    for s in range(feats):
        if blocks_in[s] is None:
            nearest = s & -s
            held_back, _ = lax.optimization_barrier((blocks_in[s ^ nearest], pieces[1]))
            blocks_in[s] = exchange(held_back, "feat", feats, nearest)
        act, gg, gu, gx = launch(
            ffn_kernel,
            [((length, hidden), BF16)] * 3 + [(line, BF16)],
            [blocks_in[s], cots[s], ffn_gate, ffn_up, ffn_down],
        )
        acts.append(act)
        ggs.append(gg)
        gus.append(gu)
        pieces.append(gx)
    if feats > 2:
        pieces[1], _ = lax.optimization_barrier((pieces[1], acts[3]))
    pieces = across_feats(pieces, feats)

    def between(pieces):
        return launch(
            partial(between_kernel, feats),
            [(line, F32), (line, F32), ((2,) + line, BF16), ((1, width), F32)],
            pieces + [resid, cotangent, norm2_gain, w_out, gelu_gate, gate_slope],
        )

    def inner_backward(grad_inner_out):
        return launch(
            backward_kernel,
            [
                ((3,) + line, BF16),
                ((length, 128), BF16),
                ((heads * head, inner), BF16),
                ((heads * head, inner), BF16),
                ((32, inner), F32),
            ],
            [ids, seg_ids, seg_ids, grad_inner_out, qk, ecol, erow, fcol, inner_w1, w2t]
            + [inner_gain]
            + list(rest),
            [
                ((heads, head), F32),
                (wide, F32),
                (slim, F32),
                (wide, F32),
                ((heads, 2 * length, inner), BF16),
                ((heads, 2 * length, head), BF16),
                (wide, BF16),
                (slim, F32),
                ((length, 128), F32),
                (square, BF16),
                (state, F32),
                ((heads, 1, head), F32),
            ],
            smem=2,
        )

    step = 16 * chips
    small_rows = -(-(16 * feats + 32) // step) * step

    def finish(triple, grad_rates, small, part, grad_resid, grad_gain_two):
        return launch(
            partial(input_kernel, feats),
            [((1,) + line, F32), ((small_rows, inner), BF16)],
            [triple, grad_rates, pair, w_query, w_key, w_value, w_rate_t, part]
            + [tokens, norm1_gain, grad_resid, small, grad_gain_two],
            keep=(False, True),
            cover=0,
        )

    if chips != 4 or (width // feats) % step or hidden % 256 or width % 256:
        grad_resid, grad_inner_out, grad_pair, grad_gain_two = between(pieces)
        out, grads = plain_totals(
            rows, feats, blocks_in, cots, acts, ggs, gus, ffn_down, pair, grad_pair, w_gate
        )
        triple, grad_rates, kept, sent, small = inner_backward(grad_inner_out)
        out = across_feats(out, feats)
        mixed = low(resid + sum(x.astype(F32) for x in out))[None]
        grad_tokens, small = finish(
            triple, grad_rates, small, grads.pop(), grad_resid, grad_gain_two
        )
        late = plain_late_totals(rows, feats, pair, triple, kept, sent, small, state)
        return arrange(mixed, grad_tokens, grads, late, state)
    ffn = launch(
        partial(ffn_weights_kernel, feats),
        [((3, width, hidden // 2), BF16)] * 2 + [(line, BF16)] * feats,
        [ids] + blocks_in + cots + acts + ggs + gus + [ffn_down],
        [((feats * length, width), BF16)] * 2 + [((feats * length, hidden), BF16)] * 3,
        smem=1,
    )
    grad_resid, grad_inner_out, grad_pair, grad_gain_two = between(pieces)
    ffn_sent, _ = lax.optimization_barrier((ffn[1], grad_pair))
    pair_other = other_core(pair, rows)
    half = width // 2
    per = width // (feats * chips) * (half // 128)
    ffn_rows = 3 * (width // chips) * (hidden // 256)
    part, early, early_sent = launch(
        partial(gate_weights_kernel, feats),
        [(line, F32)] + [((2, ffn_rows + feats * 2 * per, 128), BF16)] * 2,
        [ids, pair, pair_other, grad_pair, other_core(grad_pair, rows), w_gate]
        + [ffn[0], other_core(ffn_sent, rows)],
        [
            ((chips, feats * 2 * per, 128), BF16),
            ((2, 2 * length, width), BF16),
            ((2, 2 * length, half), BF16),
        ],
        smem=1,
    )
    early_got = first_axis(early_sent, rows)
    out, _ = lax.optimization_barrier((ffn[2:], part))
    out = across_feats(out, feats)
    triple, grad_rates, kept, sent, small = inner_backward(grad_inner_out)
    triple_other = other_core(triple, rows)
    inner_got = other_core(sent, rows)
    mixed, early, early_sent = launch(
        partial(mixed_kernel, feats),
        [((1,) + line, BF16)] + [(early.shape[1:], BF16)] * 2,
        [resid] + out + [early, early_got],
        keep=(False, True, True),
    )
    tail = 2 * heads * head // chips
    tails, tails_sent = launch(
        tails_kernel,
        [((2, tail, 128), BF16)] * 2,
        [ids, kept, inner_got],
        [((chips, tail, 128), BF16)],
        smem=1,
        cover=0,
    )
    tails_got = first_axis(tails_sent, rows)
    early_sent, _ = lax.optimization_barrier((early_sent, tails_sent))
    early_got = second_axis(early_sent, rows)
    grad_tokens, small = finish(triple, grad_rates, small, part, grad_resid, grad_gain_two)
    tails, tails_got = halved(launch, tails, tails_got, rows, 0)
    common = 2 * small_rows // chips
    late, late_sent = launch(
        partial(late_weights_kernel, feats),
        [((2, feats * 3 * per + common, 128), BF16)] * 2,
        [ids, pair, pair_other, triple, triple_other, small],
        [
            ((chips, feats * 3 * per + common, 128), BF16),
            ((2 * length, width), BF16),
            ((3, 2 * length, half), BF16),
        ],
        smem=1,
        cover=2,
    )
    late_got = first_axis(late_sent, rows)
    ffn_total, *cut = launch(
        middle_kernel,
        [((ffn_rows, 128), BF16)] + [((2 * per + tail, 128), BF16)] * feats,
        [ids, early, early_got, tails, tails_got],
        smem=1,
    )
    cut = across_feats(cut, feats)
    late, late_got = halved(launch, late, late_got, rows, 1)
    (joined,) = launch(
        join_kernel, [((2 * per + tail + ffn_rows, 128), BF16)], cut + [ffn_total]
    )
    late_cut = launch(
        partial(cut_feat_kernel, common),
        [((3 * per + common, 128), BF16)] * feats,
        [ids, late, late_got],
        smem=1,
        cover=0,
    )
    late_cut = across_feats(late_cut, feats)
    near = second_axis(joined, rows)
    far = [first_axis(joined, rows), first_axis(near, rows)]
    mirrored, late_cut[0] = lax.optimization_barrier((other_core(joined, rows), late_cut[0]))
    joined = [joined, near] + far
    (late_total,) = launch(sum_kernel, [((3 * per + common, 128), BF16)], late_cut)
    late = across_chips([late_total] * chips, rows)
    late += [other_core(x, rows) for x in late]
    joined += [mirrored] + [other_core(x, rows) for x in joined[1:]]
    share = (width // feats, width)
    late = launch(
        partial(late_totals_kernel, chips, feats, heads, head),
        [(share, F32)] * 3
        + [((heads, width // feats), F32)]
        + [((1, width // feats), F32)] * 2
        + [((heads, inner), F32)]
        + [((heads, head), F32)] * 3
        + [((1, heads), F32)],
        [ids] + late,
        [((small_rows, inner), F32)],
        smem=1,
        keep=False,
    )
    kept = (
        [((width, hidden), F32)] * 2
        + [((hidden, width), F32)]
        + [(share, F32)] * 2
        + [((heads * head, inner), F32)] * 2
    )
    early = launch(
        early_totals_kernel,
        kept,
        [ids] + joined,
        kept + [((width, hidden), F32), pltpu.SemaphoreType.DMA((len(kept),))],
        smem=1,
        keep=[None] * len(kept),
    )
    early, late = list(early), list(late)
    return arrange(mixed, grad_tokens, early[0:5], late[0:3] + early[5:7] + late[3:], state)


def arrange(mixed, grad_tokens, early, late, state):
    return (
        mixed,
        grad_tokens,
        late[6][0],
        late[0],
        late[1],
        late[2],
        early[3],
        jnp.transpose(late[5]),
        late[12][0],
        late[3].reshape(state),
        late[8],
        jnp.transpose(late[4].reshape(state), (0, 2, 1)),
        late[9],
        late[10],
        late[11],
        early[4],
        late[7][0],
        early[0],
        early[1],
        early[2],
    )


def contract(left, right):
    return low(dot(left, right, 0, 0))


def plain_features(values, rows, feats):
    width = values.shape[0]
    values = values.reshape((feats, width // feats, width))
    values = scatter_feat(scatter_rows(values, rows, 1), feats, 0)
    return gather_rows(values, rows, 0).astype(F32)


def plain_totals(
    rows, feats, blocks_in, cots, acts, ggs, gus, ffn_down, pair, grad_pair, w_gate
):
    def joined(parts):
        return jnp.concatenate(parts, 0)

    def over_rows(values):
        return gather_rows(scatter_rows(values, rows, 0), rows, 0).astype(F32)

    x, c, act = joined(blocks_in), joined(cots), joined(acts)
    out = [low(dot(a, ffn_down)) for a in acts]
    grads = [contract(x, joined(ggs)), contract(x, joined(gus)), contract(act, c)]
    grads = [over_rows(g) for g in grads]
    for i in range(2):
        grads.append(plain_features(contract(pair[i], grad_pair[i]), rows, feats))
    grads.append(dot(grad_pair[0], w_gate, 1, 1))
    return out, grads


def plain_late_totals(rows, feats, pair, triple, kept, sent, small, state):
    heads, head, _ = state
    me = lax.axis_index("feat")
    core = lax.bitwise_and(lax.axis_index("rows"), 1)
    late = [plain_features(contract(pair[0], triple[i]), rows, feats) for i in range(3)]
    both = jnp.where(core == 0, jnp.stack([kept, sent]), jnp.stack([sent, kept]))
    both = scatter_rows(both, rows, 1)
    for d in distances(feats):
        both = add_low(both, exchange(both, "feat", feats, d))
    both = gather_rows(both, rows, 1).astype(F32)
    for d in distances(rows):
        small = add_low(small, exchange(small, "rows", rows, d))
    for d in distances(feats):
        small = add_low(small, exchange(small, "feat", feats, d))
    small = small.astype(F32)
    share = pair.shape[2] // feats
    block = lax.dynamic_slice_in_dim(small, me * 16, 16, 0)[:, 0:share]
    at = feats * 16
    packed = small[at + 16 : at + 16 + heads]
    return late + [
        both[0],
        both[1],
        block[0:heads],
        block[heads : heads + 1],
        block[heads + 1 : heads + 2],
        small[at : at + heads],
        packed[:, 0:head],
        packed[:, head : 2 * head],
        packed[:, 2 * head : 3 * head],
        jnp.sum(packed[:, 3 * head :], 1)[None],
    ]


def solution(mesh):
    batch = ("rows", "feat")
    placed = (
        (P(batch, None, None), P(batch, None, None), P(batch, None), P(batch, None))
        + (P(),) * 15
        + (P(None, "feat"), P(None, "feat"), P("feat", None))
    )
    return jax.shard_map(
        partial(on_device, mesh.shape["rows"], mesh.shape["feat"]),
        mesh=mesh,
        in_specs=placed,
        out_specs=(
            P(batch, None, None),
            P(batch, None, None),
            P("feat"),
            P("feat", None),
            P("feat", None),
            P("feat", None),
            P("feat", None),
            P("feat", None),
            P(),
            P(),
            P(),
            P(),
            P(),
            P(),
            P(),
            P("feat", None),
            P("feat"),
            P(None, "feat"),
            P(None, "feat"),
            P("feat", None),
        ),
        check_vma=False,
    )
```

```python
from functools import partial

import jax
import jax.numpy as jnp
from jax import lax
from jax.experimental import pallas as pl
from jax.experimental.pallas import tpu as pltpu
from jax.sharding import PartitionSpec as P

MB = 16
FORWARD_HEADS = 6
BACKWARD_HEADS = 3
EPSILON = 1e-06
BASE_RATE = 0.1
F32 = jnp.float32
BF16 = jnp.bfloat16


def dot(left, right, left_dim=1, right_dim=0):
    return lax.dot_general(
        left, right, (((left_dim,), (right_dim,)), ((), ())), preferred_element_type=F32
    )


def low(values):
    return values.astype(BF16)


def gelu_parts(values):
    phi = 0.5 + 0.5 * lax.erf(values * 0.7071067811865476)
    density = jnp.exp(-0.5 * values * values) * 0.3989422804014327
    return (values * phi, phi + values * density, density * (2.0 - values * values))


def mean_last(values):
    return jnp.sum(values, -1, keepdims=True) * (1.0 / values.shape[-1])


def sum_rows(values):
    return jnp.sum(values, 0, keepdims=True)


def row_of(ref):
    return ref[...].astype(F32).reshape(1, ref.shape[0])


def column_of(row):
    size = row.shape[1]
    return jnp.transpose(jnp.broadcast_to(row, (size, size)))[:, 0:1]


def segment_masks(seg_row):
    size = seg_row.shape[1]
    rows = lax.broadcasted_iota(jnp.int32, (size, size), 0)
    cols = lax.broadcasted_iota(jnp.int32, (size, size), 1)
    same = column_of(seg_row) == seg_row
    block = MB.bit_length() - 1
    later = lax.shift_right_logical(rows, block) > lax.shift_right_logical(cols, block)
    inclusive = jnp.where(same & (cols <= rows), 1.0, 0.0)
    strict = jnp.where(same & later, 1.0, 0.0)
    return (inclusive, strict)


def forward_kernel(
    seg_smem,
    seg_ref,
    live_ref,
    tok_ref,
    gain1_ref,
    wq_hbm,
    wk_hbm,
    wv_hbm,
    wg_hbm,
    wr_ref,
    br_ref,
    w1_ref,
    b1_ref,
    w2t_ref,
    b2_ref,
    ig_ref,
    ib_ref,
    wo_hbm,
    gain2_ref,
    pair_ref,
    normed_two_ref,
    *refs,
):
    saved = (len(refs) - 15) // 2
    outs, kept, scratch = refs[0:saved], refs[saved : 2 * saved], refs[2 * saved :]
    (
        resid_ref,
        gelu_ref,
        slope_ref,
        qk_ref,
        ecol_ref,
        erow_ref,
        fcol_ref,
        slope1_ref,
        curve1_ref,
        act_ref,
        d1_ref,
        d2_ref,
        n_ref,
        s_ref,
        fit_ref,
        w2s_ref,
        p1_ref,
        p2_ref,
        slopeq_ref,
        nq_ref,
        sq_ref,
    ) = kept
    q_s, k_s, v_s, out_s, base_s, mix_s, w2_s, b2_s = scratch[0:8]
    b1f, b2f, igf, ibf, weights_s, sems, state_sems = scratch[8:]
    length, width = tok_ref.shape[1], tok_ref.shape[2]
    copies = [
        pltpu.make_async_copy(w, weights_s.at[i], sems.at[i])
        for i, w in enumerate((wk_hbm, wv_hbm, wq_hbm, wg_hbm, wo_hbm))
    ]
    for copy in copies:
        copy.start()
    saves = {
        i: pltpu.make_async_copy(kept[i], outs[i], sems.at[len(copies) + i])
        for i in range(saved)
        if i != 15
    }

    def save(*indices):
        for i in indices:
            saves[i].start()

    heads, head = w1_ref.shape[0], w1_ref.shape[1]
    blocks = length // MB
    tok = tok_ref[0].astype(F32)
    spread = lax.rsqrt(mean_last(tok * tok) + EPSILON)
    normed = low(tok * spread * row_of(gain1_ref))
    pair_ref[0] = normed
    seg_row = seg_ref[...].astype(F32)
    live = column_of(live_ref[...].astype(F32))
    rate_pre = dot(normed, wr_ref[...], 1, 1) + br_ref[...].astype(F32)
    sig = jax.nn.sigmoid(rate_pre)
    rates = (BASE_RATE / head) * sig * live
    ecol_ref[...] = jnp.zeros(ecol_ref.shape, F32)
    ecol_ref[:, 0:heads] = rates
    fcol_ref[...] = jnp.zeros(fcol_ref.shape, F32)
    fcol_ref[:, 0:heads] = rates * (1.0 - sig)
    erow_ref[...] = jnp.transpose(ecol_ref[...])[0 : erow_ref.shape[0]]

    def project(i, to):
        copies[i].wait()
        whole = dot(normed, weights_s[i])
        for h in range(heads):
            to[h] = whole[:, h * head : (h + 1) * head]

    project(0, k_s)
    project(1, v_s)
    b1f[...] = b1_ref[...].astype(F32)
    b2f[...] = b2_ref[...].astype(F32)
    igf[...] = ig_ref[...].astype(F32)
    ibf[...] = ib_ref[...].astype(F32)
    for h in range(heads):
        qk_ref[h, length : 2 * length] = low(k_s[h])

    d1_ref[...] = jnp.zeros(d1_ref.shape, BF16)
    inclusive, strict = segment_masks(seg_row)
    for h in range(heads):
        keys = qk_ref[h, length : 2 * length]
        mix_s[h] = low((dot(keys, keys, 1, 1) + 1.0) * (strict * erow_ref[h : h + 1, :]))
        base_s[h] = dot(keys, w1_ref[h]) + b1f[h : h + 1]

    def step(b, carry):
        here = pl.multiple_of(b * MB, MB)
        before = jnp.maximum(here - 1, 0)
        fresh = (b == 0) | (seg_smem[0, here] != seg_smem[0, before])

        ds = pl.ds(here, MB)
        rng = range(heads)
        k = [k_s[h, ds, :] for h in rng]
        v = [v_s[h, ds, :] for h in rng]
        e = [ecol_ref[ds, h : h + 1] for h in rng]
        w2f = [jnp.where(fresh, w2t_ref[h].astype(F32), w2_s[h]) for h in rng]
        w2 = [low(w2f[h]) for h in rng]
        b2 = [jnp.where(fresh, b2f[h : h + 1], b2_s[h]) for h in rng]
        g = [igf[h : h + 1] for h in rng]
        gb = [ibf[h : h + 1] for h in rng]
        parts = [gelu_parts(base_s[h, ds, :] - dot(mix_s[h, ds, :], d1_ref[h])) for h in rng]
        act = [low(parts[h][0]) for h in rng]
        z2 = [dot(act[h], w2[h], 1, 1) + b2[h] for h in rng]
        c = [z - mean_last(z) for z in z2]
        s = [lax.rsqrt(mean_last(x * x) + EPSILON) for x in c]
        n = [c[h] * s[h] for h in rng]
        fit = [g[h] * n[h] + gb[h] - (v[h] - k[h]) for h in rng]
        share = [g[h] * fit[h] for h in rng]
        m1 = [mean_last(share[h]) for h in rng]
        m2 = [mean_last(share[h] * n[h]) for h in rng]
        d2 = [s[h] * (share[h] - m1[h] - n[h] * m2[h]) for h in rng]
        back = [dot(low(d2[h]), w2[h]) for h in rng]
        d1 = [back[h] * parts[h][1] for h in rng]
        d1b = [low(d1[h]) for h in rng]
        ed2 = [d2[h] * e[h] for h in rng]
        up2 = [dot(low(ed2[h]), act[h], 0, 0) for h in rng]
        for h in rng:
            w2s_ref[b, h] = w2[h]
            w2_s[h] = w2f[h] - up2[h]
            b2_s[h] = b2[h] - sum_rows(ed2[h])
            act_ref[h, pl.ds(length + here, MB), :] = act[h]
            slope1_ref[h, ds, :] = low(parts[h][1])
            curve1_ref[h, ds, :] = low(back[h] * parts[h][2])
            d1_ref[h, ds, :] = d1b[h]
            d2_ref[h, ds, :] = low(d2[h])
            n_ref[h, ds, :] = low(n[h])
            s_ref[ds, h : h + 1] = s[h]
            fit_ref[h, ds, :] = low(fit[h])
        pltpu.make_async_copy(w2s_ref.at[b], outs[15].at[b], state_sems.at[b]).start()
        return carry

    save(4, 5, 6)
    lax.fori_loop(0, blocks, step, 0, unroll=8)
    save(7, 8, 10, 11, 12, 13, 14)
    project(2, q_s)
    for h in range(heads):
        qk_ref[h, 0:length] = low(q_s[h])
    save(3)
    for start in range(0, heads, FORWARD_HEADS):
        rng = range(start, start + FORWARD_HEADS)
        every = range(FORWARD_HEADS)
        queries = [qk_ref[h, 0:length] for h in rng]
        keys = [qk_ref[h, length : 2 * length] for h in rng]
        key_act = [act_ref[h, length : 2 * length] for h in rng]
        er = [erow_ref[h : h + 1, :] for h in rng]
        p1 = [(dot(queries[i], keys[i], 1, 1) + 1.0) * inclusive for i in every]
        zq1 = [
            dot(queries[i], w1_ref[h]) + b1f[h : h + 1] - dot(low(p1[i] * er[i]), d1_ref[h])
            for i, h in enumerate(rng)
        ]
        parts = [gelu_parts(x) for x in zq1]
        aq = [low(x[0]) for x in parts]
        p2 = [(dot(aq[i], key_act[i], 1, 1) + 1.0) * inclusive for i in every]
        zq2 = [
            dot(aq[i], w2t_ref[h], 1, 1)
            + b2f[h : h + 1]
            - dot(low(p2[i] * er[i]), d2_ref[h])
            for i, h in enumerate(rng)
        ]
        c = [z - mean_last(z) for z in zq2]
        s = [lax.rsqrt(mean_last(x * x) + EPSILON) for x in c]
        n = [c[i] * s[i] for i in every]
        for i, h in enumerate(rng):
            p1_ref[h] = low(p1[i])
            p2_ref[h] = low(p2[i])
            act_ref[h, 0:length] = aq[i]
            slopeq_ref[h] = low(parts[i][1])
            nq_ref[h] = low(n[i])
            sq_ref[:, h : h + 1] = s[i]
            out_s[:, h * head : (h + 1) * head] = (
                q_s[h] + igf[h : h + 1] * n[i] + ibf[h : h + 1]
            )
    save(9, 16, 17, 18, 19, 20)
    inner_out = out_s[...]
    copies[3].wait()
    gate, slope, _ = gelu_parts(dot(normed, weights_s[3]))
    gelu_ref[...] = gate
    slope_ref[...] = inner_out * slope
    gated = low(inner_out * gate)
    pair_ref[1] = gated
    copies[4].wait()
    resid = tok + dot(gated, weights_s[4])
    resid_ref[...] = resid
    spread_two = lax.rsqrt(mean_last(resid * resid) + EPSILON)
    normed_two_ref[...] = low(resid * spread_two * row_of(gain2_ref))
    save(0, 1, 2)
    for copy in saves.values():
        copy.wait()
    for b in range(blocks):
        pltpu.make_async_copy(w2s_ref.at[b], outs[15].at[b], state_sems.at[b]).wait()


def ffn_kernel(x_ref, c_ref, wg_ref, wu_ref, wd_ref, act_ref, gg_ref, gu_ref, gx_ref):
    x = x_ref[...]
    gate = dot(x, wg_ref[...])
    up = dot(x, wu_ref[...])
    grad_act = dot(c_ref[...], wd_ref[...], 1, 1)
    sigma = jax.nn.sigmoid(gate)
    silu = gate * sigma
    act_ref[...] = low(silu * up)
    gg = low(grad_act * up * sigma * (1.0 + gate * (1.0 - sigma)))
    gu = low(grad_act * silu)
    gg_ref[...] = gg
    gu_ref[...] = gu
    gx_ref[...] = low(dot(gg, wg_ref[...], 1, 1) + dot(gu, wu_ref[...], 1, 1))


def ffn_weights_kernel(parts, ids_smem, *refs):
    x_refs, c_refs, act_refs, gg_refs, gu_refs = (
        refs[i * parts : (i + 1) * parts] for i in range(5)
    )
    wd_ref, kept_ref, sent_ref = refs[5 * parts : 5 * parts + 3]
    out_refs = refs[5 * parts + 3 : 6 * parts + 3]
    x_s, c_s, act_s, gg_s, gu_s = refs[6 * parts + 3 :]
    rows = x_refs[0].shape[0]
    for i in range(parts):
        at = slice(i * rows, (i + 1) * rows)
        x_s[at] = x_refs[i][...]
        c_s[at] = c_refs[i][...]
        act_s[at] = act_refs[i][...]
        gg_s[at] = gg_refs[i][...]
        gu_s[at] = gu_refs[i][...]
        out_refs[i][...] = low(dot(act_refs[i][...], wd_ref[...]))
    half = kept_ref.shape[2]
    core = ids_smem[0]
    for i, (left, right) in enumerate(((x_s, gg_s), (x_s, gu_s), (c_s, act_s))):
        whole = low(dot(left[...], right[...], 0, 0))

        @pl.when(core == 0)
        def _(whole=whole, i=i):
            kept_ref[i] = whole[:, 0:half]
            sent_ref[i] = whole[:, half:]

        @pl.when(core != 0)
        def _(whole=whole, i=i):
            kept_ref[i] = whole[:, half:]
            sent_ref[i] = whole[:, 0:half]


def between_kernel(parts, *refs):
    pieces = refs[0:parts]
    resid_ref, cot_ref, gain2_ref, wo_ref, gelu_ref, slope_ref = refs[parts : parts + 6]
    resid_grad_ref, go_ref, pair_ref, gain_grad_ref = refs[parts + 6 :]
    grad = pieces[0][...].astype(F32)
    for piece in pieces[1:]:
        grad = grad + piece[...].astype(F32)
    resid = resid_ref[...]
    spread = lax.rsqrt(mean_last(resid * resid) + EPSILON)
    scaled = row_of(gain2_ref) * grad
    grad_resid = (
        cot_ref[0].astype(F32)
        + spread * scaled
        - resid * (spread * spread * spread * mean_last(scaled * resid))
    )
    gain_grad_ref[...] = sum_rows(grad * resid * spread)
    resid_grad_ref[...] = grad_resid
    grad_branch = low(grad_resid)
    grad_gated = dot(grad_branch, wo_ref[...], 1, 1)
    go_ref[...] = grad_gated * gelu_ref[...]
    pair_ref[0] = low(grad_gated * slope_ref[...])
    pair_ref[1] = grad_branch


def backward_kernel(
    ids_smem,
    seg_smem,
    seg_ref,
    go_ref,
    qk_ref,
    ecol_ref,
    erow_ref,
    fcol_ref,
    w1_ref,
    w2t_ref,
    ig_ref,
    slope1_ref,
    curve1_ref,
    act_ref,
    d1_ref,
    d2_ref,
    n_ref,
    s_ref,
    fit_ref,
    w2s_ref,
    p1_ref,
    p2_ref,
    slopeq_ref,
    nq_ref,
    sq_ref,
    triple_ref,
    gr_ref,
    kept_ref,
    sent_ref,
    small_ref,
    igf,
    t1_s,
    t2_s,
    ga_s,
    hh1_s,
    hh2_s,
    u_s,
    share_s,
    ge_s,
    mix_s,
    gw2_s,
    gb2_s,
):
    length = go_ref.shape[0]
    heads, head, inner = w1_ref.shape
    blocks = length // MB
    top, bottom = slice(0, length), slice(length, 2 * length)
    igf[...] = ig_ref[...].astype(F32)
    inclusive, strict = segment_masks(seg_ref[...].astype(F32))
    for first in range(0, heads, BACKWARD_HEADS):
        rng = range(first, first + BACKWARD_HEADS)
        every = range(BACKWARD_HEADS)
        g = [igf[h : h + 1] for h in rng]
        weigh = [inclusive * erow_ref[h : h + 1, :] for h in rng]
        n = [nq_ref[h].astype(F32) for h in rng]
        x = [go_ref[:, h * head : (h + 1) * head] * igf[h : h + 1] for h in rng]
        mx = [mean_last(x[i]) for i in every]
        mxn = [mean_last(x[i] * n[i]) for i in every]
        hq2 = [
            low(sq_ref[:, h : h + 1] * (x[i] - mx[i] - n[i] * mxn[i]))
            for i, h in enumerate(rng)
        ]
        aq = [act_ref[h, top] for h in rng]
        ak = [act_ref[h, bottom] for h in rng]
        t2 = [dot(p2_ref[h], hq2[i], 0, 0) for i, h in enumerate(rng)]
        mix = [
            low(-dot(hq2[i], d2_ref[h], 1, 1) * weigh[i]) for i, h in enumerate(rng)
        ]
        gaq = [dot(hq2[i], w2t_ref[h]) + dot(mix[i], ak[i]) for i, h in enumerate(rng)]
        ga = [dot(mix[i], aq[i], 0, 0) for i in every]
        hq1 = [low(gaq[i] * slopeq_ref[h].astype(F32)) for i, h in enumerate(rng)]
        t1 = [dot(p1_ref[h], hq1[i], 0, 0) for i, h in enumerate(rng)]
        for i, h in enumerate(rng):
            hh2_s[h, top] = hq2[i]
            t2_s[h] = t2[i]
            ga_s[h] = ga[i]
            hh1_s[h, top] = hq1[i]
            t1_s[h] = t1[i]
    ge_s[...] = jnp.zeros(ge_s.shape, F32)
    earlier = jnp.transpose(strict)
    for h in range(heads):
        keys = qk_ref[h, bottom]
        mix_s[h] = low((dot(keys, keys, 1, 1) + 1.0) * earlier)
    hh1_s[:, bottom, :] = jnp.zeros(hh1_s[:, bottom, :].shape, BF16)

    def step(i, carry):
        b = blocks - 1 - i
        here = pl.multiple_of(b * MB, MB)
        after = jnp.minimum(here + MB, length - 1)
        fresh = (i == 0) | (seg_smem[0, after] != seg_smem[0, after - 1])

        ds = pl.ds(here, MB)
        ds_low = pl.ds(length + here, MB)
        rng = range(heads)
        act = [act_ref[h, ds_low, :] for h in rng]
        e = [ecol_ref[ds, h : h + 1] for h in rng]
        w2 = [w2s_ref[b, h] for h in rng]
        gw2 = [jnp.where(fresh, 0.0, gw2_s[h]) for h in rng]
        gw2b = [low(x) for x in gw2]
        gb2 = [jnp.where(fresh, 0.0, gb2_s[h]) for h in rng]
        d1 = [d1_ref[h, ds, :].astype(F32) for h in rng]
        d2 = [d2_ref[h, ds, :].astype(F32) for h in rng]
        n = [n_ref[h, ds, :].astype(F32) for h in rng]
        s = [s_ref[ds, h : h + 1] for h in rng]
        fit = [fit_ref[h, ds, :].astype(F32) for h in rng]
        slope = [slope1_ref[h, ds, :].astype(F32) for h in rng]
        curve = [curve1_ref[h, ds, :].astype(F32) for h in rng]
        g = [igf[h : h + 1] for h in rng]
        share = [g[h] * fit[h] for h in rng]
        t1 = [t1_s[h, ds, :] + dot(mix_s[h, ds, :], hh1_s[h, bottom]) for h in rng]
        t2 = [t2_s[h, ds, :] + dot(act[h], gw2b[h], 1, 1) + gb2[h] for h in rng]
        g1 = [-e[h] * t1[h] for h in rng]
        u = [low(g1[h] * slope[h]) for h in rng]
        ed2 = [low(-e[h] * d2[h]) for h in rng]
        ga = [ga_s[h, ds, :] + dot(ed2[h], gw2b[h]) for h in rng]
        g2 = [dot(u[h], w2[h], 1, 1) - e[h] * t2[h] for h in rng]
        y = [s[h] * g2[h] for h in rng]
        my = [mean_last(y[h]) for h in rng]
        myn = [mean_last(y[h] * n[h]) for h in rng]
        msn = [mean_last(share[h] * n[h]) for h in rng]
        mgd = [mean_last(g2[h] * d2[h]) for h in rng]
        gshare = [y[h] - my[h] - n[h] * myn[h] for h in rng]
        gn = [g[h] * (g[h] * gshare[h]) - y[h] * msn[h] - share[h] * myn[h] for h in rng]
        mn = [mean_last(gn[h]) for h in rng]
        mnn = [mean_last(gn[h] * n[h]) for h in rng]
        h2 = [
            low(s[h] * (gn[h] - mn[h] - n[h] * (mnn[h] + mgd[h]))) for h in rng
        ]
        ga = [ga[h] + dot(h2[h], w2[h]) for h in rng]
        h1f = [ga[h] * slope[h] + g1[h] * curve[h] for h in rng]
        h1 = [low(x) for x in h1f]
        up2 = [
            dot(low(d2[h]), u[h], 0, 0) + dot(h2[h], act[h], 0, 0) for h in rng
        ]
        for h in rng:
            w2n = gw2[h] + up2[h]
            gw2_s[h] = w2n
            gb2_s[h] = gb2[h] + sum_rows(h2[h].astype(F32))
            u_s[h, ds, :] = u[h]
            hh1_s[h, ds_low, :] = h1[h]
            hh2_s[h, ds_low, :] = h2[h]
            share_s[h, ds, :] = gshare[h]
            ge_s[ds, h : h + 1] = -jnp.sum(d1[h] * t1[h], -1, keepdims=True) - jnp.sum(
                d2[h] * t2[h], -1, keepdims=True
            )
        return carry

    lax.fori_loop(0, blocks, step, 0, unroll=4)
    small_ref[...] = jnp.zeros(small_ref.shape, F32)
    core = ids_smem[0]
    pad = small_ref.shape[0] // 2
    for start in range(0, heads, BACKWARD_HEADS):
        rng = range(start, start + BACKWARD_HEADS)
        every = range(BACKWARD_HEADS)
        cols = [slice(h * head, (h + 1) * head) for h in rng]
        g = [igf[h : h + 1] for h in rng]
        er = [erow_ref[h : h + 1, :] for h in rng]
        hh1 = [hh1_s[h] for h in rng]
        hh2 = [hh2_s[h] for h in rng]
        qk = [qk_ref[h] for h in rng]
        keys = [qk_ref[h, bottom] for h in rng]
        share = [share_s[h] for h in rng]
        go = [go_ref[:, cols[i]] for i in every]
        both = [dot(hh1[i], d1_ref[h], 1, 1) for i, h in enumerate(rng)]
        direct = [dot(hh1[i], w1_ref[h], 1, 1) for i, h in enumerate(rng)]
        mixq = [low(-both[i][top] * (inclusive * er[i])) for i in every]
        mixk = [low(-both[i][bottom] * (strict * er[i])) for i in every]
        first = [low(dot(qk[i], hh1[i], 0, 0)) for i in every]
        second = [
            low(dot(hh2[i], act_ref[h], 0, 0) + dot(d2_ref[h], u_s[h], 0, 0))
            for i, h in enumerate(rng)
        ]
        gq = [low(go[i] + direct[i][top] + dot(mixq[i], keys[i])) for i in every]
        spread = [
            dot(mixq[i], qk_ref[h, top], 0, 0) + dot(mixk[i], keys[i], 0, 0)
            for i, h in enumerate(rng)
        ]
        gk = [
            low(g[i] * share[i] + direct[i][bottom] + dot(mixk[i], keys[i]) + spread[i])
            for i in every
        ]
        for i, h in enumerate(rng):
            triple_ref[0, :, cols[i]] = gq[i]
            triple_ref[1, :, cols[i]] = gk[i]
            triple_ref[2, :, cols[i]] = low(-g[i] * share[i])
            kept_ref[cols[i]] = jnp.where(core == 0, first[i], second[i])
            sent_ref[cols[i]] = jnp.where(core == 0, second[i], first[i])
            small_ref[h : h + 1] = sum_rows(hh1[i].astype(F32))
            row = slice(pad + h, pad + h + 1)
            small_ref[row, 0:head] = sum_rows(hh2[i].astype(F32))
            small_ref[row, head : 2 * head] = sum_rows(
                go[i] * nq_ref[h].astype(F32)
                + share[i] * (fit_ref[h].astype(F32) + g[i] * n_ref[h].astype(F32))
            )
            small_ref[row, 2 * head : 3 * head] = sum_rows(go[i]) + g[i] * sum_rows(share[i])
    grad_rates = ge_s[...] * fcol_ref[...]
    gr_ref[...] = low(grad_rates)
    total = jnp.broadcast_to(sum_rows(grad_rates), (grad_rates.shape[1], grad_rates.shape[1]))
    total = jnp.transpose(total)[0:heads, 0:1]
    high = low(total).astype(F32)
    slot = lax.broadcasted_iota(jnp.int32, (heads, head), 1)
    mine = ids_smem[3]
    small_ref[pad : pad + heads, 3 * head : 4 * head] = jnp.where(
        slot == mine, high, 0.0
    ) + jnp.where(slot == mine + head // 2, total - high, 0.0)


def put_matrix(to_ref, values, index, count, feats):
    chips = to_ref.shape[0]
    rows = values.shape[0] // (feats * chips)
    chunks = values.shape[1] // 128
    for f in range(feats):
        for l in range(chunks):
            row = ((f * count + index) * chunks + l) * rows
            for j in range(chips):
                at = (f * chips + j) * rows
                to_ref[j, row : row + rows, :] = values[at : at + rows, l * 128 : (l + 1) * 128]


def core_columns(core, values):
    half = values.shape[1] // 2
    return jnp.where(core == 0, values[:, 0:half], values[:, half:])


def put_halves(ids_smem, kept_ref, sent_ref, put):
    core, chip = ids_smem[0], ids_smem[1]
    first, second = 1 + core, 2 - core
    put(kept_ref.at[0], chip)
    put(kept_ref.at[1], lax.bitwise_xor(chip, second))
    put(sent_ref.at[0], lax.bitwise_xor(chip, first))
    put(sent_ref.at[1], lax.bitwise_xor(chip, 3))


def gate_weights_kernel(
    feats,
    ids_smem,
    mine_ref,
    other_ref,
    grads_ref,
    other_grads_ref,
    wg_ref,
    kept_ref,
    got_ref,
    part_ref,
    kept_out,
    sent_out,
    pieces_s,
    left_s,
    right_s,
):
    core = ids_smem[0]
    length = mine_ref.shape[1]
    for i in range(2):
        left_s[i, 0:length] = mine_ref[i]
        left_s[i, length : 2 * length] = other_ref[i]
        right_s[i, 0:length] = core_columns(core, grads_ref[i])
        right_s[i, length : 2 * length] = core_columns(core, other_grads_ref[i])
    for i in range(2):
        put_matrix(pieces_s, low(dot(left_s[i], right_s[i], 0, 0)), i, 2, feats)
    count, _, half = kept_ref.shape
    chunks = half // 128
    before = kept_out.shape[1] - pieces_s.shape[1]
    rows = before // (count * chunks)

    def put(out, place):
        at = pl.ds(pl.multiple_of(place * rows, rows), rows)
        for i in range(count):
            both = low(kept_ref[i, at, :].astype(F32) + got_ref[i, at, :].astype(F32))
            for l in range(chunks):
                row = (i * chunks + l) * rows
                out[row : row + rows] = both[:, l * 128 : (l + 1) * 128]
        out[before:] = pieces_s[place]

    put_halves(ids_smem, kept_out, sent_out, put)
    part_ref[...] = dot(grads_ref[0], wg_ref[...], 1, 1)


def input_kernel(
    feats,
    triple_ref,
    gr_ref,
    pair_ref,
    wq_ref,
    wk_ref,
    wv_ref,
    wr_ref,
    part_ref,
    tok_ref,
    gain1_ref,
    resid_grad_ref,
    small_ref,
    gain_two_ref,
    grad_ref,
    small_out,
):
    heads = wr_ref.shape[0]
    grad = part_ref[...] + dot(triple_ref[0], wq_ref[...], 1, 1)
    grad = grad + dot(triple_ref[1], wk_ref[...], 1, 1) + dot(triple_ref[2], wv_ref[...], 1, 1)
    gr = gr_ref[...]
    grad = grad + dot(gr[:, 0:heads], wr_ref[...])
    tok = tok_ref[0].astype(F32)
    spread = lax.rsqrt(mean_last(tok * tok) + EPSILON)
    scaled = row_of(gain1_ref) * grad
    grad_ref[0] = (
        resid_grad_ref[...]
        + spread * scaled
        - tok * (spread * spread * spread * mean_last(scaled * tok))
    )
    rate_rows = dot(gr, pair_ref[0], 0, 0)
    gain_row = sum_rows(grad * tok * spread)
    small_out[...] = jnp.zeros(small_out.shape, BF16)
    share = tok.shape[1] // feats
    for f in range(feats):
        cols = slice(f * share, (f + 1) * share)
        small_out[f * 16 : f * 16 + 16, 0:share] = low(
            jnp.concatenate(
                [rate_rows[0:heads, cols], gain_row[:, cols], gain_two_ref[:, cols]]
                + [jnp.zeros((14 - heads, share), F32)],
                0,
            )
        )
    at = feats * 16
    small_out[at : at + small_ref.shape[0]] = low(small_ref[...])


def tails_kernel(ids_smem, kept_ref, got_ref, kept_out, sent_out, tails_s):
    chips = tails_s.shape[0]
    inner = low(kept_ref[...].astype(F32) + got_ref[...].astype(F32))
    rows = inner.shape[0] // chips
    for j in range(chips):
        for l in range(2):
            tails_s[j, l * rows : (l + 1) * rows] = inner[
                j * rows : (j + 1) * rows, l * 128 : (l + 1) * 128
            ]

    def put(out, place):
        out[...] = tails_s[place]

    put_halves(ids_smem, kept_out, sent_out, put)


def late_weights_kernel(
    feats,
    ids_smem,
    mine_ref,
    other_ref,
    triple_ref,
    other_triple_ref,
    small_ref,
    kept_out,
    sent_out,
    pieces_s,
    left_s,
    right_s,
):
    core = ids_smem[0]
    length = mine_ref.shape[1]
    left_s[0:length] = mine_ref[0]
    left_s[length : 2 * length] = other_ref[0]
    for i in range(3):
        right_s[i, 0:length] = core_columns(core, triple_ref[i])
        right_s[i, length : 2 * length] = core_columns(core, other_triple_ref[i])
    for i in range(3):
        put_matrix(pieces_s, low(dot(left_s[...], right_s[i], 0, 0)), i, 3, feats)
    chips, most, _ = pieces_s.shape
    extra = small_ref.shape[0] // chips
    for j in range(chips):
        for l in range(2):
            at = most - (2 - l) * extra
            pieces_s[j, at : at + extra] = small_ref[
                j * extra : (j + 1) * extra, l * 128 : (l + 1) * 128
            ]

    def put(out, place):
        out[...] = pieces_s[place]

    put_halves(ids_smem, kept_out, sent_out, put)


def mixed_kernel(feats, resid_ref, *refs):
    kept_ref, got_ref, mixed_ref, stay_ref, go_ref = refs[feats:]
    total = resid_ref[...]
    for ref in refs[0:feats]:
        total = total + ref[...].astype(F32)
    mixed_ref[0] = low(total)
    add_kernel(kept_ref, got_ref, stay_ref, go_ref)


def add_kernel(kept_ref, got_ref, stay_ref, go_ref):
    stay_ref[...] = low(kept_ref[0].astype(F32) + got_ref[0].astype(F32))
    go_ref[...] = low(kept_ref[1].astype(F32) + got_ref[1].astype(F32))


def sum_at(refs, at):
    value = refs[0][at].astype(F32)
    for ref in refs[1:]:
        value = value + ref[at].astype(F32)
    return low(value)


def cut_feat_kernel(common, ids_smem, *refs):
    parts, outs = refs[0:2], refs[2:]
    rows = outs[0].shape[0] - common
    shared = sum_at(parts, (slice(rows * len(outs), rows * len(outs) + common), slice(None)))
    for s, out in enumerate(outs):
        at = pl.ds(pl.multiple_of(lax.bitwise_xor(ids_smem[2], s) * rows, 16), rows)
        out[0:rows] = sum_at(parts, (at, slice(None)))
        out[rows:] = shared


def sum_kernel(*refs):
    values = [ref[...].astype(F32) for ref in refs[:-1]]
    while len(values) > 1:
        values = [values[i] + values[i + 1] for i in range(0, len(values), 2)]
    refs[-1][...] = low(values[0])


def join_kernel(*refs):
    total_ref, out_ref = refs[-2:]
    rows = refs[0].shape[0]
    sum_kernel(*refs[:-2], out_ref.at[0:rows])
    out_ref[rows:] = total_ref[...]


def middle_kernel(ids_smem, *refs):
    pair, tail = refs[0:2], refs[2:4]
    total_ref, outs = refs[4], refs[5:]
    before = total_ref.shape[0]
    rows = (pair[0].shape[0] - before) // len(outs)
    shared = sum_at(tail, (slice(None), slice(None)))
    for s, out in enumerate(outs):
        at = pl.multiple_of(before + lax.bitwise_xor(ids_smem[2], s) * rows, 16)
        out[0:rows] = sum_at(pair, (pl.ds(at, rows), slice(None)))
        out[rows:] = shared
    total_ref[...] = sum_at(pair, (slice(0, before), slice(None)))


def take_matrices(ids_smem, pieces, outs, start=0, order=None):
    core, chip = ids_smem[0], ids_smem[1]
    chunks = outs[0].shape[1] // 256
    rows = outs[0].shape[0] // len(pieces)
    for s, both in enumerate(pieces):
        ats = [
            pl.ds(pl.multiple_of(lax.bitwise_xor(chip, d) * rows, 16), rows)
            for d in (order[s] if order else (s, s))
        ]
        for i, out in enumerate(outs):
            for l in range(chunks):
                row = start + (i * chunks + l) * rows
                mine = both[0][row : row + rows, :].astype(F32)
                other = both[1][row : row + rows, :].astype(F32)
                low_cols = slice(l * 128, (l + 1) * 128)
                high_cols = slice((chunks + l) * 128, (chunks + l + 1) * 128)

                @pl.when(core == 0)
                def _(out=out, ats=ats, mine=mine, other=other, a=low_cols, b=high_cols):
                    out[ats[0], a] = mine
                    out[ats[1], b] = other

                @pl.when(core != 0)
                def _(out=out, ats=ats, mine=mine, other=other, a=low_cols, b=high_cols):
                    out[ats[0], b] = mine
                    out[ats[1], a] = other


def early_totals_kernel(ids_smem, *refs):
    core, chip = ids_smem[0], ids_smem[1]
    first, second = 1 + core, 2 - core
    pieces = [(refs[s], refs[4 + s]) for s in range(4)]
    order = [(0, 0), (second, first), (first, second), (3, 3)]
    outs, kept, down_s, sems = refs[8:15], refs[15:22], refs[22], refs[23]
    gate_ref, up_ref, down_ref, wg_ref, wo_ref, first_ref, second_ref = kept
    saves = [pltpu.make_async_copy(kept[i], outs[i], sems.at[i]) for i in range(7)]
    rows = first_ref.shape[0] // 4
    start = 2 * (wg_ref.shape[0] // 4) * (wg_ref.shape[1] // 256)
    take_matrices(ids_smem, pieces, (gate_ref, up_ref, down_s), start + 2 * rows, order)
    saves[0].start()
    saves[1].start()
    down_ref[...] = jnp.transpose(down_s[...])
    saves[2].start()
    for s, both in enumerate(pieces):
        ats = [
            pl.ds(pl.multiple_of(lax.bitwise_xor(chip, d) * rows, 16), rows) for d in order[s]
        ]
        for l in range(2):
            cols = slice(l * 128, (l + 1) * 128)
            row = start + l * rows
            mine = both[0][row : row + rows].astype(F32)
            other = both[1][row : row + rows].astype(F32)

            @pl.when(core == 0)
            def _(ats=ats, cols=cols, mine=mine, other=other):
                first_ref[ats[0], cols] = mine
                second_ref[ats[1], cols] = other

            @pl.when(core != 0)
            def _(ats=ats, cols=cols, mine=mine, other=other):
                first_ref[ats[1], cols] = other
                second_ref[ats[0], cols] = mine

    saves[5].start()
    saves[6].start()
    take_matrices(ids_smem, pieces, (wg_ref, wo_ref), order=order)
    saves[3].start()
    saves[4].start()
    for copy in saves:
        copy.wait()


def late_totals_kernel(chips, feats, heads, head, ids_smem, *refs):
    pieces = [(refs[s], refs[chips + s]) for s in range(chips)]
    matrices = refs[2 * chips : 2 * chips + 3]
    (rate_ref, norm1_ref, norm2_ref, b1_ref, b2_ref, ig_ref, ib_ref, br_ref, small_s) = refs[
        2 * chips + 3 :
    ]
    chip, feat = ids_smem[1], ids_smem[2]
    take_matrices(ids_smem, pieces, matrices)
    extra = small_s.shape[0] // chips
    most = refs[0].shape[0]
    for s, both in enumerate(pieces):
        at = pl.ds(pl.multiple_of(lax.bitwise_xor(chip, s) * extra, 16), extra)
        for l in range(2):
            row = most - (2 - l) * extra
            small_s[at, l * 128 : (l + 1) * 128] = both[0][row : row + extra].astype(
                F32
            ) + both[1][row : row + extra].astype(F32)
    share = rate_ref.shape[1]
    block = small_s[pl.ds(pl.multiple_of(feat * 16, 16), 16), :]
    rate_ref[...] = block[0:heads, 0:share]
    norm1_ref[...] = block[heads : heads + 1, 0:share]
    norm2_ref[...] = block[heads + 1 : heads + 2, 0:share]
    at = feats * 16
    b1_ref[...] = small_s[at : at + heads, :]
    packed = small_s[at + 16 : at + 16 + heads, :]
    b2_ref[...] = packed[:, 0:head]
    ig_ref[...] = packed[:, head : 2 * head]
    ib_ref[...] = packed[:, 2 * head : 3 * head]
    turned = jnp.transpose(small_s[at + 16 : at + 32, 128:])
    br_ref[...] = sum_rows(turned[3 * head - 128 :])[:, 0:heads]


def held(values):
    return pltpu.with_memory_space_constraint(values, pltpu.VMEM)


def in_order():
    last = []

    def ordered(kernel, outs, inputs, scratch=(), **options):
        inputs = list(inputs)
        at = options.get("smem", 0)
        if last:
            inputs[at], _ = lax.optimization_barrier((inputs[at], last.pop()))
        found = call(kernel, outs, inputs, scratch, **options)
        last.append(found[0])
        return found

    return ordered


def call(
    kernel, outs, inputs, scratch=(), smem=0, cover=1, plain=(), loose=(), keep=True, mib=24
):
    specs, placed = [], []
    for i, x in enumerate(inputs):
        if i < smem:
            specs.append(pl.BlockSpec(memory_space=pltpu.SMEM))
            placed.append(x)
        elif i in loose:
            specs.append(pl.BlockSpec(memory_space=pltpu.HBM))
            placed.append(pltpu.with_memory_space_constraint(x, pltpu.HBM))
        elif i in plain:
            specs.append(pl.BlockSpec(memory_space=pltpu.VMEM))
            placed.append(pltpu.with_memory_space_constraint(x, pltpu.HBM))
        else:
            specs.append(pl.BlockSpec(memory_space=pltpu.VMEM))
            placed.append(held(x))
    kept = [keep] * len(outs) if isinstance(keep, bool) else list(keep)
    return pl.pallas_call(
        kernel,
        out_shape=[
            pltpu.VMEM(s, d) if k else pltpu.HBM(s, d) for (s, d), k in zip(outs, kept)
        ],
        in_specs=specs,
        out_specs=[
            pl.BlockSpec(memory_space=pltpu.HBM if k is None else pltpu.VMEM) for k in kept
        ],
        scratch_shapes=[pltpu.VMEM(*x) if isinstance(x, tuple) else x for x in scratch],
        cost_estimate=pl.CostEstimate(
            flops=int(2e10 * cover + 1e6), bytes_accessed=int(2e7 * cover + 1e3), transcendentals=0
        ),
        compiler_params=pltpu.CompilerParams(vmem_limit_bytes=mib * 2**20),
    )(*placed)


def exchange(values, axis, size, distance):
    return lax.ppermute(values, axis, [(i, i ^ distance) for i in range(size)])


def add_low(left, right):
    return low(left.astype(F32) + right.astype(F32))


def halve(values, axis, size, distance, dim):
    side = lax.bitwise_and(lax.axis_index(axis) // distance, 1)
    half = values.shape[dim] // 2
    kept = lax.dynamic_slice_in_dim(values, side * half, half, dim)
    sent = lax.dynamic_slice_in_dim(values, (1 - side) * half, half, dim)
    return add_low(kept, exchange(sent, axis, size, distance))


def double(values, axis, size, distance, dim):
    side = lax.bitwise_and(lax.axis_index(axis) // distance, 1)
    other = exchange(values, axis, size, distance)
    return jnp.where(
        side == 0,
        jnp.concatenate([values, other], dim),
        jnp.concatenate([other, values], dim),
    )


def distances(size):
    found = []
    step = 1
    while step < size:
        found.append(step)
        step *= 2
    return found


def across_chips(values, rows):
    return [values[0]] + [
        exchange(values[s], "rows", rows, 2 * s) for s in range(1, len(values))
    ]


def across_feats(values, feats):
    return [values[0]] + [exchange(values[s], "feat", feats, s) for s in range(1, feats)]


def first_axis(values, rows):
    return lax.ppermute(values, "rows", [(i, i ^ (2 << (i & 1))) for i in range(rows)])


def second_axis(values, rows):
    return lax.ppermute(values, "rows", [(i, i ^ (4 >> (i & 1))) for i in range(rows)])


def halved(launch, kept, got, rows, cover):
    stay, go = launch(add_kernel, [(kept.shape[1:], BF16)] * 2, [kept, got], cover=cover)
    return stay, second_axis(go, rows)


def other_core(values, rows):
    return exchange(values, "rows", rows, 1)


def scatter_rows(values, size, dim):
    for d in distances(size):
        values = halve(values, "rows", size, d, dim)
    return values


def gather_rows(values, size, dim):
    for d in reversed(distances(size)):
        values = double(values, "rows", size, d, dim)
    return values


def scatter_feat(values, size, dim):
    me = lax.axis_index("feat")
    total = lax.dynamic_index_in_dim(values, me, dim, keepdims=False).astype(F32)
    for s in range(1, size):
        piece = lax.dynamic_index_in_dim(values, lax.bitwise_xor(me, s), dim, keepdims=False)
        total = total + exchange(piece, "feat", size, s).astype(F32)
    return low(total)


def on_device(
    rows,
    feats,
    tokens,
    cotangent,
    seg_ids,
    pad_mask,
    norm1_gain,
    w_query,
    w_key,
    w_value,
    w_gate,
    w_rate,
    b_rate,
    inner_w1,
    inner_b1,
    inner_w2,
    inner_b2,
    inner_gain,
    inner_bias,
    w_out,
    norm2_gain,
    ffn_gate,
    ffn_up,
    ffn_down,
):
    launch = in_order()
    _, length, width = tokens.shape
    heads, head, inner = inner_w1.shape
    hidden = ffn_gate.shape[1]
    blocks = length // MB
    chips = rows // 2
    line = (length, width)
    wide = (heads, length, inner)
    slim = (heads, length, head)
    square = (heads, length, length)
    state = (heads, head, inner)
    w2t = jnp.transpose(inner_w2, (0, 2, 1))
    w_rate_t = jnp.transpose(w_rate)
    place = lax.axis_index("rows")
    me = lax.axis_index("feat")
    slot = lax.bitwise_and(place * feats + me, head // 2 - 1)
    ids = jnp.stack(
        [lax.bitwise_and(place, 1), lax.shift_right_logical(place, 1), me, slot]
    )
    cots = across_feats([cotangent[0]] * feats, feats)
    kept = [
        (line, F32),
        (line, F32),
        (line, F32),
        ((heads, 2 * length, head), BF16),
        ((length, 128), F32),
        ((16, length), F32),
        ((length, 128), F32),
        (wide, BF16),
        (wide, BF16),
        ((heads, 2 * length, inner), BF16),
        (wide, BF16),
        (slim, BF16),
        (slim, BF16),
        ((length, 128), F32),
        (slim, BF16),
        ((blocks,) + state, BF16),
        (square, BF16),
        (square, BF16),
        (wide, BF16),
        (slim, BF16),
        ((length, 128), F32),
    ]
    saved = launch(
        forward_kernel,
        [((2,) + line, BF16), (line, BF16)] + kept,
        [
            seg_ids,
            seg_ids,
            pad_mask,
            tokens,
            norm1_gain,
            w_query,
            w_key,
            w_value,
            w_gate,
            w_rate_t,
            b_rate[None],
            inner_w1,
            inner_b1,
            w2t,
            inner_b2,
            inner_gain,
            inner_bias,
            w_out,
            norm2_gain,
        ],
        kept
        + [
            (slim, F32),
            (slim, F32),
            (slim, F32),
            (line, F32),
            (wide, F32),
            (square, BF16),
            (state, F32),
            ((heads, 1, head), F32),
            ((heads, inner), F32),
            ((heads, head), F32),
            ((heads, head), F32),
            ((heads, head), F32),
            ((5, width, width), BF16),
            pltpu.SemaphoreType.DMA((5 + len(kept),)),
            pltpu.SemaphoreType.DMA((blocks,)),
        ],
        smem=1,
        plain=range(19),
        loose=(5, 6, 7, 8, 17),
        keep=[True, True] + [None] * len(kept),
        mib=48,
    )
    pair, normed_two, resid, gelu_gate, gate_slope = saved[0:5]
    qk, ecol, erow, fcol = saved[5:9]
    rest = saved[9:]
    normed_two, *cots = lax.optimization_barrier([normed_two] + cots)
    blocks_in = [normed_two]
    acts, ggs, gus, pieces = [], [], [], []
    for s in range(1, feats):
        if s & (s - 1) == 0:
            blocks_in.append(exchange(normed_two, "feat", feats, s))
        else:
            blocks_in.append(None)
    for s in range(feats):
        if blocks_in[s] is None:
            nearest = s & -s
            held_back, _ = lax.optimization_barrier((blocks_in[s ^ nearest], pieces[1]))
            blocks_in[s] = exchange(held_back, "feat", feats, nearest)
        act, gg, gu, gx = launch(
            ffn_kernel,
            [((length, hidden), BF16)] * 3 + [(line, BF16)],
            [blocks_in[s], cots[s], ffn_gate, ffn_up, ffn_down],
        )
        acts.append(act)
        ggs.append(gg)
        gus.append(gu)
        pieces.append(gx)
    if feats > 2:
        pieces[1], _ = lax.optimization_barrier((pieces[1], acts[3]))
    pieces = across_feats(pieces, feats)

    def between(pieces):
        return launch(
            partial(between_kernel, feats),
            [(line, F32), (line, F32), ((2,) + line, BF16), ((1, width), F32)],
            pieces + [resid, cotangent, norm2_gain, w_out, gelu_gate, gate_slope],
        )

    def inner_backward(grad_inner_out):
        return launch(
            backward_kernel,
            [
                ((3,) + line, BF16),
                ((length, 128), BF16),
                ((heads * head, inner), BF16),
                ((heads * head, inner), BF16),
                ((32, inner), F32),
            ],
            [ids, seg_ids, seg_ids, grad_inner_out, qk, ecol, erow, fcol, inner_w1, w2t]
            + [inner_gain]
            + list(rest),
            [
                ((heads, head), F32),
                (wide, F32),
                (slim, F32),
                (wide, F32),
                ((heads, 2 * length, inner), BF16),
                ((heads, 2 * length, head), BF16),
                (wide, BF16),
                (slim, F32),
                ((length, 128), F32),
                (square, BF16),
                (state, F32),
                ((heads, 1, head), F32),
            ],
            smem=2,
        )

    step = 16 * chips
    small_rows = -(-(16 * feats + 32) // step) * step

    def finish(triple, grad_rates, small, part, grad_resid, grad_gain_two):
        return launch(
            partial(input_kernel, feats),
            [((1,) + line, F32), ((small_rows, inner), BF16)],
            [triple, grad_rates, pair, w_query, w_key, w_value, w_rate_t, part]
            + [tokens, norm1_gain, grad_resid, small, grad_gain_two],
            keep=(False, True),
            cover=0,
        )

    if chips != 4 or (width // feats) % step or hidden % 256 or width % 256:
        grad_resid, grad_inner_out, grad_pair, grad_gain_two = between(pieces)
        out, grads = plain_totals(
            rows, feats, blocks_in, cots, acts, ggs, gus, ffn_down, pair, grad_pair, w_gate
        )
        triple, grad_rates, kept, sent, small = inner_backward(grad_inner_out)
        out = across_feats(out, feats)
        mixed = low(resid + sum(x.astype(F32) for x in out))[None]
        grad_tokens, small = finish(
            triple, grad_rates, small, grads.pop(), grad_resid, grad_gain_two
        )
        late = plain_late_totals(rows, feats, pair, triple, kept, sent, small, state)
        return arrange(mixed, grad_tokens, grads, late, state)
    ffn = launch(
        partial(ffn_weights_kernel, feats),
        [((3, width, hidden // 2), BF16)] * 2 + [(line, BF16)] * feats,
        [ids] + blocks_in + cots + acts + ggs + gus + [ffn_down],
        [((feats * length, width), BF16)] * 2 + [((feats * length, hidden), BF16)] * 3,
        smem=1,
    )
    grad_resid, grad_inner_out, grad_pair, grad_gain_two = between(pieces)
    ffn_sent, _ = lax.optimization_barrier((ffn[1], grad_pair))
    pair_other = other_core(pair, rows)
    half = width // 2
    per = width // (feats * chips) * (half // 128)
    ffn_rows = 3 * (width // chips) * (hidden // 256)
    part, early, early_sent = launch(
        partial(gate_weights_kernel, feats),
        [(line, F32)] + [((2, ffn_rows + feats * 2 * per, 128), BF16)] * 2,
        [ids, pair, pair_other, grad_pair, other_core(grad_pair, rows), w_gate]
        + [ffn[0], other_core(ffn_sent, rows)],
        [
            ((chips, feats * 2 * per, 128), BF16),
            ((2, 2 * length, width), BF16),
            ((2, 2 * length, half), BF16),
        ],
        smem=1,
    )
    early_got = first_axis(early_sent, rows)
    out, _ = lax.optimization_barrier((ffn[2:], part))
    out = across_feats(out, feats)
    triple, grad_rates, kept, sent, small = inner_backward(grad_inner_out)
    triple_other = other_core(triple, rows)
    inner_got = other_core(sent, rows)
    mixed, early, early_sent = launch(
        partial(mixed_kernel, feats),
        [((1,) + line, BF16)] + [(early.shape[1:], BF16)] * 2,
        [resid] + out + [early, early_got],
        keep=(False, True, True),
    )
    tail = 2 * heads * head // chips
    tails, tails_sent = launch(
        tails_kernel,
        [((2, tail, 128), BF16)] * 2,
        [ids, kept, inner_got],
        [((chips, tail, 128), BF16)],
        smem=1,
        cover=0,
    )
    tails_got = first_axis(tails_sent, rows)
    early_sent, _ = lax.optimization_barrier((early_sent, tails_sent))
    early_got = second_axis(early_sent, rows)
    grad_tokens, small = finish(triple, grad_rates, small, part, grad_resid, grad_gain_two)
    tails, tails_got = halved(launch, tails, tails_got, rows, 1)
    common = 2 * small_rows // chips
    late, late_sent = launch(
        partial(late_weights_kernel, feats),
        [((2, feats * 3 * per + common, 128), BF16)] * 2,
        [ids, pair, pair_other, triple, triple_other, small],
        [
            ((chips, feats * 3 * per + common, 128), BF16),
            ((2 * length, width), BF16),
            ((3, 2 * length, half), BF16),
        ],
        smem=1,
        cover=2,
    )
    late_got = first_axis(late_sent, rows)
    ffn_total, *cut = launch(
        middle_kernel,
        [((ffn_rows, 128), BF16)] + [((2 * per + tail, 128), BF16)] * feats,
        [ids, early, early_got, tails, tails_got],
        smem=1,
    )
    cut = across_feats(cut, feats)
    late, late_got = halved(launch, late, late_got, rows, 1)
    (joined,) = launch(
        join_kernel, [((2 * per + tail + ffn_rows, 128), BF16)], cut + [ffn_total]
    )
    late_cut = launch(
        partial(cut_feat_kernel, common),
        [((3 * per + common, 128), BF16)] * feats,
        [ids, late, late_got],
        smem=1,
        cover=0,
    )
    late_cut = across_feats(late_cut, feats)
    near = second_axis(joined, rows)
    far = [first_axis(joined, rows), first_axis(near, rows)]
    mirrored, late_cut[0] = lax.optimization_barrier((other_core(joined, rows), late_cut[0]))
    joined = [joined, near] + far
    (late_total,) = launch(sum_kernel, [((3 * per + common, 128), BF16)], late_cut)
    late = across_chips([late_total] * chips, rows)
    late += [other_core(x, rows) for x in late]
    joined += [mirrored] + [other_core(x, rows) for x in joined[1:]]
    share = (width // feats, width)
    late = launch(
        partial(late_totals_kernel, chips, feats, heads, head),
        [(share, F32)] * 3
        + [((heads, width // feats), F32)]
        + [((1, width // feats), F32)] * 2
        + [((heads, inner), F32)]
        + [((heads, head), F32)] * 3
        + [((1, heads), F32)],
        [ids] + late,
        [((small_rows, inner), F32)],
        smem=1,
        keep=False,
    )
    kept = (
        [((width, hidden), F32)] * 2
        + [((hidden, width), F32)]
        + [(share, F32)] * 2
        + [((heads * head, inner), F32)] * 2
    )
    early = launch(
        early_totals_kernel,
        kept,
        [ids] + joined,
        kept + [((width, hidden), F32), pltpu.SemaphoreType.DMA((len(kept),))],
        smem=1,
        keep=[None] * len(kept),
    )
    early, late = list(early), list(late)
    return arrange(mixed, grad_tokens, early[0:5], late[0:3] + early[5:7] + late[3:], state)


def arrange(mixed, grad_tokens, early, late, state):
    return (
        mixed,
        grad_tokens,
        late[6][0],
        late[0],
        late[1],
        late[2],
        early[3],
        jnp.transpose(late[5]),
        late[12][0],
        late[3].reshape(state),
        late[8],
        jnp.transpose(late[4].reshape(state), (0, 2, 1)),
        late[9],
        late[10],
        late[11],
        early[4],
        late[7][0],
        early[0],
        early[1],
        early[2],
    )


def contract(left, right):
    return low(dot(left, right, 0, 0))


def plain_features(values, rows, feats):
    width = values.shape[0]
    values = values.reshape((feats, width // feats, width))
    values = scatter_feat(scatter_rows(values, rows, 1), feats, 0)
    return gather_rows(values, rows, 0).astype(F32)


def plain_totals(
    rows, feats, blocks_in, cots, acts, ggs, gus, ffn_down, pair, grad_pair, w_gate
):
    def joined(parts):
        return jnp.concatenate(parts, 0)

    def over_rows(values):
        return gather_rows(scatter_rows(values, rows, 0), rows, 0).astype(F32)

    x, c, act = joined(blocks_in), joined(cots), joined(acts)
    out = [low(dot(a, ffn_down)) for a in acts]
    grads = [contract(x, joined(ggs)), contract(x, joined(gus)), contract(act, c)]
    grads = [over_rows(g) for g in grads]
    for i in range(2):
        grads.append(plain_features(contract(pair[i], grad_pair[i]), rows, feats))
    grads.append(dot(grad_pair[0], w_gate, 1, 1))
    return out, grads


def plain_late_totals(rows, feats, pair, triple, kept, sent, small, state):
    heads, head, _ = state
    me = lax.axis_index("feat")
    core = lax.bitwise_and(lax.axis_index("rows"), 1)
    late = [plain_features(contract(pair[0], triple[i]), rows, feats) for i in range(3)]
    both = jnp.where(core == 0, jnp.stack([kept, sent]), jnp.stack([sent, kept]))
    both = scatter_rows(both, rows, 1)
    for d in distances(feats):
        both = add_low(both, exchange(both, "feat", feats, d))
    both = gather_rows(both, rows, 1).astype(F32)
    for d in distances(rows):
        small = add_low(small, exchange(small, "rows", rows, d))
    for d in distances(feats):
        small = add_low(small, exchange(small, "feat", feats, d))
    small = small.astype(F32)
    share = pair.shape[2] // feats
    block = lax.dynamic_slice_in_dim(small, me * 16, 16, 0)[:, 0:share]
    at = feats * 16
    packed = small[at + 16 : at + 16 + heads]
    return late + [
        both[0],
        both[1],
        block[0:heads],
        block[heads : heads + 1],
        block[heads + 1 : heads + 2],
        small[at : at + heads],
        packed[:, 0:head],
        packed[:, head : 2 * head],
        packed[:, 2 * head : 3 * head],
        jnp.sum(packed[:, 3 * head :], 1)[None],
    ]


def solution(mesh):
    batch = ("rows", "feat")
    placed = (
        (P(batch, None, None), P(batch, None, None), P(batch, None), P(batch, None))
        + (P(),) * 15
        + (P(None, "feat"), P(None, "feat"), P("feat", None))
    )
    return jax.shard_map(
        partial(on_device, mesh.shape["rows"], mesh.shape["feat"]),
        mesh=mesh,
        in_specs=placed,
        out_specs=(
            P(batch, None, None),
            P(batch, None, None),
            P("feat"),
            P("feat", None),
            P("feat", None),
            P("feat", None),
            P("feat", None),
            P("feat", None),
            P(),
            P(),
            P(),
            P(),
            P(),
            P(),
            P(),
            P("feat", None),
            P("feat"),
            P(None, "feat"),
            P(None, "feat"),
            P("feat", None),
        ),
        check_vma=False,
    )
```
